32 devices in a mesh: seq: 4 (over y, x), tensor: 8 (over z, core).
Axes of the slice: x: 2, y: 2, z: 4, core: 2. Of those that a mesh axis runs over, the one named last changes fastest.
Arguments:
- tokens: bfloat16 [1024, 4096], P(('seq', 'tensor')), may hold values from -6 to 6
- w_gate: bfloat16 [4096, 8192], P('seq', 'tensor'), may hold values from -0.09375 to 0.09375
- w_xin: bfloat16 [4096, 8192], P('seq', 'tensor'), may hold values from -0.09375 to 0.09375
- w_bc: bfloat16 [4096, 2048], P('seq', 'tensor'), may hold values from -0.09375 to 0.09375
- w_dt: bfloat16 [4096, 128], P('seq', 'tensor'), may hold values from -0.09375 to 0.09375
- conv_x: float32 [4, 8192], P(None, 'tensor'), may hold values from -3 to 3
- conv_x_bias: float32 [8192], P('tensor'), may hold values from -3 to 3
- conv_bc: float32 [4, 2048], P(None, 'tensor'), may hold values from -3 to 3
- conv_bc_bias: float32 [2048], P('tensor'), may hold values from -3 to 3
- dt_bias: float32 [128], P('tensor'), may hold values from -1 to 1
- decay_rate: float32 [128], P('tensor'), may hold values from 0.000390625 to 0.08, as said below
- d_skip: float32 [128], P('tensor'), may hold values from 0.5 to 1.5
- norm_gain: float32 [8192], P('tensor'), may hold values from 0.25 to 1.75
- w_out: bfloat16 [8192, 4096], P('tensor', 'seq'), may hold values from -0.0625 to 0.0625
- lengths: int32 [8], replicated, may hold values from 1 to 512, 1024 in all
Outputs:
- mixed: bfloat16 [1024, 4096], P(('seq', 'tensor'))
The draws below stay inside these ranges and needn't reach their ends.
Inputs may be any that keep to these rules, and one draw needn't show every extreme that they name: lengths of 8 prompts that fill the pack of 1024 tokens exactly; the longest is exactly 512. `decay_rate`: positive rates.
All inputs are finite; a program needn't handle non-finite values.
Results may differ from the reference program's by a relative error of at most 0.03.
Values may be sent and summed in bfloat16 or wider, within the bound.
A program may use at most 64 MiB of HBM per device.

```python
import math
import jax
import jax.numpy as jnp
import numpy as np
from jax import lax

D = 4096
HEADS = 128
HDIM = 64
GROUPS = 8
STATE = 128
CONV = 4
STRETCH = 256
TOK_SPAN = 256
REQS = 8
INNER = 8192
TOKENS = 1024
MAXLEN = 512
INNER_DEV = 1024
N_TENSOR = 8


def draw_decay_rate(key, part):
    first, second, third = jax.random.split(key, 3)
    share = 0.5
    slowish = jax.random.uniform(first, (HEADS,)) < share
    slow_rate = jnp.exp(jax.random.uniform(second, (HEADS,), minval=jnp.log(0.2 / MAXLEN), maxval=jnp.log(1.0 / MAXLEN)))
    fast_rate = jnp.exp(jax.random.uniform(third, (HEADS,), minval=jnp.log(0.02), maxval=jnp.log(0.08)))
    return jnp.where(slowish, slow_rate, fast_rate).astype(jnp.float32)


def levels(rng, shape, cuts, low, largest):
    def one(dim, shards_of):
        steps = jax.random.uniform(jax.random.fold_in(jax.random.fold_in(rng, 6), dim), (shards_of,), jnp.float32, low / len(cuts), largest / len(cuts))
        return jnp.repeat(jnp.exp(steps), shape[dim] // shards_of).reshape((-1,) + (1,) * (len(shape) - dim - 1))

    loudness = one(*cuts[0])
    for cut in cuts[1:]:
        loudness = loudness * one(*cut)
    return loudness


def split_up(count, total, reach, slope):
    weights = [(1 << 20) // math.isqrt(grade ** slope) + 1 for grade in range(2, count + 1)]
    rest, holding = total - reach - (count - 1), [1] * (count - 1)
    while rest > 0:
        free = [i for i in range(count - 1) if holding[i] < reach]
        whole, remaining = sum([weights[i] for i in free]), rest
        for i in free:
            addition = min(reach - holding[i], max(1, remaining * weights[i] // whole), rest)
            holding[i] = holding[i] + addition
            rest = rest - addition
    return np.array([reach] + holding)


def ragged(stream_key, amount, total, most, lean):
    if amount == 2:
        one = jax.random.randint(stream_key, (), max(1, total - most), min(most, total - 1) + 1)
        return jnp.stack([one, total - one])
    sizes = jnp.asarray(split_up(amount, total, most, lean), jnp.int32)
    pairs = (amount - 1) // 2
    giver, taker = sizes[1:1 + 2 * pairs:2], sizes[2:2 + 2 * pairs:2]
    slack = jnp.minimum(giver - 1, most - taker)
    passed = jax.random.randint(jax.random.fold_in(stream_key, 1), (pairs,), 0, 1 << 20) % (slack + 1)
    sizes = sizes.at[1:1 + 2 * pairs:2].set(giver - passed).at[2:2 + 2 * pairs:2].set(taker + passed)
    return sizes[jax.random.permutation(jax.random.fold_in(stream_key, 2), amount)]


def scatter_about(key, extent, deviation, limit, cuts=(), held_as=jnp.bfloat16):
    values = deviation * jax.random.normal(key, extent, jnp.float32)
    if cuts:
        values = values * levels(key, extent, cuts, -0.22, 0.18)
    return jnp.clip(values, -limit, limit).astype(held_as)


def setup_inputs(seed: int = 0) -> dict:
    arg_keys = jax.random.split(jax.random.key(seed), 16)
    tokens = scatter_about(arg_keys[0], (TOKENS, D), 1.0, 6.0, ((0, 32),))
    w_gate = scatter_about(arg_keys[1], (D, INNER), D ** -0.5, 0.09375, ((0, 4), (1, 8)))
    w_xin = scatter_about(arg_keys[2], (D, INNER), D ** -0.5, 0.09375, ((0, 4), (1, 8)))
    w_bc = scatter_about(arg_keys[3], (D, 2 * GROUPS * STATE), D ** -0.5, 0.09375, ((0, 4), (1, 8)))
    w_dt = scatter_about(arg_keys[4], (D, HEADS), D ** -0.5, 0.09375, ((0, 4), (1, 8)))
    conv_x = scatter_about(arg_keys[5], (CONV, INNER), CONV ** -0.5, 3.0, ((1, 8),), jnp.float32)
    conv_x_bias = scatter_about(arg_keys[6], (INNER,), 0.5, 3.0, ((0, 8),), jnp.float32)
    conv_bc = scatter_about(arg_keys[7], (CONV, 2 * GROUPS * STATE), CONV ** -0.5, 3.0, ((1, 8),), jnp.float32)
    conv_bc_bias = scatter_about(arg_keys[8], (2 * GROUPS * STATE,), 0.5, 3.0, ((0, 8),), jnp.float32)
    dt_bias = jnp.clip(jax.random.uniform(arg_keys[9], (HEADS,), jnp.float32, -1.0, 1.0) * levels(arg_keys[9], (HEADS,), ((0, 8),), -0.4, 0.0), -1.0, 1.0)
    decay_rate = draw_decay_rate(jax.random.fold_in(arg_keys[15], 71), 0)
    d_skip = jnp.clip(0.5 + 1.0 * jax.random.uniform(arg_keys[11], (HEADS,), jnp.float32) ** levels(arg_keys[11], (HEADS,), ((0, 8),), -0.2, 0.2), 0.5, 1.5)
    norm_gain = jnp.clip(1.0 + 0.15 * jax.random.normal(arg_keys[12], (INNER,), jnp.float32), 0.25, 1.75)
    w_out = scatter_about(arg_keys[13], (INNER, D), INNER ** -0.5, 0.0625, ((0, 8), (1, 4)))
    lengths = ragged(arg_keys[14], REQS, TOKENS, MAXLEN, 2).astype(jnp.int32)
    return dict(tokens=tokens, w_gate=w_gate, w_xin=w_xin, w_bc=w_bc, w_dt=w_dt, conv_x=conv_x, conv_x_bias=conv_x_bias, conv_bc=conv_bc, conv_bc_bias=conv_bc_bias, dt_bias=dt_bias, decay_rate=decay_rate, d_skip=d_skip, norm_gain=norm_gain, w_out=w_out, lengths=lengths)


HIGH = lax.Precision.HIGHEST

def doc_ids(lengths, positions):
    starts = (jnp.cumsum(lengths) - lengths).astype(jnp.int32)
    counted = lax.optimization_barrier(jnp.sum((starts[None, :] <= positions[:, None]).astype(jnp.int32), axis=1))
    return (counted - 1).astype(jnp.int32)

def causal_conv(values, edge, weights, bias, docs, edge_docs):
    count = values.shape[0]
    extended = jnp.concatenate([edge, values], axis=0).astype(jnp.float32)
    all_docs = jnp.concatenate([edge_docs, docs])
    summed = jnp.zeros(values.shape, jnp.float32) + bias[None, :]
    for offset in range(weights.shape[0]):
        same = (all_docs[offset:offset + count] == docs).astype(jnp.float32)
        summed = summed + weights[offset][None, :] * extended[offset:offset + count] * same[:, None]
    return lax.optimization_barrier(jax.nn.silu(summed).astype(jnp.bfloat16))

def ssd_blocks(xvals, dtv, rate, bmat, cmat, docs, prev_doc, head_group, block):
    count, heads, hdim = xvals.shape
    nstate = bmat.shape[2]
    blocks = count // block
    logs = -dtv * rate[None, :]

    def split(array):
        return array.reshape((blocks, block) + array.shape[1:])
    lower = jnp.tril(jnp.ones((block, block), bool))

    def step(carry, pieces):
        state, last_doc = carry
        xblk, dblk, lblk, bblk, cblk, docblk = pieces
        cum = jnp.cumsum(lblk, axis=0)
        same = (docblk[:, None] == docblk[None, :]) & lower
        diff = cum.T[:, :, None] - cum.T[:, None, :]
        decay = jnp.exp(jnp.where(same[None], diff, -jnp.inf))
        scores = jnp.einsum('ign,jgn->gij', cblk, bblk, precision=HIGH)
        mixing = scores[head_group] * decay * dblk.T[:, None, :]
        inner = jnp.einsum('hij,jhp->ihp', mixing, xblk, precision=HIGH)
        open_in = (docblk == last_doc).astype(jnp.float32)
        carry_in = jnp.exp(cum) * open_in[:, None]
        chead = cblk[:, head_group, :]
        outer = jnp.einsum('ihn,hpn->ihp', chead, state, precision=HIGH) * carry_in[:, :, None]
        end_doc = docblk[-1]
        tail = jnp.exp(cum[-1][None, :] - cum) * (docblk == end_doc).astype(jnp.float32)[:, None] * dblk
        bhead = bblk[:, head_group, :]
        fresh = jnp.einsum('jh,jhp,jhn->hpn', tail, xblk, bhead, precision=HIGH)
        state = carry_in[-1][:, None, None] * state + fresh
        return ((state, end_doc), inner + outer)
    init = (jnp.zeros((heads, hdim, nstate), jnp.float32), prev_doc)
    (state, end_doc), outs = lax.scan(step, init, (split(xvals), split(dtv), split(logs), split(bmat), split(cmat), split(docs)))
    return (outs.reshape(count, heads, hdim), state)

def reference(tokens, w_gate, w_xin, w_bc, w_dt, conv_x, conv_x_bias, conv_bc, conv_bc_bias, dt_bias, decay_rate, d_skip, norm_gain, w_out, lengths):
    gate = jnp.dot(tokens, w_gate, preferred_element_type=jnp.float32).astype(jnp.bfloat16)
    xin = jnp.dot(tokens, w_xin, preferred_element_type=jnp.float32).astype(jnp.bfloat16)
    bcin = jnp.dot(tokens, w_bc, preferred_element_type=jnp.float32).astype(jnp.bfloat16)
    dtin = jnp.dot(tokens, w_dt, preferred_element_type=jnp.float32).astype(jnp.bfloat16)
    gate, xin, bcin, dtin = lax.optimization_barrier((gate, xin, bcin, dtin))
    positions = jnp.arange(TOKENS, dtype=jnp.int32)
    docs = doc_ids(lengths, positions)
    edge_docs = doc_ids(lengths, jnp.arange(-(CONV - 1), 0, dtype=jnp.int32))
    x_conv = causal_conv(xin, jnp.zeros((CONV - 1, INNER), jnp.bfloat16), conv_x, conv_x_bias, docs, edge_docs)
    bc_conv = causal_conv(bcin, jnp.zeros((CONV - 1, 2 * GROUPS * STATE), jnp.bfloat16), conv_bc, conv_bc_bias, docs, edge_docs)
    dtv = jax.nn.softplus(dtin.astype(jnp.float32) + dt_bias[None, :])
    xvals = x_conv.astype(jnp.float32).reshape(TOKENS, HEADS, HDIM)
    both = jnp.transpose(bc_conv.astype(jnp.float32).reshape(TOKENS, 2 * STATE, GROUPS), (0, 2, 1))
    bmat = both[:, :, :STATE]
    cmat = both[:, :, STATE:]
    head_group = np.arange(HEADS) // (HEADS // GROUPS)
    block = min(STRETCH, TOK_SPAN)
    ssd_out, last_state = ssd_blocks(xvals, dtv, decay_rate, bmat, cmat, docs, jnp.int32(-1), head_group, block)
    yvals = (ssd_out + d_skip[None, :, None] * xvals).reshape(TOKENS, INNER)
    gated = yvals * jax.nn.silu(gate.astype(jnp.float32))
    grouped = gated.reshape(TOKENS, GROUPS, INNER // GROUPS)
    scale = lax.rsqrt(lax.optimization_barrier(jnp.mean(grouped * grouped, axis=-1, keepdims=True)) + 1e-05)
    normed = ((grouped * scale).reshape(TOKENS, INNER) * norm_gain[None, :]).astype(jnp.bfloat16)

    def add_block(index, summed):
        begin = (index * INNER_DEV).astype(jnp.int32)
        rows = lax.dynamic_slice_in_dim(normed, begin, INNER_DEV, 1)
        wrows = lax.dynamic_slice_in_dim(w_out, begin, INNER_DEV, 0)
        part = jnp.dot(rows, wrows, preferred_element_type=jnp.float32).astype(jnp.bfloat16)
        return summed + lax.optimization_barrier(part).astype(jnp.float32)
    summed = lax.fori_loop(0, N_TENSOR, add_block, jnp.zeros((TOKENS, D), jnp.float32))
    return summed.astype(jnp.bfloat16)
```

```python
import jax
import jax.numpy as jnp
import numpy as np
from jax import lax
from jax.experimental import pallas as pl
from jax.experimental.pallas import tpu as pltpu
from jax.sharding import PartitionSpec as P

HDIM = 64
GROUPS = 8
STATE = 128
CONV = 4
STRETCH = 256
INNER = 8192


HIGH = lax.Precision.HIGHEST


def from_behind(x, axis, by):
    count = lax.axis_size(axis)
    pairs = [(i, i + by) for i in range(count) if 0 <= i + by < count]
    return lax.ppermute(x, axis, pairs)


def carried_in(x, axis, combine, identity):
    count, here = (lax.axis_size(axis), lax.axis_index(axis))
    everything = jax.tree.map(
        lambda part, kind: lax.all_gather(part.astype(kind), axis), x, (jnp.bfloat16, jnp.bfloat16)
    )
    start = jax.tree.map(
        lambda part, zero: jnp.broadcast_to(jnp.asarray(zero, part.dtype), part.shape), x, identity
    )

    def hop(k, before):
        reached = k < here
        new = combine(
            before, jax.tree.map(lambda part, own: part[k].astype(own.dtype), everything, x)
        )
        return jax.tree.map(lambda a, b: jnp.where(reached, a, b), new, before)

    return lax.fori_loop(0, count, hop, start)


def doc_ids(lengths, positions):
    starts = jnp.cumsum(lengths) - lengths
    counted = jnp.sum((starts[None, :] <= positions[:, None]).astype(jnp.int32), axis=1)
    return counted - 1


def causal_conv(values, edge, weights, bias, docs, edge_docs):
    count = values.shape[0]
    extended = jnp.concatenate([edge, values], axis=0).astype(jnp.float32)
    all_docs = jnp.concatenate([edge_docs, docs])
    summed = jnp.zeros(values.shape, jnp.float32) + bias[None, :]
    for offset in range(weights.shape[0]):
        same = (all_docs[offset : offset + count] == docs).astype(jnp.float32)
        summed = (
            summed + weights[offset][None, :] * extended[offset : offset + count] * same[:, None]
        )
    return lax.optimization_barrier(jax.nn.silu(summed).astype(jnp.bfloat16))


def ssd_blocks(xvals, dtv, rate, bmat, cmat, docs, prev_doc, head_group, block):
    count, heads, hdim = xvals.shape
    nstate = bmat.shape[2]
    blocks = count // block
    logs = -dtv * rate[None, :]

    def split(array):
        return array.reshape((blocks, block) + array.shape[1:])

    lower = jnp.tril(jnp.ones((block, block), bool))

    def step(carry, pieces):
        state, last_doc = carry
        xblk, dblk, lblk, bblk, cblk, docblk = pieces
        cum = jnp.cumsum(lblk, axis=0)
        same = (docblk[:, None] == docblk[None, :]) & lower
        diff = cum.T[:, :, None] - cum.T[:, None, :]
        decay = jnp.exp(jnp.where(same[None], diff, -jnp.inf))
        scores = jnp.einsum("ign,jgn->gij", cblk, bblk, precision=HIGH)
        mixing = scores[head_group] * decay * dblk.T[:, None, :]
        inner = jnp.einsum("hij,jhp->ihp", mixing, xblk, precision=HIGH)
        open_in = (docblk == last_doc).astype(jnp.float32)
        carry_in = jnp.exp(cum) * open_in[:, None]
        chead = cblk[:, head_group, :]
        outer = jnp.einsum("ihn,hpn->ihp", chead, state, precision=HIGH) * carry_in[:, :, None]
        end_doc = docblk[-1]
        tail = (
            jnp.exp(cum[-1][None, :] - cum)
            * (docblk == end_doc).astype(jnp.float32)[:, None]
            * dblk
        )
        bhead = bblk[:, head_group, :]
        fresh = jnp.einsum("jh,jhp,jhn->hpn", tail, xblk, bhead, precision=HIGH)
        state = carry_in[-1][:, None, None] * state + fresh
        return ((state, end_doc), inner + outer)

    init = (jnp.zeros((heads, hdim, nstate), jnp.float32), prev_doc)
    (state, end_doc), outs = lax.scan(
        step, init, (split(xvals), split(dtv), split(logs), split(bmat), split(cmat), split(docs))
    )
    return (outs.reshape(count, heads, hdim), state)


def shards_wide(
    tokens,
    w_gate,
    w_xin,
    w_bc,
    w_dt,
    conv_x,
    conv_x_bias,
    conv_bc,
    conv_bc_bias,
    dt_bias,
    decay_rate,
    d_skip,
    norm_gain,
    w_out,
    lengths,
):
    tensor_count = lax.axis_size("tensor")
    seq_index = lax.axis_index("seq")
    tensor_index = lax.axis_index("tensor")
    span_rows = lax.all_gather(tokens, "tensor", axis=0, tiled=True)
    span_len = span_rows.shape[0]
    pieces = (
        lax.all_gather(w_gate, "seq", axis=0, tiled=True),
        lax.all_gather(w_xin, "seq", axis=0, tiled=True),
        lax.all_gather(w_bc, "seq", axis=0, tiled=True),
        lax.all_gather(w_dt, "seq", axis=0, tiled=True),
    )
    gate_acc, xin_acc, bc_acc, dt_acc = tuple(
        (
            jnp.dot(span_rows, weight_piece, preferred_element_type=jnp.float32)
            for weight_piece in pieces
        )
    )
    gate = gate_acc.astype(jnp.bfloat16)
    xin = xin_acc.astype(jnp.bfloat16)
    bcin = bc_acc.astype(jnp.bfloat16)
    dtin = dt_acc.astype(jnp.bfloat16)
    gate, xin, bcin, dtin = lax.optimization_barrier((gate, xin, bcin, dtin))
    positions = seq_index * span_len + jnp.arange(span_len, dtype=jnp.int32)
    docs = doc_ids(lengths, positions)
    edge_docs = doc_ids(lengths, seq_index * span_len + jnp.arange(-(CONV - 1), 0, dtype=jnp.int32))
    prev_span_doc = doc_ids(lengths, positions[:1] - 1)[0]
    edge_x, edge_bc = from_behind(
        (xin[span_len - (CONV - 1) :], bcin[span_len - (CONV - 1) :]), "seq", 1
    )
    x_conv = causal_conv(xin, edge_x, conv_x, conv_x_bias, docs, edge_docs)
    bc_conv = causal_conv(bcin, edge_bc, conv_bc, conv_bc_bias, docs, edge_docs)
    group_span = tensor_count // GROUPS
    my_group = tensor_index // group_span
    every_group = lax.all_gather(bc_conv, "tensor", axis=1, tiled=True)
    arranged = every_group.reshape(span_len, 2 * STATE, GROUPS)
    group_cols = lax.dynamic_slice_in_dim(arranged, my_group, 1, 2).reshape(span_len, 2 * STATE)
    head_dev = w_dt.shape[1]
    head_group = np.zeros(head_dev, dtype=np.int32)
    both = group_cols.astype(jnp.float32)
    bmat = both[:, None, :STATE]
    cmat = both[:, None, STATE:]
    xvals = x_conv.astype(jnp.float32).reshape(span_len, head_dev, HDIM)
    dtv = jax.nn.softplus(dtin.astype(jnp.float32) + dt_bias[None, :])
    block = min(STRETCH, span_len)
    y_local, end_state = ssd_blocks(
        xvals, dtv, decay_rate, bmat, cmat, docs, prev_span_doc, head_group, block
    )
    cum_span = jnp.cumsum(-dtv * decay_rate[None, :], axis=0)
    open_span = (docs == prev_span_doc).astype(jnp.float32)
    span_decay = jnp.exp(cum_span[-1]) * open_span[-1]

    def combine(earlier, later):
        return (earlier[0] * later[0], later[0][:, None, None] * earlier[1] + later[1])

    entering = carried_in(
        (span_decay, end_state),
        "seq",
        combine,
        (jnp.ones_like(span_decay), jnp.zeros_like(end_state)),
    )[1]
    carried = jnp.exp(cum_span) * open_span[:, None]
    y_enter = (
        jnp.einsum("ihn,hpn->ihp", cmat[:, head_group, :], entering, precision=HIGH)
        * carried[:, :, None]
    )
    yvals = (y_local + y_enter + d_skip[None, :, None] * xvals).reshape(span_len, head_dev * HDIM)
    gated = yvals * jax.nn.silu(gate.astype(jnp.float32))
    local_sq = jnp.sum(gated * gated, axis=1)
    group_mark = (jnp.arange(GROUPS) == my_group).astype(jnp.float32)
    every_sum = lax.psum(local_sq[:, None] * group_mark[None, :], "tensor")
    group_mean = jnp.sum(every_sum * group_mark[None, :], axis=1) / (INNER // GROUPS)
    normed = (gated * lax.rsqrt(group_mean + 1e-05)[:, None] * norm_gain[None, :]).astype(
        jnp.bfloat16
    )
    w_full = lax.all_gather(w_out, "seq", axis=1, tiled=True)
    return lax.psum_scatter(
        jnp.dot(normed, w_full, preferred_element_type=jnp.float32).astype(jnp.bfloat16),
        "tensor",
        scatter_dimension=0,
        tiled=True,
    )


def enter(peers):
    barrier = pltpu.get_barrier_semaphore()
    for peer in peers:
        pl.semaphore_signal(barrier, inc=1, device_id=peer, device_id_type=pl.DeviceIdType.MESH)
    pl.semaphore_wait(barrier, len(peers))


def remote(src, dst, send, recv, peer):
    return pltpu.make_async_remote_copy(
        src_ref=src,
        dst_ref=dst,
        send_sem=send,
        recv_sem=recv,
        device_id=peer,
        device_id_type=pl.DeviceIdType.MESH,
    )


def places():
    s, t = lax.axis_index("seq"), lax.axis_index("tensor")
    seqs, chips = lax.axis_size("seq"), lax.axis_size("tensor") // 2
    z, c = t // 2, t % 2

    def along(ds, dz):
        return lax.rem(s + ds, seqs), lax.rem(z + dz, chips)

    return s, z, c, seqs, chips, along


def out_kernel(
    g_ref, gain_ref, w_ref, out_ref, held, normed, part, sib, pair, got,
    g_send, g_recv, p_send, p_recv, o_send, o_recv,
):
    s, z, c, seqs, chips, along = places()
    span = g_ref.shape[0] // seqs
    width = g_ref.shape[1]
    own = out_ref.shape[0]
    cols = w_ref.shape[1]
    sibling = (s, 2 * z + 1 - c)
    offsets = [(ds, dz) for ds in range(seqs) for dz in range(chips) if ds or dz]
    enter([(along(ds, dz)[0], 2 * along(ds, dz)[1] + c) for ds, dz in offsets] + [sibling])
    order = list(range(1, seqs)) + [0]
    gathers = {}
    for k in order:
        for ds in range(1, seqs):
            rows = pl.ds(pl.multiple_of(lax.rem(s + ds + k, seqs) * span, span), span)
            gathers[k, ds] = remote(
                g_ref.at[rows],
                held.at[ds, rows],
                g_send.at[k, ds],
                g_recv.at[k, ds],
                (along(ds, 0)[0], 2 * z + c),
            )
            gathers[k, ds].start()
    pairs, sends = {}, []

    def finish(k):
        q = lax.rem(s + k, seqs)
        pairs[k].wait_recv()
        for dz in range(chips):
            there = along(0, dz)[1]
            both = part[q, there, c].astype(jnp.float32) + sib[q, there].astype(jnp.float32)
            if k == 0 and dz == 0:
                got[0, 0] = both.astype(jnp.bfloat16)
            else:
                pair[k, dz] = both.astype(jnp.bfloat16)
                sends.append(
                    remote(
                        pair.at[k, dz],
                        got.at[k, dz],
                        o_send.at[k, dz],
                        o_recv.at[k, dz],
                        (q, 2 * there + c),
                    )
                )
                sends[-1].start()

    for step, k in enumerate(order):
        q = lax.rem(s + k, seqs)
        rows = pl.ds(pl.multiple_of(q * span, span), span)
        for ds in range(1, seqs):
            gathers[k, ds].wait_recv()
        blocks = [g_ref[rows, :].astype(jnp.float32)] + [
            held[ds, rows, :].astype(jnp.float32) for ds in range(1, seqs)
        ]
        squares = blocks[0] * blocks[0]
        for b in blocks[1:]:
            squares = squares + b * b
        scale = lax.rsqrt(jnp.sum(squares, axis=1, keepdims=True) / (width * seqs) + 1e-05)
        froms = [pl.multiple_of(lax.rem(s + seqs - ds, seqs) * width, width) for ds in range(seqs)]
        for ds in range(seqs):
            normed[ds] = (blocks[ds] * scale * gain_ref[:, pl.ds(froms[ds], width)]).astype(
                jnp.bfloat16
            )
        tile = 256

        def column(n, _):
            here = pl.ds(pl.multiple_of(n * tile, tile), tile)
            acc = jnp.zeros((span, tile), jnp.float32)
            for ds in range(seqs):
                acc = acc + jnp.dot(
                    normed[ds],
                    w_ref[pl.ds(froms[ds], width), here],
                    preferred_element_type=jnp.float32,
                )
            part[q, :, :, :, here] = acc.astype(jnp.bfloat16).reshape(chips, 2, own, tile)
            return 0

        lax.fori_loop(0, cols // tile, column, 0)
        pairs[k] = remote(
            part.at[q, :, 1 - c], sib.at[q], p_send.at[k], p_recv.at[k], sibling
        )
        pairs[k].start()
        if step:
            finish(order[step - 1])
    finish(order[-1])
    for copy in sends:
        copy.wait_recv()
    for ds in range(seqs):
        total = got[ds, 0].astype(jnp.float32)
        for dz in range(1, chips):
            total = total + got[ds, dz].astype(jnp.float32)
        begin = pl.multiple_of(lax.rem(s + seqs - ds, seqs) * cols, cols)
        out_ref[:, pl.ds(begin, cols)] = total.astype(jnp.bfloat16)
    for copy in list(gathers.values()) + list(pairs.values()) + sends:
        copy.wait_send()


def project_out(gated, gain, w_out, own, seqs, chips):
    total, width = gated.shape
    cols = w_out.shape[1]
    dma = pltpu.SemaphoreType.DMA
    vmem = pl.BlockSpec(memory_space=pltpu.VMEM)
    return pl.pallas_call(
        out_kernel,
        out_shape=jax.ShapeDtypeStruct((own, cols * seqs), jnp.bfloat16),
        in_specs=[vmem] * 3,
        out_specs=vmem,
        scratch_shapes=[
            pltpu.VMEM((seqs, total, width), jnp.bfloat16),
            pltpu.VMEM((seqs, total // seqs, width), jnp.bfloat16),
            pltpu.VMEM((seqs, chips, 2, own, cols), jnp.bfloat16),
            pltpu.VMEM((seqs, chips, own, cols), jnp.bfloat16),
            pltpu.VMEM((seqs, chips, own, cols), jnp.bfloat16),
            pltpu.VMEM((seqs, chips, own, cols), jnp.bfloat16),
            dma((seqs, seqs)),
            dma((seqs, seqs)),
            dma((seqs,)),
            dma((seqs,)),
            dma((seqs, chips)),
            dma((seqs, chips)),
        ],
        compiler_params=pltpu.CompilerParams(
            collective_id=1, has_side_effects=True, vmem_limit_bytes=40 * 2**20
        ),
    )(gated, gain[None, :], w_out)


SEQS, CHIPS, OWN, SPAN, WIDE, HALF = 4, 4, 32, 256, 256, 128
LOG2E = 1.4426950408889634


def silu(v):
    return v / (1.0 + jnp.exp(-v))


class Sums:
    def __init__(self, bufs, sems, s, z, c):
        self.sa, self.sb, self.ra, self.rb, self.qa, self.qb, self.pa, self.pb, self.k0, self.k1, self.k2 = bufs
        self.sems = sems
        self.x, self.y = (s ^ 1, 2 * z + c), (s ^ 2, 2 * z + c)

    def copies(self, u):
        send, recv = self.sems
        return (
            remote(self.sa.at[u], self.ra.at[u], send.at[u, 0], recv.at[u, 0], self.x),
            remote(self.sb.at[u], self.rb.at[u], send.at[u, 1], recv.at[u, 1], self.y),
            remote(self.qa.at[u], self.pa.at[u], send.at[u, 2], recv.at[u, 2], self.y),
            remote(self.qb.at[u], self.pb.at[u], send.at[u, 3], recv.at[u, 3], self.x),
        )

    def emit(self, u, get):
        first, second, _, _ = self.copies(u)
        far = get(3)
        self.sa[u, 1] = far[:, :HALF].astype(jnp.bfloat16)
        self.sb[u, 1] = far[:, HALF:].astype(jnp.bfloat16)
        near = get(1)
        self.sa[u, 0] = near[:, :HALF].astype(jnp.bfloat16)
        first.start()
        self.k1[u] = near[:, HALF:]
        near = get(2)
        self.sb[u, 0] = near[:, HALF:].astype(jnp.bfloat16)
        second.start()
        self.k2[u] = near[:, :HALF]
        self.k0[u] = get(0)

    def relay(self, u):
        first, second, third, fourth = self.copies(u)
        first.wait_recv()
        self.qa[u] = (self.k2[u] + self.ra[u, 1].astype(jnp.float32)).astype(jnp.bfloat16)
        third.start()
        second.wait_recv()
        self.qb[u] = (self.k1[u] + self.rb[u, 1].astype(jnp.float32)).astype(jnp.bfloat16)
        fourth.start()

    def final(self, u):
        _, _, third, fourth = self.copies(u)
        third.wait_recv()
        fourth.wait_recv()
        own = self.k0[u]
        left = own[:, :HALF] + self.ra[u, 0].astype(jnp.float32) + self.pa[u].astype(jnp.float32)
        right = own[:, HALF:] + self.rb[u, 0].astype(jnp.float32) + self.pb[u].astype(jnp.float32)
        return jnp.concatenate([left, right], axis=1).astype(jnp.bfloat16)

    def drain(self, u):
        for copy in self.copies(u):
            copy.wait_send()


def mix_kernel(
    tok_ref, wg_hbm, wx_hbm, wb_hbm, wdt_ref, cx_ref, cxb_ref, cb_ref, cbb_ref,
    bias_s, rate_s, skip_s, len_s, out_ref,
    tok, wg, wx, wb, rel, xs, xc, bs, halo, bct, bca, bcp, dts, dtg, dtv,
    *rest,
):
    big, rest = rest[:11], rest[11:]
    few, rest = rest[:11], rest[11:]
    (
        w_sem, t_send, t_recv, zu_send, zd_send, z_recv, f_send, f_recv,
        g_send, g_recv, b_send, b_recv, h_send, h_recv, d_send, d_recv,
        e_send, e_recv, a_send, a_recv,
    ) = rest
    s, t = lax.axis_index("seq"), lax.axis_index("tensor")
    tens = 2 * CHIPS
    z, c = t // 2, t % 2
    sibling = (s, 2 * z + 1 - c)
    loads = [
        pltpu.make_async_copy(src, dst, w_sem.at[i])
        for i, (src, dst) in enumerate(((wb_hbm, wb), (wx_hbm, wx), (wg_hbm, wg)))
    ]
    for load in loads:
        load.start()
    along = [(s ^ r, t) for r in range(1, SEQS)]
    across = [(s, lax.rem(t + d, tens)) for d in range(1, tens)]
    enter(along + across)

    depth = wx.shape[0]
    spread = [
        remote(
            tok_ref.at[:, pl.ds(pl.multiple_of(peer[0] * depth, depth), depth)],
            tok.at[z, c, s], t_send.at[i], t_recv.at[i], peer,
        )
        for i, peer in enumerate(along)
    ]
    for copy in spread:
        copy.start()
    tok[z, c, s] = tok_ref[:, pl.ds(pl.multiple_of(s * depth, depth), depth)]

    total = SEQS * SPAN
    pos = lax.broadcasted_iota(jnp.int32, (total, HALF), 0)
    begin, start = jnp.zeros((total, HALF), jnp.int32), jnp.int32(0)
    for r in range(len_s.shape[0]):
        begin = jnp.where(pos >= start, start, begin)
        start = start + len_s[r]
    rel[...] = pos - begin

    first = z - 1 + 2 * ((3 - z) // 3)
    last = 3 * (1 - z // 2)
    order = [z, first, 6 - z - first - last, last]

    def hops(zb):
        part = tok.at[zb, c]
        up = remote(part, part, zu_send.at[zb], z_recv.at[zb], (s, 2 * lax.rem(z + 1, CHIPS) + c))
        down = remote(part, part, zd_send.at[zb], z_recv.at[zb], (s, 2 * lax.rem(z + CHIPS - 1, CHIPS) + c))
        over = remote(part, part, f_send.at[zb], f_recv.at[zb], sibling)
        return up, down, over, (z < CHIPS - 1) & (zb <= z), (z > 0) & (zb >= z)

    def arrive(i):
        zb = order[i]
        up, down, over, goes_up, goes_down = hops(zb)
        if i:
            up.wait_recv()
        else:
            for copy in spread:
                copy.wait_recv()
        pl.when(goes_up)(up.start)
        pl.when(goes_down)(down.start)
        over.start()
        over.wait_recv()

    sums = Sums(big, (g_send, g_recv), s, z, c)
    sumb = Sums(few, (b_send, b_recv), s, z, c)

    def product(rows, w):
        def get(r):
            cols = pl.ds(pl.multiple_of((s ^ r) * WIDE, WIDE), WIDE)
            return jnp.dot(rows, w[:, cols], preferred_element_type=jnp.float32)

        return get

    for i in range(CHIPS):
        arrive(i)
        rows = tok[order[i]].reshape(SPAN, depth)
        if i == 0:
            loads[0].wait()
        bcp[...] = jnp.dot(rows, wb[...], preferred_element_type=jnp.float32).reshape(2, SEQS, OWN, WIDE)
        sumb.emit(i, lambda r: bcp[:, s ^ r].reshape(2 * OWN, WIDE))
        if i == 0:
            loads[1].wait()
        sums.emit(i, product(rows, wx))
        if i:
            sumb.relay(i - 1)
            sums.relay(i - 1)
    sumb.relay(CHIPS - 1)

    def span_rows(q):
        return tok[:, :, q].reshape(SPAN, depth)

    for q in range(SEQS):
        dts[:, q * SPAN : (q + 1) * SPAN] = lax.dot_general(
            wdt_ref[...], span_rows(q), (((1,), (1,)), ((), ())), preferred_element_type=jnp.float32
        ).astype(jnp.bfloat16)
    steps = [
        remote(dts, dtg.at[i], d_send.at[i], d_recv.at[i], peer) for i, peer in enumerate(along)
    ]
    for copy in steps:
        copy.start()
    for i in range(CHIPS):
        bs[pl.ds(pl.multiple_of(16 + order[i] * 2 * OWN, 16), 2 * OWN), :] = sumb.final(i).astype(jnp.float32)
    halo[0] = bs[16 + SPAN - 16 :, :].astype(jnp.bfloat16)
    edge = remote(halo.at[0], halo.at[1], h_send, h_recv, (lax.rem(s + 1, SEQS), t))
    edge.start()
    sums.relay(CHIPS - 1)
    loads[2].wait()
    sums.emit(4, product(span_rows(0), wg))

    edge.wait_recv()
    bs[:16, :] = halo[1].astype(jnp.float32)
    away = rel[pl.ds(pl.multiple_of(s * SPAN, SPAN), SPAN), :1]

    def conv(src, begin, w, bias, away):
        out = w[CONV - 1 :, :] * src[begin : begin + SPAN, :] + bias
        for back in range(1, CONV):
            tap = w[CONV - 1 - back : CONV - back, :] * src[begin - back : begin - back + SPAN, :]
            out = out + jnp.where(away >= back, tap, 0.0)
        return silu(out).astype(jnp.bfloat16)

    bcc = conv(bs, 16, cb_ref[...], cbb_ref[...], away)
    to = lax.broadcasted_iota(jnp.int32, (WIDE, WIDE), 0)
    frm = lax.broadcasted_iota(jnp.int32, (WIDE, WIDE), 1)
    pick = (frm == (to % 32) * GROUPS + to // 32).astype(jnp.float32).astype(jnp.bfloat16)
    bct[...] = (
        lax.dot_general(pick, bcc, (((1,), (1,)), ((), ())), preferred_element_type=jnp.float32)
        .astype(jnp.bfloat16)
        .reshape(GROUPS, 32, SPAN)
    )
    swaps = [
        remote(bct.at[peer[1]], bca.at[s, t], e_send.at[i], e_recv.at[i], peer)
        for i, peer in enumerate(across)
    ]
    for copy in swaps:
        copy.start()
    bca[s, t] = bct[t]
    for i in range(CHIPS):
        full = sums.final(i).astype(jnp.float32).reshape(2, SEQS, OWN, WIDE)
        for half in range(2):
            for q in range(SEQS):
                at = 16 + q * SPAN + half * OWN + order[i] * 2 * OWN
                xs[pl.ds(pl.multiple_of(at, 16), OWN), :] = full[half, q]
    for copy in swaps:
        copy.wait_recv()
    groups = [
        remote(bca.at[s], bca.at[s], a_send.at[i], a_recv.at[i], peer)
        for i, peer in enumerate(along)
    ]
    for copy in groups:
        copy.start()
    sums.emit(5, product(span_rows(1), wg))
    sums.relay(4)
    sums.emit(6, product(span_rows(2), wg))
    sums.emit(7, product(span_rows(3), wg))
    xs[:16, :] = jnp.zeros((16, WIDE), jnp.float32)
    mine = pl.ds(pl.multiple_of(s * WIDE, WIDE), WIDE)
    for q in range(SEQS):
        xc[q * SPAN : (q + 1) * SPAN, :] = conv(
            xs, 16 + q * SPAN, cx_ref[:, mine], cxb_ref[:, mine], rel[q * SPAN : (q + 1) * SPAN, :1]
        ).astype(jnp.float32)
    sums.relay(5)
    for copy in steps:
        copy.wait_recv()
    dtv[...] = (
        dts[...].astype(jnp.float32)
        + dtg[0].astype(jnp.float32)
        + dtg[1].astype(jnp.float32)
        + dtg[2].astype(jnp.float32)
    ).astype(jnp.bfloat16).astype(jnp.float32)
    heads = 4
    line = lax.broadcasted_iota(jnp.int32, (8, total), 0)
    dt8, rate8 = jnp.zeros((8, total), jnp.float32), jnp.zeros((8, total), jnp.float32)
    for h in range(heads):
        row = dtv[pl.ds(heads * s + h, 1), :] + bias_s[heads * s + h]
        row = jnp.maximum(row, 0.0) + jnp.log1p(jnp.exp(-jnp.abs(row)))
        dt8 = jnp.where(line == h, row, dt8)
        dt8 = jnp.where(line == heads + h, row * (-LOG2E * rate_s[heads * s + h]), dt8)

    dif = to - frm
    upto = (dif <= 0).astype(jnp.float32)
    lane = frm // HDIM
    skip = jnp.zeros((1, WIDE), jnp.float32)
    for h in range(heads):
        skip = jnp.where(lane[:1] == h, skip_s[heads * s + h], skip)
    for copy in groups:
        copy.wait_recv()
    state = jnp.zeros((STATE, WIDE), jnp.float32)
    local = to[:, :1]
    for q in range(SEQS):
        here = slice(q * SPAN, (q + 1) * SPAN)
        away = rel[here, :1]
        bt = bca[q, :4].reshape(STATE, SPAN)
        cn = bca[q, 4:].reshape(STATE, SPAN).astype(jnp.float32).T.astype(jnp.bfloat16)
        scores = jnp.dot(cn, bt, preferred_element_type=jnp.float32)
        scores = jnp.where((dif >= 0) & (dif <= away), scores, 0.0)
        both = dt8[:, here]
        cum = jnp.dot(both, upto, precision=HIGH, preferred_element_type=jnp.float32)
        both = jnp.where(line[:, :SPAN] < heads, both, cum)
        cols = jnp.concatenate([both, jnp.zeros((HALF - 8, SPAN), jnp.float32)], axis=0).T

        def expand(first):
            out = jnp.broadcast_to(cols[:, first : first + 1], (SPAN, WIDE))
            for h in range(1, heads):
                out = jnp.where(lane == h, cols[:, first + h : first + h + 1], out)
            return out

        dte, cume = expand(0), expand(heads)
        xv = xc[here, :]
        xdt = xv * dte
        inner = jnp.zeros((SPAN, WIDE), jnp.float32)
        for h in range(heads):
            gap = cols[:, heads + h : heads + h + 1] - both[heads + h : heads + h + 1, :]
            mixing = (jnp.exp2(jnp.minimum(gap, 0.0)) * scores).astype(jnp.bfloat16)
            inner = inner + jnp.dot(
                mixing, jnp.where(lane == h, xdt, 0.0).astype(jnp.bfloat16),
                preferred_element_type=jnp.float32,
            )
        carry = jnp.where(away > local, jnp.exp2(cume), 0.0)
        ends = cume[SPAN - 1 :, :]
        tail = jnp.where(local >= SPAN - 1 - away[SPAN - 1 :, :], jnp.exp2(ends - cume), 0.0)
        fresh = jnp.dot(bt, (tail * xdt).astype(jnp.bfloat16), preferred_element_type=jnp.float32)
        outer = jnp.dot(cn, state.astype(jnp.bfloat16), preferred_element_type=jnp.float32)
        state = carry[SPAN - 1 :, :] * state + fresh
        y = inner + outer * carry + skip * xv
        if q == 0:
            sums.relay(6)
        if q == 1:
            sums.relay(7)
        gate = sums.final(4 + q).astype(jnp.float32)
        out_ref[here, :] = (y * silu(gate)).astype(jnp.bfloat16)

    for zb in range(CHIPS):
        up, down, over, goes_up, goes_down = hops(zb)
        pl.when(goes_up)(up.wait_send)
        pl.when(goes_down)(down.wait_send)
        over.wait_send()
    for copy in spread + steps + [edge] + swaps + groups:
        copy.wait_send()
    for u in range(8):
        sums.drain(u)
    for u in range(4):
        sumb.drain(u)


def mix_in(tokens, w_gate, w_xin, w_bc, w_dt, conv_x, conv_xb, conv_b, conv_bb, bias, rate, skip, lengths):
    depth, width = w_xin.shape
    total = SEQS * SPAN
    dma = pltpu.SemaphoreType.DMA
    vmem, smem, anyw = (pl.BlockSpec(memory_space=m) for m in (pltpu.VMEM, pltpu.SMEM, pl.ANY))
    bf, f32 = jnp.bfloat16, jnp.float32

    def sums(n, rows):
        pair = pltpu.VMEM((n, 2, rows, HALF), bf)
        one = pltpu.VMEM((n, rows, HALF), bf)
        return [pair] * 4 + [one] * 4 + [pltpu.VMEM((n, rows, WIDE), f32)] + [pltpu.VMEM((n, rows, HALF), f32)] * 2

    return pl.pallas_call(
        mix_kernel,
        out_shape=jax.ShapeDtypeStruct((total, WIDE), bf),
        in_specs=[vmem, anyw, anyw, anyw] + [vmem] * 5 + [smem] * 4,
        out_specs=vmem,
        scratch_shapes=[
            pltpu.VMEM((CHIPS, 2, SEQS, OWN, depth), bf),
            pltpu.VMEM(w_gate.shape, bf),
            pltpu.VMEM(w_xin.shape, bf),
            pltpu.VMEM(w_bc.shape, bf),
            pltpu.VMEM((total, HALF), jnp.int32),
            pltpu.VMEM((16 + total, WIDE), f32),
            pltpu.VMEM((total, WIDE), f32),
            pltpu.VMEM((16 + SPAN, WIDE), f32),
            pltpu.VMEM((2, 16, WIDE), bf),
            pltpu.VMEM((GROUPS, 32, SPAN), bf),
            pltpu.VMEM((SEQS, GROUPS, 32, SPAN), bf),
            pltpu.VMEM((2, SEQS, OWN, WIDE), f32),
            pltpu.VMEM((16, total), bf),
            pltpu.VMEM((3, 16, total), bf),
            pltpu.VMEM((16, total), f32),
        ]
        + sums(8, SPAN)
        + sums(4, 2 * OWN)
        + [
            dma((3,)), dma((3,)), dma((3,)), dma((4,)), dma((4,)), dma((4,)), dma((4,)), dma((4,)),
            dma((8, 4)), dma((8, 4)), dma((4, 4)), dma((4, 4)),
            dma, dma, dma((3,)), dma((3,)), dma((7,)), dma((7,)), dma((3,)), dma((3,)),
        ],
        compiler_params=pltpu.CompilerParams(
            collective_id=2, has_side_effects=True, vmem_limit_bytes=52 * 2**20
        ),
    )(
        tokens, w_gate, w_xin, w_bc, w_dt.T, conv_x, conv_xb[None, :], conv_b, conv_bb[None, :],
        bias, rate, skip, lengths,
    )


def shards(
    tokens,
    w_gate,
    w_xin,
    w_bc,
    w_dt,
    conv_x,
    conv_x_bias,
    conv_bc,
    conv_bc_bias,
    dt_bias,
    decay_rate,
    d_skip,
    norm_gain,
    w_out,
    lengths,
):
    seqs = lax.axis_size("seq")
    tens = lax.axis_size("tensor")
    gated = mix_in(
        tokens, w_gate, w_xin, w_bc, w_dt, conv_x, conv_x_bias, conv_bc, conv_bc_bias,
        dt_bias, decay_rate, d_skip, lengths,
    )
    return project_out(gated, norm_gain, w_out, tokens.shape[0], seqs, tens // 2)


def solution(mesh):
    seqs, tens = mesh.shape["seq"], mesh.shape["tensor"]
    narrow = seqs == SEQS and tens == GROUPS == 2 * CHIPS
    body = shards if narrow else shards_wide
    in_specs = (
        P(("seq", "tensor"), None),
        P("seq", "tensor"),
        P("seq", "tensor"),
        P("seq", "tensor"),
        P("seq", "tensor"),
        P(None, "tensor"),
        P("tensor"),
        P(None, "tensor"),
        P("tensor"),
        P("tensor"),
        P("tensor"),
        P("tensor"),
        P("tensor"),
        P("tensor", "seq"),
        P(),
    )
    out_specs = P(("seq", "tensor"), None)
    return jax.shard_map(body, mesh=mesh, in_specs=in_specs, out_specs=out_specs, check_vma=False)
```

```python
import jax
import jax.numpy as jnp
import numpy as np
from jax import lax
from jax.experimental import pallas as pl
from jax.experimental.pallas import tpu as pltpu
from jax.sharding import PartitionSpec as P

HDIM = 64
GROUPS = 8
STATE = 128
CONV = 4
STRETCH = 256
INNER = 8192


HIGH = lax.Precision.HIGHEST


def from_behind(x, axis, by):
    count = lax.axis_size(axis)
    pairs = [(i, i + by) for i in range(count) if 0 <= i + by < count]
    return lax.ppermute(x, axis, pairs)


def carried_in(x, axis, combine, identity):
    count, here = (lax.axis_size(axis), lax.axis_index(axis))
    everything = jax.tree.map(
        lambda part, kind: lax.all_gather(part.astype(kind), axis), x, (jnp.bfloat16, jnp.bfloat16)
    )
    start = jax.tree.map(
        lambda part, zero: jnp.broadcast_to(jnp.asarray(zero, part.dtype), part.shape), x, identity
    )

    def hop(k, before):
        reached = k < here
        new = combine(
            before, jax.tree.map(lambda part, own: part[k].astype(own.dtype), everything, x)
        )
        return jax.tree.map(lambda a, b: jnp.where(reached, a, b), new, before)

    return lax.fori_loop(0, count, hop, start)


def doc_ids(lengths, positions):
    starts = jnp.cumsum(lengths) - lengths
    counted = jnp.sum((starts[None, :] <= positions[:, None]).astype(jnp.int32), axis=1)
    return counted - 1


def causal_conv(values, edge, weights, bias, docs, edge_docs):
    count = values.shape[0]
    extended = jnp.concatenate([edge, values], axis=0).astype(jnp.float32)
    all_docs = jnp.concatenate([edge_docs, docs])
    summed = jnp.zeros(values.shape, jnp.float32) + bias[None, :]
    for offset in range(weights.shape[0]):
        same = (all_docs[offset : offset + count] == docs).astype(jnp.float32)
        summed = (
            summed + weights[offset][None, :] * extended[offset : offset + count] * same[:, None]
        )
    return lax.optimization_barrier(jax.nn.silu(summed).astype(jnp.bfloat16))


def ssd_blocks(xvals, dtv, rate, bmat, cmat, docs, prev_doc, head_group, block):
    count, heads, hdim = xvals.shape
    nstate = bmat.shape[2]
    blocks = count // block
    logs = -dtv * rate[None, :]

    def split(array):
        return array.reshape((blocks, block) + array.shape[1:])

    lower = jnp.tril(jnp.ones((block, block), bool))

    def step(carry, pieces):
        state, last_doc = carry
        xblk, dblk, lblk, bblk, cblk, docblk = pieces
        cum = jnp.cumsum(lblk, axis=0)
        same = (docblk[:, None] == docblk[None, :]) & lower
        diff = cum.T[:, :, None] - cum.T[:, None, :]
        decay = jnp.exp(jnp.where(same[None], diff, -jnp.inf))
        scores = jnp.einsum("ign,jgn->gij", cblk, bblk, precision=HIGH)
        mixing = scores[head_group] * decay * dblk.T[:, None, :]
        inner = jnp.einsum("hij,jhp->ihp", mixing, xblk, precision=HIGH)
        open_in = (docblk == last_doc).astype(jnp.float32)
        carry_in = jnp.exp(cum) * open_in[:, None]
        chead = cblk[:, head_group, :]
        outer = jnp.einsum("ihn,hpn->ihp", chead, state, precision=HIGH) * carry_in[:, :, None]
        end_doc = docblk[-1]
        tail = (
            jnp.exp(cum[-1][None, :] - cum)
            * (docblk == end_doc).astype(jnp.float32)[:, None]
            * dblk
        )
        bhead = bblk[:, head_group, :]
        fresh = jnp.einsum("jh,jhp,jhn->hpn", tail, xblk, bhead, precision=HIGH)
        state = carry_in[-1][:, None, None] * state + fresh
        return ((state, end_doc), inner + outer)

    init = (jnp.zeros((heads, hdim, nstate), jnp.float32), prev_doc)
    (state, end_doc), outs = lax.scan(
        step, init, (split(xvals), split(dtv), split(logs), split(bmat), split(cmat), split(docs))
    )
    return (outs.reshape(count, heads, hdim), state)


def shards_wide(
    tokens,
    w_gate,
    w_xin,
    w_bc,
    w_dt,
    conv_x,
    conv_x_bias,
    conv_bc,
    conv_bc_bias,
    dt_bias,
    decay_rate,
    d_skip,
    norm_gain,
    w_out,
    lengths,
):
    tensor_count = lax.axis_size("tensor")
    seq_index = lax.axis_index("seq")
    tensor_index = lax.axis_index("tensor")
    span_rows = lax.all_gather(tokens, "tensor", axis=0, tiled=True)
    span_len = span_rows.shape[0]
    pieces = (
        lax.all_gather(w_gate, "seq", axis=0, tiled=True),
        lax.all_gather(w_xin, "seq", axis=0, tiled=True),
        lax.all_gather(w_bc, "seq", axis=0, tiled=True),
        lax.all_gather(w_dt, "seq", axis=0, tiled=True),
    )
    gate_acc, xin_acc, bc_acc, dt_acc = tuple(
        (
            jnp.dot(span_rows, weight_piece, preferred_element_type=jnp.float32)
            for weight_piece in pieces
        )
    )
    gate = gate_acc.astype(jnp.bfloat16)
    xin = xin_acc.astype(jnp.bfloat16)
    bcin = bc_acc.astype(jnp.bfloat16)
    dtin = dt_acc.astype(jnp.bfloat16)
    gate, xin, bcin, dtin = lax.optimization_barrier((gate, xin, bcin, dtin))
    positions = seq_index * span_len + jnp.arange(span_len, dtype=jnp.int32)
    docs = doc_ids(lengths, positions)
    edge_docs = doc_ids(lengths, seq_index * span_len + jnp.arange(-(CONV - 1), 0, dtype=jnp.int32))
    prev_span_doc = doc_ids(lengths, positions[:1] - 1)[0]
    edge_x, edge_bc = from_behind(
        (xin[span_len - (CONV - 1) :], bcin[span_len - (CONV - 1) :]), "seq", 1
    )
    x_conv = causal_conv(xin, edge_x, conv_x, conv_x_bias, docs, edge_docs)
    bc_conv = causal_conv(bcin, edge_bc, conv_bc, conv_bc_bias, docs, edge_docs)
    group_span = tensor_count // GROUPS
    my_group = tensor_index // group_span
    every_group = lax.all_gather(bc_conv, "tensor", axis=1, tiled=True)
    arranged = every_group.reshape(span_len, 2 * STATE, GROUPS)
    group_cols = lax.dynamic_slice_in_dim(arranged, my_group, 1, 2).reshape(span_len, 2 * STATE)
    head_dev = w_dt.shape[1]
    head_group = np.zeros(head_dev, dtype=np.int32)
    both = group_cols.astype(jnp.float32)
    bmat = both[:, None, :STATE]
    cmat = both[:, None, STATE:]
    xvals = x_conv.astype(jnp.float32).reshape(span_len, head_dev, HDIM)
    dtv = jax.nn.softplus(dtin.astype(jnp.float32) + dt_bias[None, :])
    block = min(STRETCH, span_len)
    y_local, end_state = ssd_blocks(
        xvals, dtv, decay_rate, bmat, cmat, docs, prev_span_doc, head_group, block
    )
    cum_span = jnp.cumsum(-dtv * decay_rate[None, :], axis=0)
    open_span = (docs == prev_span_doc).astype(jnp.float32)
    span_decay = jnp.exp(cum_span[-1]) * open_span[-1]

    def combine(earlier, later):
        return (earlier[0] * later[0], later[0][:, None, None] * earlier[1] + later[1])

    entering = carried_in(
        (span_decay, end_state),
        "seq",
        combine,
        (jnp.ones_like(span_decay), jnp.zeros_like(end_state)),
    )[1]
    carried = jnp.exp(cum_span) * open_span[:, None]
    y_enter = (
        jnp.einsum("ihn,hpn->ihp", cmat[:, head_group, :], entering, precision=HIGH)
        * carried[:, :, None]
    )
    yvals = (y_local + y_enter + d_skip[None, :, None] * xvals).reshape(span_len, head_dev * HDIM)
    gated = yvals * jax.nn.silu(gate.astype(jnp.float32))
    local_sq = jnp.sum(gated * gated, axis=1)
    group_mark = (jnp.arange(GROUPS) == my_group).astype(jnp.float32)
    every_sum = lax.psum(local_sq[:, None] * group_mark[None, :], "tensor")
    group_mean = jnp.sum(every_sum * group_mark[None, :], axis=1) / (INNER // GROUPS)
    normed = (gated * lax.rsqrt(group_mean + 1e-05)[:, None] * norm_gain[None, :]).astype(
        jnp.bfloat16
    )
    w_full = lax.all_gather(w_out, "seq", axis=1, tiled=True)
    return lax.psum_scatter(
        jnp.dot(normed, w_full, preferred_element_type=jnp.float32).astype(jnp.bfloat16),
        "tensor",
        scatter_dimension=0,
        tiled=True,
    )


def enter(peers):
    barrier = pltpu.get_barrier_semaphore()
    for peer in peers:
        pl.semaphore_signal(barrier, inc=1, device_id=peer, device_id_type=pl.DeviceIdType.MESH)
    pl.semaphore_wait(barrier, len(peers))


def remote(src, dst, send, recv, peer):
    return pltpu.make_async_remote_copy(
        src_ref=src,
        dst_ref=dst,
        send_sem=send,
        recv_sem=recv,
        device_id=peer,
        device_id_type=pl.DeviceIdType.MESH,
    )


SEQS, CHIPS, OWN, SPAN, WIDE, HALF = 4, 4, 32, 256, 256, 128
LOG2E = 1.4426950408889634


def silu(v):
    return v / (1.0 + jnp.exp(-v))


class Sums:
    def __init__(self, bufs, sems, s, z, c):
        self.sa, self.sb, self.ra, self.rb, self.qa, self.qb, self.pa, self.pb, self.k0, self.k1, self.k2 = bufs
        self.sems = sems
        self.x, self.y = (s ^ 1, 2 * z + c), (s ^ 2, 2 * z + c)

    def copies(self, u):
        send, recv = self.sems
        return (
            remote(self.sa.at[u], self.ra.at[u], send.at[u, 0], recv.at[u, 0], self.x),
            remote(self.sb.at[u], self.rb.at[u], send.at[u, 1], recv.at[u, 1], self.y),
            remote(self.qa.at[u], self.pa.at[u], send.at[u, 2], recv.at[u, 2], self.y),
            remote(self.qb.at[u], self.pb.at[u], send.at[u, 3], recv.at[u, 3], self.x),
        )

    def emit(self, u, get):
        first, second, _, _ = self.copies(u)
        far = get(3)
        self.sa[u, 1] = far[:, :HALF].astype(jnp.bfloat16)
        self.sb[u, 1] = far[:, HALF:].astype(jnp.bfloat16)
        near = get(1)
        self.sa[u, 0] = near[:, :HALF].astype(jnp.bfloat16)
        first.start()
        self.k1[u] = near[:, HALF:]
        near = get(2)
        self.sb[u, 0] = near[:, HALF:].astype(jnp.bfloat16)
        second.start()
        self.k2[u] = near[:, :HALF]
        self.k0[u] = get(0)

    def relay(self, u):
        first, second, third, fourth = self.copies(u)
        first.wait_recv()
        self.qa[u] = (self.k2[u] + self.ra[u, 1].astype(jnp.float32)).astype(jnp.bfloat16)
        third.start()
        second.wait_recv()
        self.qb[u] = (self.k1[u] + self.rb[u, 1].astype(jnp.float32)).astype(jnp.bfloat16)
        fourth.start()

    def final(self, u):
        _, _, third, fourth = self.copies(u)
        third.wait_recv()
        fourth.wait_recv()
        own = self.k0[u]
        left = own[:, :HALF] + self.ra[u, 0].astype(jnp.float32) + self.pa[u].astype(jnp.float32)
        right = own[:, HALF:] + self.rb[u, 0].astype(jnp.float32) + self.pb[u].astype(jnp.float32)
        return jnp.concatenate([left, right], axis=1).astype(jnp.bfloat16)

    def drain(self, u):
        for copy in self.copies(u):
            copy.wait_send()


def mix_kernel(
    tok_hbm, wg_hbm, wx_hbm, wb_hbm, wdt_hbm, cx_hbm, cxb_hbm, cb_hbm, cbb_hbm, gain_hbm, wo_hbm,
    bias_hbm, rate_hbm, skip_hbm, len_hbm, out_ref,
    wg, wx, wb, wdt, cx, cxb, cb, cbb, gain, wo, bias_s, rate_s, skip_s, len_s,
    tok, rel, xs, xc, bs, halo, bct, bca, bcp, dts, dtg, dtv,
    held, normed, part, sib, pair, got, done, res,
    *rest,
):
    big, rest = rest[:11], rest[11:]
    few, rest = rest[:11], rest[11:]
    (
        w_sem, t_send, t_recv, zu_send, zd_send, z_recv, f_send, f_recv,
        g_send, g_recv, b_send, b_recv, h_send, h_recv, d_send, d_recv,
        e_send, e_recv, a_send, a_recv,
        y_send, y_recv, p_send, p_recv, r_send, r_recv, o_send, o_recv,
    ) = rest
    s, t = lax.axis_index("seq"), lax.axis_index("tensor")
    tens = 2 * CHIPS
    z, c = t // 2, t % 2
    sibling = (s, 2 * z + 1 - c)
    depth = wx.shape[0]
    own_cols = pl.ds(pl.multiple_of(s * depth, depth), depth)
    loads = [
        pltpu.make_async_copy(src, dst, w_sem.at[i])
        for i, (src, dst) in enumerate((
            (len_hbm, len_s), (tok_hbm.at[:, own_cols], tok.at[z, c, s]), (wb_hbm, wb), (wx_hbm, wx),
            (wdt_hbm, wdt), (wg_hbm, wg), (cb_hbm, cb), (cbb_hbm, cbb), (cx_hbm, cx), (cxb_hbm, cxb),
            (bias_hbm, bias_s), (rate_hbm, rate_s), (skip_hbm, skip_s), (gain_hbm, gain), (wo_hbm, wo),
        ))
    ]
    for load in loads:
        load.start()
    along = [(s ^ r, t) for r in range(1, SEQS)]
    across = [(s, lax.rem(t + d, tens)) for d in range(1, tens)]
    enter(along + across)

    spread = [
        remote(
            tok_hbm.at[:, pl.ds(pl.multiple_of(peer[0] * depth, depth), depth)],
            tok.at[z, c, s], t_send.at[i], t_recv.at[i], peer,
        )
        for i, peer in enumerate(along)
    ]
    for copy in spread:
        copy.start()
    loads[0].wait()

    total = SEQS * SPAN
    pos = lax.broadcasted_iota(jnp.int32, (total, HALF), 0)
    begin, start = jnp.zeros((total, HALF), jnp.int32), jnp.int32(0)
    for r in range(len_s.shape[0]):
        begin = jnp.where(pos >= start, start, begin)
        start = start + len_s[r]
    rel[...] = pos - begin

    first = z - 1 + 2 * ((3 - z) // 3)
    last = 3 * (1 - z // 2)
    order = [z, first, 6 - z - first - last, last]

    def hops(zb):
        part = tok.at[zb, c]
        up = remote(part, part, zu_send.at[zb], z_recv.at[zb], (s, 2 * lax.rem(z + 1, CHIPS) + c))
        down = remote(part, part, zd_send.at[zb], z_recv.at[zb], (s, 2 * lax.rem(z + CHIPS - 1, CHIPS) + c))
        over = remote(part, part, f_send.at[zb], f_recv.at[zb], sibling)
        return up, down, over, (z < CHIPS - 1) & (zb <= z), (z > 0) & (zb >= z)

    def arrive(i):
        zb = order[i]
        up, down, over, goes_up, goes_down = hops(zb)
        if i:
            up.wait_recv()
        else:
            loads[1].wait()
            for copy in spread:
                copy.wait_recv()
        pl.when(goes_up)(up.start)
        pl.when(goes_down)(down.start)
        over.start()
        over.wait_recv()

    sums = Sums(big, (g_send, g_recv), s, z, c)
    sumb = Sums(few, (b_send, b_recv), s, z, c)

    def product(rows, w):
        def get(r):
            cols = pl.ds(pl.multiple_of((s ^ r) * WIDE, WIDE), WIDE)
            return jnp.dot(rows, w[:, cols], preferred_element_type=jnp.float32)

        return get

    for i in range(CHIPS):
        arrive(i)
        rows = tok[order[i]].reshape(SPAN, depth)
        if i == 0:
            loads[2].wait()
        bcp[...] = jnp.dot(rows, wb[...], preferred_element_type=jnp.float32).reshape(2, SEQS, OWN, WIDE)
        sumb.emit(i, lambda r: bcp[:, s ^ r].reshape(2 * OWN, WIDE))
        if i == 0:
            loads[3].wait()
        sums.emit(i, product(rows, wx))
        if i:
            sumb.relay(i - 1)
            sums.relay(i - 1)
    sumb.relay(CHIPS - 1)

    def span_rows(q):
        return tok[:, :, q].reshape(SPAN, depth)

    loads[4].wait()
    for q in range(SEQS):
        dts[:, q * SPAN : (q + 1) * SPAN] = lax.dot_general(
            wdt[...], span_rows(q), (((1,), (1,)), ((), ())), preferred_element_type=jnp.float32
        ).astype(jnp.bfloat16)
    steps = [
        remote(dts, dtg.at[i], d_send.at[i], d_recv.at[i], peer) for i, peer in enumerate(along)
    ]
    for copy in steps:
        copy.start()
    for i in range(CHIPS):
        bs[pl.ds(pl.multiple_of(16 + order[i] * 2 * OWN, 16), 2 * OWN), :] = sumb.final(i).astype(jnp.float32)
    halo[0] = bs[16 + SPAN - 16 :, :].astype(jnp.bfloat16)
    edge = remote(halo.at[0], halo.at[1], h_send, h_recv, (lax.rem(s + 1, SEQS), t))
    edge.start()
    sums.relay(CHIPS - 1)
    loads[5].wait()
    sums.emit(4, product(span_rows(0), wg))

    for load in loads[6:]:
        load.wait()
    edge.wait_recv()
    bs[:16, :] = halo[1].astype(jnp.float32)
    away = rel[pl.ds(pl.multiple_of(s * SPAN, SPAN), SPAN), :1]

    def conv(src, begin, w, bias, away):
        out = w[CONV - 1 :, :] * src[begin : begin + SPAN, :] + bias
        for back in range(1, CONV):
            tap = w[CONV - 1 - back : CONV - back, :] * src[begin - back : begin - back + SPAN, :]
            out = out + jnp.where(away >= back, tap, 0.0)
        return silu(out).astype(jnp.bfloat16)

    bcc = conv(bs, 16, cb[...], cbb[...], away)
    to = lax.broadcasted_iota(jnp.int32, (WIDE, WIDE), 0)
    frm = lax.broadcasted_iota(jnp.int32, (WIDE, WIDE), 1)
    pick = (frm == (to % 32) * GROUPS + to // 32).astype(jnp.float32).astype(jnp.bfloat16)
    bct[...] = (
        lax.dot_general(pick, bcc, (((1,), (1,)), ((), ())), preferred_element_type=jnp.float32)
        .astype(jnp.bfloat16)
        .reshape(GROUPS, 32, SPAN)
    )
    swaps = [
        remote(bct.at[peer[1]], bca.at[s, t], e_send.at[i], e_recv.at[i], peer)
        for i, peer in enumerate(across)
    ]
    for copy in swaps:
        copy.start()
    bca[s, t] = bct[t]
    for i in range(CHIPS):
        full = sums.final(i).astype(jnp.float32).reshape(2, SEQS, OWN, WIDE)
        for half in range(2):
            for q in range(SEQS):
                at = 16 + q * SPAN + half * OWN + order[i] * 2 * OWN
                xs[pl.ds(pl.multiple_of(at, 16), OWN), :] = full[half, q]
    for copy in swaps:
        copy.wait_recv()
    groups = [
        remote(bca.at[s], bca.at[s], a_send.at[i], a_recv.at[i], peer)
        for i, peer in enumerate(along)
    ]
    for copy in groups:
        copy.start()
    sums.emit(5, product(span_rows(1), wg))
    sums.relay(4)
    sums.emit(6, product(span_rows(2), wg))
    sums.emit(7, product(span_rows(3), wg))
    xs[:16, :] = jnp.zeros((16, WIDE), jnp.float32)
    mine = pl.ds(pl.multiple_of(s * WIDE, WIDE), WIDE)
    for q in range(SEQS):
        xc[q * SPAN : (q + 1) * SPAN, :] = conv(
            xs, 16 + q * SPAN, cx[:, mine], cxb[:, mine], rel[q * SPAN : (q + 1) * SPAN, :1]
        ).astype(jnp.float32)
    sums.relay(5)
    for copy in steps:
        copy.wait_recv()
    dtv[...] = (
        dts[...].astype(jnp.float32)
        + dtg[0].astype(jnp.float32)
        + dtg[1].astype(jnp.float32)
        + dtg[2].astype(jnp.float32)
    ).astype(jnp.bfloat16).astype(jnp.float32)
    heads = 4
    line = lax.broadcasted_iota(jnp.int32, (8, total), 0)
    dt8, rate8 = jnp.zeros((8, total), jnp.float32), jnp.zeros((8, total), jnp.float32)
    for h in range(heads):
        row = dtv[pl.ds(heads * s + h, 1), :] + bias_s[heads * s + h]
        row = jnp.maximum(row, 0.0) + jnp.log1p(jnp.exp(-jnp.abs(row)))
        dt8 = jnp.where(line == h, row, dt8)
        dt8 = jnp.where(line == heads + h, row * (-LOG2E * rate_s[heads * s + h]), dt8)

    dif = to - frm
    upto = (dif <= 0).astype(jnp.float32)
    lane = frm // HDIM
    skip = jnp.zeros((1, WIDE), jnp.float32)
    for h in range(heads):
        skip = jnp.where(lane[:1] == h, skip_s[heads * s + h], skip)
    for copy in groups:
        copy.wait_recv()

    cols_out = wo.shape[1]
    gathers = [
        [
            remote(held.at[s, q], held.at[s, q], y_send.at[q, i], y_recv.at[q, i], peer)
            for i, peer in enumerate(along)
        ]
        for q in range(SEQS)
    ]
    pairs = [
        remote(part.at[q, 1 - c], sib.at[q], p_send.at[q], p_recv.at[q], sibling) for q in range(SEQS)
    ]

    def reduces(q):
        peers = [lax.rem(z + d, CHIPS) for d in range(1, CHIPS)]
        return [
            remote(pair.at[q, to], got.at[q, i], r_send.at[q, i], r_recv.at[q, i], (s, 2 * to + c))
            for i, to in enumerate(peers)
        ]

    def deliver(q, frm):
        return remote(done.at[q], res.at[frm], o_send.at[q], o_recv.at[frm], (q, t))

    def project(q):
        for copy in gathers[q]:
            copy.wait_recv()
        squares = jnp.zeros((SPAN, WIDE), jnp.float32)
        for k in range(SEQS):
            piece = held[k, q].astype(jnp.float32)
            squares = squares + piece * piece
        scale = lax.rsqrt(jnp.sum(squares, axis=1, keepdims=True) / (SEQS * WIDE) + 1e-05)
        for k in range(SEQS):
            wide = slice(k * WIDE, (k + 1) * WIDE)
            normed[:, wide] = (held[k, q].astype(jnp.float32) * scale * gain[:, wide]).astype(jnp.bfloat16)
        for n in range(cols_out // WIDE):
            wide = slice(n * WIDE, (n + 1) * WIDE)
            acc = jnp.dot(normed[...], wo[:, wide], preferred_element_type=jnp.float32)
            acc = acc.astype(jnp.bfloat16).reshape(CHIPS, 2, OWN, WIDE)
            for half in range(2):
                part[q, half, :, :, wide] = acc[:, half]
        pairs[q].start()

    def combine(q):
        pairs[q].wait_recv()
        pair[q] = (part[q, c].astype(jnp.float32) + sib[q].astype(jnp.float32)).astype(jnp.bfloat16)
        for copy in reduces(q):
            copy.start()

    def collect(q):
        for copy in reduces(q):
            copy.wait_recv()
        total = pair[q, z].astype(jnp.float32)
        for i in range(CHIPS - 1):
            total = total + got[q, i].astype(jnp.float32)
        done[q] = total.astype(jnp.bfloat16)
        pl.when(s != q)(deliver(q, s).start)

        @pl.when(s == q)
        def _():
            res[q] = done[q]

    state = jnp.zeros((STATE, WIDE), jnp.float32)
    local = to[:, :1]
    for q in range(SEQS):
        here = slice(q * SPAN, (q + 1) * SPAN)
        away = rel[here, :1]
        bt = bca[q, :4].reshape(STATE, SPAN)
        cn = bca[q, 4:].reshape(STATE, SPAN).astype(jnp.float32).T.astype(jnp.bfloat16)
        scores = jnp.dot(cn, bt, preferred_element_type=jnp.float32)
        scores = jnp.where((dif >= 0) & (dif <= away), scores, 0.0)
        both = dt8[:, here]
        cum = jnp.dot(both, upto, precision=HIGH, preferred_element_type=jnp.float32)
        both = jnp.where(line[:, :SPAN] < heads, both, cum)
        cols = jnp.concatenate([both, jnp.zeros((HALF - 8, SPAN), jnp.float32)], axis=0).T

        def expand(first):
            out = jnp.broadcast_to(cols[:, first : first + 1], (SPAN, WIDE))
            for h in range(1, heads):
                out = jnp.where(lane == h, cols[:, first + h : first + h + 1], out)
            return out

        dte, cume = expand(0), expand(heads)
        xv = xc[here, :]
        xdt = xv * dte
        inner = jnp.zeros((SPAN, WIDE), jnp.float32)
        for h in range(heads):
            gap = cols[:, heads + h : heads + h + 1] - both[heads + h : heads + h + 1, :]
            mixing = (jnp.exp2(jnp.minimum(gap, 0.0)) * scores).astype(jnp.bfloat16)
            inner = inner + jnp.dot(
                mixing, jnp.where(lane == h, xdt, 0.0).astype(jnp.bfloat16),
                preferred_element_type=jnp.float32,
            )
        carry = jnp.where(away > local, jnp.exp2(cume), 0.0)
        ends = cume[SPAN - 1 :, :]
        tail = jnp.where(local >= SPAN - 1 - away[SPAN - 1 :, :], jnp.exp2(ends - cume), 0.0)
        fresh = jnp.dot(bt, (tail * xdt).astype(jnp.bfloat16), preferred_element_type=jnp.float32)
        outer = jnp.dot(cn, state.astype(jnp.bfloat16), preferred_element_type=jnp.float32)
        state = carry[SPAN - 1 :, :] * state + fresh
        y = inner + outer * carry + skip * xv
        if q == 0:
            sums.relay(6)
        if q == 1:
            sums.relay(7)
        gate = sums.final(4 + q).astype(jnp.float32)
        held[s, q] = (y * silu(gate)).astype(jnp.bfloat16)
        for copy in gathers[q]:
            copy.start()
        if q:
            project(q - 1)
        if q > 1:
            combine(q - 2)
    project(SEQS - 1)
    combine(SEQS - 2)
    collect(0)
    collect(SEQS - 3)
    combine(SEQS - 1)
    collect(SEQS - 2)
    collect(SEQS - 1)
    for q in range(SEQS):
        pl.when(s != q)(deliver(0, q).wait_recv)
        out_ref[:, q * cols_out : (q + 1) * cols_out] = res[q]

    for zb in range(CHIPS):
        up, down, over, goes_up, goes_down = hops(zb)
        pl.when(goes_up)(up.wait_send)
        pl.when(goes_down)(down.wait_send)
        over.wait_send()
    for copy in spread + steps + [edge] + swaps + groups:
        copy.wait_send()
    for q in range(SEQS):
        for copy in gathers[q] + [pairs[q]] + reduces(q):
            copy.wait_send()
        pl.when(s != q)(deliver(q, s).wait_send)
    for u in range(8):
        sums.drain(u)
    for u in range(4):
        sumb.drain(u)


def mix(operands, own, seqs):
    tokens, w_gate, w_xin, w_bc, w_dt, conv_x, conv_xb, conv_b, conv_bb, gain, w_out = operands[:11]
    depth = w_xin.shape[0]
    total = SEQS * SPAN
    cols = w_out.shape[1]
    dma = pltpu.SemaphoreType.DMA
    bf, f32 = jnp.bfloat16, jnp.float32

    def sums(n, rows):
        pair = pltpu.VMEM((n, 2, rows, HALF), bf)
        one = pltpu.VMEM((n, rows, HALF), bf)
        return [pair] * 4 + [one] * 4 + [pltpu.VMEM((n, rows, WIDE), f32)] + [pltpu.VMEM((n, rows, HALF), f32)] * 2

    return pl.pallas_call(
        mix_kernel,
        out_shape=jax.ShapeDtypeStruct((own, cols * seqs), bf),
        in_specs=[pl.BlockSpec(memory_space=pl.ANY)] * len(operands),
        out_specs=pl.BlockSpec(memory_space=pltpu.VMEM),
        scratch_shapes=[pltpu.VMEM(a.shape, a.dtype) for a in operands[1:11]]
        + [pltpu.SMEM(a.shape, a.dtype) for a in operands[11:]]
        + [
            pltpu.VMEM((CHIPS, 2, SEQS, OWN, depth), bf),
            pltpu.VMEM((total, HALF), jnp.int32),
            pltpu.VMEM((16 + total, WIDE), f32),
            pltpu.VMEM((total, WIDE), f32),
            pltpu.VMEM((16 + SPAN, WIDE), f32),
            pltpu.VMEM((2, 16, WIDE), bf),
            pltpu.VMEM((GROUPS, 32, SPAN), bf),
            pltpu.VMEM((SEQS, GROUPS, 32, SPAN), bf),
            pltpu.VMEM((2, SEQS, OWN, WIDE), f32),
            pltpu.VMEM((16, total), bf),
            pltpu.VMEM((3, 16, total), bf),
            pltpu.VMEM((16, total), f32),
            pltpu.VMEM((SEQS, SEQS, SPAN, WIDE), bf),
            pltpu.VMEM((SPAN, SEQS * WIDE), bf),
            pltpu.VMEM((SEQS, 2, CHIPS, OWN, cols), bf),
            pltpu.VMEM((SEQS, CHIPS, OWN, cols), bf),
            pltpu.VMEM((SEQS, CHIPS, OWN, cols), bf),
            pltpu.VMEM((SEQS, CHIPS - 1, OWN, cols), bf),
            pltpu.VMEM((SEQS, OWN, cols), bf),
            pltpu.VMEM((SEQS, OWN, cols), bf),
        ]
        + sums(8, SPAN)
        + sums(4, 2 * OWN)
        + [
            dma((15,)), dma((3,)), dma((3,)), dma((4,)), dma((4,)), dma((4,)), dma((4,)), dma((4,)),
            dma((8, 4)), dma((8, 4)), dma((4, 4)), dma((4, 4)),
            dma, dma, dma((3,)), dma((3,)), dma((7,)), dma((7,)), dma((3,)), dma((3,)),
            dma((4, 3)), dma((4, 3)), dma((4,)), dma((4,)), dma((4, 3)), dma((4, 3)), dma((4,)), dma((4,)),
        ],
        compiler_params=pltpu.CompilerParams(
            collective_id=2, has_side_effects=True, vmem_limit_bytes=56 * 2**20
        ),
    )(*operands)


def shards(
    tokens,
    w_gate,
    w_xin,
    w_bc,
    w_dt,
    conv_x,
    conv_x_bias,
    conv_bc,
    conv_bc_bias,
    dt_bias,
    decay_rate,
    d_skip,
    norm_gain,
    w_out,
    lengths,
):
    operands = (
        tokens, w_gate, w_xin, w_bc, w_dt.T, conv_x, conv_x_bias[None, :], conv_bc, conv_bc_bias[None, :],
        norm_gain[None, :], w_out, dt_bias, decay_rate, d_skip, lengths,
    )
    return mix(operands, tokens.shape[0], lax.axis_size("seq"))


def solution(mesh):
    seqs, tens = mesh.shape["seq"], mesh.shape["tensor"]
    narrow = seqs == SEQS and tens == GROUPS == 2 * CHIPS
    body = shards if narrow else shards_wide
    in_specs = (
        P(("seq", "tensor"), None),
        P("seq", "tensor"),
        P("seq", "tensor"),
        P("seq", "tensor"),
        P("seq", "tensor"),
        P(None, "tensor"),
        P("tensor"),
        P(None, "tensor"),
        P("tensor"),
        P("tensor"),
        P("tensor"),
        P("tensor"),
        P("tensor"),
        P("tensor", "seq"),
        P(),
    )
    out_specs = P(("seq", "tensor"), None)
    return jax.shard_map(body, mesh=mesh, in_specs=in_specs, out_specs=out_specs, check_vma=False)
```

```python
import jax
import jax.numpy as jnp
import numpy as np
from jax import lax
from jax.experimental import pallas as pl
from jax.experimental.pallas import tpu as pltpu
from jax.sharding import PartitionSpec as P

HDIM = 64
GROUPS = 8
STATE = 128
CONV = 4
STRETCH = 256
INNER = 8192


HIGH = lax.Precision.HIGHEST


def from_behind(x, axis, by):
    count = lax.axis_size(axis)
    pairs = [(i, i + by) for i in range(count) if 0 <= i + by < count]
    return lax.ppermute(x, axis, pairs)


def carried_in(x, axis, combine, identity):
    count, here = (lax.axis_size(axis), lax.axis_index(axis))
    everything = jax.tree.map(
        lambda part, kind: lax.all_gather(part.astype(kind), axis), x, (jnp.bfloat16, jnp.bfloat16)
    )
    start = jax.tree.map(
        lambda part, zero: jnp.broadcast_to(jnp.asarray(zero, part.dtype), part.shape), x, identity
    )

    def hop(k, before):
        reached = k < here
        new = combine(
            before, jax.tree.map(lambda part, own: part[k].astype(own.dtype), everything, x)
        )
        return jax.tree.map(lambda a, b: jnp.where(reached, a, b), new, before)

    return lax.fori_loop(0, count, hop, start)


def doc_ids(lengths, positions):
    starts = jnp.cumsum(lengths) - lengths
    counted = jnp.sum((starts[None, :] <= positions[:, None]).astype(jnp.int32), axis=1)
    return counted - 1


def causal_conv(values, edge, weights, bias, docs, edge_docs):
    count = values.shape[0]
    extended = jnp.concatenate([edge, values], axis=0).astype(jnp.float32)
    all_docs = jnp.concatenate([edge_docs, docs])
    summed = jnp.zeros(values.shape, jnp.float32) + bias[None, :]
    for offset in range(weights.shape[0]):
        same = (all_docs[offset : offset + count] == docs).astype(jnp.float32)
        summed = (
            summed + weights[offset][None, :] * extended[offset : offset + count] * same[:, None]
        )
    return lax.optimization_barrier(jax.nn.silu(summed).astype(jnp.bfloat16))


def ssd_blocks(xvals, dtv, rate, bmat, cmat, docs, prev_doc, head_group, block):
    count, heads, hdim = xvals.shape
    nstate = bmat.shape[2]
    blocks = count // block
    logs = -dtv * rate[None, :]

    def split(array):
        return array.reshape((blocks, block) + array.shape[1:])

    lower = jnp.tril(jnp.ones((block, block), bool))

    def step(carry, pieces):
        state, last_doc = carry
        xblk, dblk, lblk, bblk, cblk, docblk = pieces
        cum = jnp.cumsum(lblk, axis=0)
        same = (docblk[:, None] == docblk[None, :]) & lower
        diff = cum.T[:, :, None] - cum.T[:, None, :]
        decay = jnp.exp(jnp.where(same[None], diff, -jnp.inf))
        scores = jnp.einsum("ign,jgn->gij", cblk, bblk, precision=HIGH)
        mixing = scores[head_group] * decay * dblk.T[:, None, :]
        inner = jnp.einsum("hij,jhp->ihp", mixing, xblk, precision=HIGH)
        open_in = (docblk == last_doc).astype(jnp.float32)
        carry_in = jnp.exp(cum) * open_in[:, None]
        chead = cblk[:, head_group, :]
        outer = jnp.einsum("ihn,hpn->ihp", chead, state, precision=HIGH) * carry_in[:, :, None]
        end_doc = docblk[-1]
        tail = (
            jnp.exp(cum[-1][None, :] - cum)
            * (docblk == end_doc).astype(jnp.float32)[:, None]
            * dblk
        )
        bhead = bblk[:, head_group, :]
        fresh = jnp.einsum("jh,jhp,jhn->hpn", tail, xblk, bhead, precision=HIGH)
        state = carry_in[-1][:, None, None] * state + fresh
        return ((state, end_doc), inner + outer)

    init = (jnp.zeros((heads, hdim, nstate), jnp.float32), prev_doc)
    (state, end_doc), outs = lax.scan(
        step, init, (split(xvals), split(dtv), split(logs), split(bmat), split(cmat), split(docs))
    )
    return (outs.reshape(count, heads, hdim), state)


def shards_wide(
    tokens,
    w_gate,
    w_xin,
    w_bc,
    w_dt,
    conv_x,
    conv_x_bias,
    conv_bc,
    conv_bc_bias,
    dt_bias,
    decay_rate,
    d_skip,
    norm_gain,
    w_out,
    lengths,
):
    tensor_count = lax.axis_size("tensor")
    seq_index = lax.axis_index("seq")
    tensor_index = lax.axis_index("tensor")
    span_rows = lax.all_gather(tokens, "tensor", axis=0, tiled=True)
    span_len = span_rows.shape[0]
    pieces = (
        lax.all_gather(w_gate, "seq", axis=0, tiled=True),
        lax.all_gather(w_xin, "seq", axis=0, tiled=True),
        lax.all_gather(w_bc, "seq", axis=0, tiled=True),
        lax.all_gather(w_dt, "seq", axis=0, tiled=True),
    )
    gate_acc, xin_acc, bc_acc, dt_acc = tuple(
        (
            jnp.dot(span_rows, weight_piece, preferred_element_type=jnp.float32)
            for weight_piece in pieces
        )
    )
    gate = gate_acc.astype(jnp.bfloat16)
    xin = xin_acc.astype(jnp.bfloat16)
    bcin = bc_acc.astype(jnp.bfloat16)
    dtin = dt_acc.astype(jnp.bfloat16)
    gate, xin, bcin, dtin = lax.optimization_barrier((gate, xin, bcin, dtin))
    positions = seq_index * span_len + jnp.arange(span_len, dtype=jnp.int32)
    docs = doc_ids(lengths, positions)
    edge_docs = doc_ids(lengths, seq_index * span_len + jnp.arange(-(CONV - 1), 0, dtype=jnp.int32))
    prev_span_doc = doc_ids(lengths, positions[:1] - 1)[0]
    edge_x, edge_bc = from_behind(
        (xin[span_len - (CONV - 1) :], bcin[span_len - (CONV - 1) :]), "seq", 1
    )
    x_conv = causal_conv(xin, edge_x, conv_x, conv_x_bias, docs, edge_docs)
    bc_conv = causal_conv(bcin, edge_bc, conv_bc, conv_bc_bias, docs, edge_docs)
    group_span = tensor_count // GROUPS
    my_group = tensor_index // group_span
    every_group = lax.all_gather(bc_conv, "tensor", axis=1, tiled=True)
    arranged = every_group.reshape(span_len, 2 * STATE, GROUPS)
    group_cols = lax.dynamic_slice_in_dim(arranged, my_group, 1, 2).reshape(span_len, 2 * STATE)
    head_dev = w_dt.shape[1]
    head_group = np.zeros(head_dev, dtype=np.int32)
    both = group_cols.astype(jnp.float32)
    bmat = both[:, None, :STATE]
    cmat = both[:, None, STATE:]
    xvals = x_conv.astype(jnp.float32).reshape(span_len, head_dev, HDIM)
    dtv = jax.nn.softplus(dtin.astype(jnp.float32) + dt_bias[None, :])
    block = min(STRETCH, span_len)
    y_local, end_state = ssd_blocks(
        xvals, dtv, decay_rate, bmat, cmat, docs, prev_span_doc, head_group, block
    )
    cum_span = jnp.cumsum(-dtv * decay_rate[None, :], axis=0)
    open_span = (docs == prev_span_doc).astype(jnp.float32)
    span_decay = jnp.exp(cum_span[-1]) * open_span[-1]

    def combine(earlier, later):
        return (earlier[0] * later[0], later[0][:, None, None] * earlier[1] + later[1])

    entering = carried_in(
        (span_decay, end_state),
        "seq",
        combine,
        (jnp.ones_like(span_decay), jnp.zeros_like(end_state)),
    )[1]
    carried = jnp.exp(cum_span) * open_span[:, None]
    y_enter = (
        jnp.einsum("ihn,hpn->ihp", cmat[:, head_group, :], entering, precision=HIGH)
        * carried[:, :, None]
    )
    yvals = (y_local + y_enter + d_skip[None, :, None] * xvals).reshape(span_len, head_dev * HDIM)
    gated = yvals * jax.nn.silu(gate.astype(jnp.float32))
    local_sq = jnp.sum(gated * gated, axis=1)
    group_mark = (jnp.arange(GROUPS) == my_group).astype(jnp.float32)
    every_sum = lax.psum(local_sq[:, None] * group_mark[None, :], "tensor")
    group_mean = jnp.sum(every_sum * group_mark[None, :], axis=1) / (INNER // GROUPS)
    normed = (gated * lax.rsqrt(group_mean + 1e-05)[:, None] * norm_gain[None, :]).astype(
        jnp.bfloat16
    )
    w_full = lax.all_gather(w_out, "seq", axis=1, tiled=True)
    return lax.psum_scatter(
        jnp.dot(normed, w_full, preferred_element_type=jnp.float32).astype(jnp.bfloat16),
        "tensor",
        scatter_dimension=0,
        tiled=True,
    )


def enter(peers):
    barrier = pltpu.get_barrier_semaphore()
    for peer in peers:
        pl.semaphore_signal(barrier, inc=1, device_id=peer, device_id_type=pl.DeviceIdType.MESH)
    pl.semaphore_wait(barrier, len(peers))


def remote(src, dst, send, recv, peer):
    return pltpu.make_async_remote_copy(
        src_ref=src,
        dst_ref=dst,
        send_sem=send,
        recv_sem=recv,
        device_id=peer,
        device_id_type=pl.DeviceIdType.MESH,
    )


SEQS, CHIPS, OWN, SPAN, WIDE, HALF = 4, 4, 32, 256, 256, 128
LOG2E = 1.4426950408889634


def silu(v):
    return v / (1.0 + jnp.exp(-v))


class Sums:
    def __init__(self, bufs, sems, s, z, c):
        self.sa, self.sb, self.ra, self.rb, self.qa, self.qb, self.pa, self.pb, self.k0, self.k1, self.k2 = bufs
        self.sems = sems
        self.x, self.y = (s ^ 1, 2 * z + c), (s ^ 2, 2 * z + c)

    def copies(self, u):
        send, recv = self.sems
        return (
            remote(self.sa.at[u], self.ra.at[u], send.at[u, 0], recv.at[u, 0], self.x),
            remote(self.sb.at[u], self.rb.at[u], send.at[u, 1], recv.at[u, 1], self.y),
            remote(self.qa.at[u], self.pa.at[u], send.at[u, 2], recv.at[u, 2], self.y),
            remote(self.qb.at[u], self.pb.at[u], send.at[u, 3], recv.at[u, 3], self.x),
        )

    def emit(self, u, get):
        first, second, _, _ = self.copies(u)
        far = get(3)
        self.sa[u, 1] = far[:, :HALF].astype(jnp.bfloat16)
        self.sb[u, 1] = far[:, HALF:].astype(jnp.bfloat16)
        near = get(1)
        self.sa[u, 0] = near[:, :HALF].astype(jnp.bfloat16)
        first.start()
        self.k1[u] = near[:, HALF:]
        near = get(2)
        self.sb[u, 0] = near[:, HALF:].astype(jnp.bfloat16)
        second.start()
        self.k2[u] = near[:, :HALF]
        self.k0[u] = get(0)

    def relay(self, u):
        first, second, third, fourth = self.copies(u)
        first.wait_recv()
        self.qa[u] = (self.k2[u] + self.ra[u, 1].astype(jnp.float32)).astype(jnp.bfloat16)
        third.start()
        second.wait_recv()
        self.qb[u] = (self.k1[u] + self.rb[u, 1].astype(jnp.float32)).astype(jnp.bfloat16)
        fourth.start()

    def final(self, u):
        _, _, third, fourth = self.copies(u)
        third.wait_recv()
        fourth.wait_recv()
        own = self.k0[u]
        left = own[:, :HALF] + self.ra[u, 0].astype(jnp.float32) + self.pa[u].astype(jnp.float32)
        right = own[:, HALF:] + self.rb[u, 0].astype(jnp.float32) + self.pb[u].astype(jnp.float32)
        return jnp.concatenate([left, right], axis=1).astype(jnp.bfloat16)

    def drain(self, u):
        for copy in self.copies(u):
            copy.wait_send()


def mix_kernel(
    tok_hbm, wg_hbm, wx_hbm, wb_hbm, wdt_hbm, cx_hbm, cxb_hbm, cb_hbm, cbb_hbm, gain_hbm, wo_hbm,
    bias_hbm, rate_hbm, skip_hbm, len_hbm, out_ref,
    wg, wx, wb, wdt, cx, cxb, cb, cbb, gain, wo, bias_s, rate_s, skip_s, len_s,
    tok, rel, xs, xc, bs, halo, bct, bca, bcp, dts, dtg, dtv,
    held, normed, part, sib, pair, got, done, res,
    *rest,
):
    big, rest = rest[:11], rest[11:]
    few, rest = rest[:11], rest[11:]
    rim, rest = rest[:11], rest[11:]
    (
        w_sem, t_send, t_recv, zu_send, zd_send, z_recv, f_send, f_recv,
        g_send, g_recv, b_send, b_recv, h_send, h_recv, d_send, d_recv,
        e_send, e_recv, a_send, a_recv,
        y_send, y_recv, p_send, p_recv, r_send, r_recv, o_send, o_recv,
    ) = rest
    s, t = lax.axis_index("seq"), lax.axis_index("tensor")
    tens = 2 * CHIPS
    z, c = t // 2, t % 2
    sibling = (s, 2 * z + 1 - c)
    depth = wx.shape[0]
    own_cols = pl.ds(pl.multiple_of(s * depth, depth), depth)
    loads = [
        pltpu.make_async_copy(src, dst, w_sem.at[i])
        for i, (src, dst) in enumerate((
            (len_hbm, len_s), (tok_hbm.at[:, own_cols], tok.at[z, c, s]), (wb_hbm, wb), (wx_hbm, wx),
            (wdt_hbm, wdt), (wg_hbm, wg), (cb_hbm, cb), (cbb_hbm, cbb), (cx_hbm, cx), (cxb_hbm, cxb),
            (bias_hbm, bias_s), (rate_hbm, rate_s), (skip_hbm, skip_s), (gain_hbm, gain), (wo_hbm, wo),
        ))
    ]
    for load in loads:
        load.start()
    along = [(s ^ r, t) for r in range(1, SEQS)]
    across = [(s, lax.rem(t + d, tens)) for d in range(1, tens)]
    enter(along + across)

    spread = [
        remote(
            tok_hbm.at[:, pl.ds(pl.multiple_of(peer[0] * depth, depth), depth)],
            tok.at[z, c, s], t_send.at[i], t_recv.at[i], peer,
        )
        for i, peer in enumerate(along)
    ]
    for copy in spread:
        copy.start()
    loads[0].wait()

    total = SEQS * SPAN
    pos = lax.broadcasted_iota(jnp.int32, (total, HALF), 0)
    begin, start = jnp.zeros((total, HALF), jnp.int32), jnp.int32(0)
    for r in range(len_s.shape[0]):
        begin = jnp.where(pos >= start, start, begin)
        start = start + len_s[r]
    rel[...] = pos - begin

    first = z - 1 + 2 * ((3 - z) // 3)
    last = 3 * (1 - z // 2)
    order = [z, first, 6 - z - first - last, last]

    inner_chip = (z > 0) & (z < CHIPS - 1)

    def hops(zb, r):
        part = tok.at[zb, c, s ^ r]
        up = remote(part, part, zu_send.at[zb, r], z_recv.at[zb, r], (s, 2 * lax.rem(z + 1, CHIPS) + c))
        down = remote(
            part, part, zd_send.at[zb, r], z_recv.at[zb, r], (s, 2 * lax.rem(z + CHIPS - 1, CHIPS) + c)
        )
        over = remote(part, part, f_send.at[zb, r], f_recv.at[zb, r], sibling)
        return up, down, over, (z < CHIPS - 1) & (zb <= z), (z > 0) & (zb >= z)

    def arrive(i, pieces=range(1, SEQS)):
        for r in pieces:
            up, down, over, goes_up, goes_down = hops(order[i], r)
            if i:
                up.wait_recv()
            elif r:
                spread[r - 1].wait_recv()
            else:
                loads[1].wait()
            pl.when(goes_up)(up.start)
            pl.when(goes_down)(down.start)
            over.start()

    def arrive_if(which, i, pieces=range(SEQS)):
        if i < CHIPS:
            pl.when(which)(lambda: arrive(i, pieces))

    sums = Sums(big, (g_send, g_recv), s, z, c)
    sumb = Sums(few, (b_send, b_recv), s, z, c)
    sumh = Sums(rim, (h_send, h_recv), s, z, c)

    def product(rows, w):
        def get(r):
            cols = pl.ds(pl.multiple_of((s ^ r) * WIDE, WIDE), WIDE)
            return jnp.dot(rows, w[:, cols], preferred_element_type=jnp.float32)

        return get

    arrive(0, [0])
    arrive(1, [0])
    arrive_if(inner_chip, 2, [0])
    arrive(0)
    for i in range(CHIPS):
        if i:
            if i == 1:
                arrive(i)
            else:
                arrive_if(~inner_chip, i)
            arrive_if(inner_chip, i + 1, range(1 if i == 1 else 0, SEQS))
        for r in range(SEQS):
            hops(order[i], r)[2].wait_recv()
        rows = tok[order[i]].reshape(SPAN, depth)
        if i == 0:
            loads[2].wait()
        bcp[...] = jnp.dot(rows, wb[...], preferred_element_type=jnp.float32).reshape(2, SEQS, OWN, WIDE)
        sumb.emit(i, lambda r: bcp[:, s ^ r].reshape(2 * OWN, WIDE))

        @pl.when(order[i] == CHIPS - 1)
        def _():
            halo[...] = bcp[1, :, OWN - 16 :, :]

        if i == CHIPS - 1:
            sumh.emit(0, lambda r: halo[lax.rem((s ^ r) + SEQS - 1, SEQS)])
        if i == 0:
            loads[3].wait()
        sums.emit(i, product(rows, wx))
        if i:
            sumb.relay(i - 1)
            sums.relay(i - 1)
    sumb.relay(CHIPS - 1)
    sumh.relay(0)

    def span_rows(q):
        return tok[:, :, q].reshape(SPAN, depth)

    loads[5].wait()
    sums.emit(4, product(span_rows(0), wg))
    bs[:16, :] = sumh.final(0).astype(jnp.float32)
    for i in range(CHIPS):
        bs[pl.ds(pl.multiple_of(16 + order[i] * 2 * OWN, 16), 2 * OWN), :] = sumb.final(i).astype(jnp.float32)

    for load in loads[4:5] + loads[6:]:
        load.wait()
    away = rel[pl.ds(pl.multiple_of(s * SPAN, SPAN), SPAN), :1]

    def conv(src, begin, w, bias, away):
        out = w[CONV - 1 :, :] * src[begin : begin + SPAN, :] + bias
        for back in range(1, CONV):
            tap = w[CONV - 1 - back : CONV - back, :] * src[begin - back : begin - back + SPAN, :]
            out = out + jnp.where(away >= back, tap, 0.0)
        return silu(out).astype(jnp.bfloat16)

    bcc = conv(bs, 16, cb[...], cbb[...], away)
    to = lax.broadcasted_iota(jnp.int32, (WIDE, WIDE), 0)
    frm = lax.broadcasted_iota(jnp.int32, (WIDE, WIDE), 1)
    pick = (frm == (to % 32) * GROUPS + to // 32).astype(jnp.float32).astype(jnp.bfloat16)
    bct[...] = (
        lax.dot_general(pick, bcc, (((1,), (1,)), ((), ())), preferred_element_type=jnp.float32)
        .astype(jnp.bfloat16)
        .reshape(GROUPS, 32, SPAN)
    )
    swaps = [
        remote(bct.at[peer[1]], bca.at[s, t], e_send.at[i], e_recv.at[i], peer)
        for i, peer in enumerate(across)
    ]
    for copy in swaps:
        copy.start()
    bca[s, t] = bct[t]
    sums.relay(CHIPS - 1)
    for q in range(SEQS):
        dts[:, q * SPAN : (q + 1) * SPAN] = lax.dot_general(
            wdt[...], span_rows(q), (((1,), (1,)), ((), ())), preferred_element_type=jnp.float32
        ).astype(jnp.bfloat16)
    steps = [
        remote(dts, dtg.at[i], d_send.at[i], d_recv.at[i], peer) for i, peer in enumerate(along)
    ]
    for copy in steps:
        copy.start()
    sums.emit(5, product(span_rows(1), wg))
    for copy in swaps:
        copy.wait_recv()
    groups = [
        remote(bca.at[s], bca.at[s], a_send.at[i], a_recv.at[i], peer)
        for i, peer in enumerate(along)
    ]
    for copy in groups:
        copy.start()
    sums.relay(4)
    for i in range(CHIPS):
        full = sums.final(i).astype(jnp.float32).reshape(2, SEQS, OWN, WIDE)
        for half in range(2):
            for q in range(SEQS):
                at = 16 + q * SPAN + half * OWN + order[i] * 2 * OWN
                xs[pl.ds(pl.multiple_of(at, 16), OWN), :] = full[half, q]
    sums.emit(6, product(span_rows(2), wg))
    xs[:16, :] = jnp.zeros((16, WIDE), jnp.float32)
    mine = pl.ds(pl.multiple_of(s * WIDE, WIDE), WIDE)
    for q in range(SEQS):
        xc[q * SPAN : (q + 1) * SPAN, :] = conv(
            xs, 16 + q * SPAN, cx[:, mine], cxb[:, mine], rel[q * SPAN : (q + 1) * SPAN, :1]
        ).astype(jnp.float32)
    sums.relay(5)
    sums.emit(7, product(span_rows(3), wg))
    for copy in steps:
        copy.wait_recv()
    dtv[...] = (
        dts[...].astype(jnp.float32)
        + dtg[0].astype(jnp.float32)
        + dtg[1].astype(jnp.float32)
        + dtg[2].astype(jnp.float32)
    ).astype(jnp.bfloat16).astype(jnp.float32)
    heads = 4
    line = lax.broadcasted_iota(jnp.int32, (8, total), 0)
    dt8, rate8 = jnp.zeros((8, total), jnp.float32), jnp.zeros((8, total), jnp.float32)
    for h in range(heads):
        row = dtv[pl.ds(heads * s + h, 1), :] + bias_s[heads * s + h]
        row = jnp.maximum(row, 0.0) + jnp.log1p(jnp.exp(-jnp.abs(row)))
        dt8 = jnp.where(line == h, row, dt8)
        dt8 = jnp.where(line == heads + h, row * (-LOG2E * rate_s[heads * s + h]), dt8)

    dif = to - frm
    upto = (dif <= 0).astype(jnp.float32)
    lane = frm // HDIM
    skip = jnp.zeros((1, WIDE), jnp.float32)
    for h in range(heads):
        skip = jnp.where(lane[:1] == h, skip_s[heads * s + h], skip)
    for copy in groups:
        copy.wait_recv()

    cols_out = wo.shape[1]
    few_rows = OWN // 2
    gathers = [
        [
            remote(held.at[s, k], held.at[s, k], y_send.at[k, i], y_recv.at[k, i], peer)
            for i, peer in enumerate(along)
        ]
        for k in range(2 * SEQS)
    ]
    pairs = [
        remote(part.at[k, 1 - c], sib.at[k], p_send.at[k], p_recv.at[k], sibling)
        for k in range(2 * SEQS)
    ]

    def reduces(k):
        peers = [lax.rem(z + d, CHIPS) for d in range(1, CHIPS)]
        return [
            remote(pair.at[k, to], got.at[k, i], r_send.at[k, i], r_recv.at[k, i], (s, 2 * to + c))
            for i, to in enumerate(peers)
        ]

    def deliver(k, frm):
        return remote(done.at[k], res.at[frm, k % 2], o_send.at[k], o_recv.at[frm, k % 2], (k // 2, t))

    def project(k):
        for copy in gathers[k]:
            copy.wait_recv()
        squares = jnp.zeros((SPAN // 2, WIDE), jnp.float32)
        for n in range(SEQS):
            piece = held[n, k].astype(jnp.float32)
            squares = squares + piece * piece
        scale = lax.rsqrt(jnp.sum(squares, axis=1, keepdims=True) / (SEQS * WIDE) + 1e-05)
        for n in range(SEQS):
            wide = slice(n * WIDE, (n + 1) * WIDE)
            normed[:, wide] = (held[n, k].astype(jnp.float32) * scale * gain[:, wide]).astype(jnp.bfloat16)
        for n in range(cols_out // WIDE):
            wide = slice(n * WIDE, (n + 1) * WIDE)
            acc = jnp.dot(normed[...], wo[:, wide], preferred_element_type=jnp.float32)
            acc = acc.reshape(CHIPS, 2, few_rows, WIDE).astype(jnp.bfloat16)
            for half in range(2):
                part[k, half, :, :, wide] = acc[:, half]
        pairs[k].start()

    def combine(k):
        pairs[k].wait_recv()
        pair[k] = (part[k, c].astype(jnp.float32) + sib[k].astype(jnp.float32)).astype(jnp.bfloat16)
        for copy in reduces(k):
            copy.start()

    def collect(k):
        for copy in reduces(k):
            copy.wait_recv()
        total = pair[k, z].astype(jnp.float32)
        for i in range(CHIPS - 1):
            total = total + got[k, i].astype(jnp.float32)
        done[k] = total.astype(jnp.bfloat16)
        pl.when(s != k // 2)(deliver(k, s).start)

        @pl.when(s == k // 2)
        def _():
            res[k // 2, k % 2] = done[k]

    def advance(k):
        project(k)
        if k > 0:
            combine(k - 1)
        if k > 1:
            collect(k - 2)

    state = jnp.zeros((STATE, WIDE), jnp.float32)
    local = to[:, :1]
    for q in range(SEQS):
        here = slice(q * SPAN, (q + 1) * SPAN)
        away = rel[here, :1]
        bt = bca[q, :4].reshape(STATE, SPAN)
        cn = bca[q, 4:].reshape(STATE, SPAN).astype(jnp.float32).T.astype(jnp.bfloat16)
        scores = jnp.dot(cn, bt, preferred_element_type=jnp.float32)
        scores = jnp.where((dif >= 0) & (dif <= away), scores, 0.0)
        both = dt8[:, here]
        cum = jnp.dot(both, upto, precision=HIGH, preferred_element_type=jnp.float32)
        both = jnp.where(line[:, :SPAN] < heads, both, cum)
        cols = jnp.concatenate([both, jnp.zeros((HALF - 8, SPAN), jnp.float32)], axis=0).T

        def expand(first):
            out = jnp.broadcast_to(cols[:, first : first + 1], (SPAN, WIDE))
            for h in range(1, heads):
                out = jnp.where(lane == h, cols[:, first + h : first + h + 1], out)
            return out

        dte, cume = expand(0), expand(heads)
        xv = xc[here, :]
        xdt = xv * dte
        inner = jnp.zeros((SPAN, WIDE), jnp.float32)
        for h in range(heads):
            gap = cols[:, heads + h : heads + h + 1] - both[heads + h : heads + h + 1, :]
            mixing = (jnp.exp2(jnp.minimum(gap, 0.0)) * scores).astype(jnp.bfloat16)
            inner = inner + jnp.dot(
                mixing, jnp.where(lane == h, xdt, 0.0).astype(jnp.bfloat16),
                preferred_element_type=jnp.float32,
            )
        carry = jnp.where(away > local, jnp.exp2(cume), 0.0)
        ends = cume[SPAN - 1 :, :]
        tail = jnp.where(local >= SPAN - 1 - away[SPAN - 1 :, :], jnp.exp2(ends - cume), 0.0)
        fresh = jnp.dot(bt, (tail * xdt).astype(jnp.bfloat16), preferred_element_type=jnp.float32)
        outer = jnp.dot(cn, state.astype(jnp.bfloat16), preferred_element_type=jnp.float32)
        state = carry[SPAN - 1 :, :] * state + fresh
        y = inner + outer * carry + skip * xv
        if q == 0:
            sums.relay(6)
        if q == 1:
            sums.relay(7)
        gate = sums.final(4 + q).astype(jnp.float32)
        gated = (y * silu(gate)).reshape(2 * CHIPS, 2, few_rows, WIDE)
        for half in range(2):
            held[s, 2 * q + half] = gated[:, half].reshape(SPAN // 2, WIDE).astype(jnp.bfloat16)
            for copy in gathers[2 * q + half]:
                copy.start()
        if q:
            advance(2 * q - 2)
            advance(2 * q - 1)
    last_k = 2 * SEQS - 1
    advance(last_k - 1)
    advance(last_k)
    combine(last_k)
    collect(last_k - 1)
    collect(last_k)
    for q in range(SEQS):
        for half in range(2):
            pl.when(s != q)(deliver(half, q).wait_recv)
            out_ref[half * few_rows : (half + 1) * few_rows, q * cols_out : (q + 1) * cols_out] = res[q, half]

    for zb in range(CHIPS):
        for r in range(SEQS):
            up, down, over, goes_up, goes_down = hops(zb, r)
            pl.when(goes_up)(up.wait_send)
            pl.when(goes_down)(down.wait_send)
            over.wait_send()
    for copy in spread + steps + swaps + groups:
        copy.wait_send()
    for k in range(2 * SEQS):
        for copy in gathers[k] + [pairs[k]] + reduces(k):
            copy.wait_send()
        pl.when(s != k // 2)(deliver(k, s).wait_send)
    for u in range(8):
        sums.drain(u)
    for u in range(4):
        sumb.drain(u)
    sumh.drain(0)


def mix(operands, own, seqs):
    tokens, w_gate, w_xin, w_bc, w_dt, conv_x, conv_xb, conv_b, conv_bb, gain, w_out = operands[:11]
    depth = w_xin.shape[0]
    total = SEQS * SPAN
    cols = w_out.shape[1]
    dma = pltpu.SemaphoreType.DMA
    bf, f32 = jnp.bfloat16, jnp.float32

    def sums(n, rows):
        pair = pltpu.VMEM((n, 2, rows, HALF), bf)
        one = pltpu.VMEM((n, rows, HALF), bf)
        return [pair] * 4 + [one] * 4 + [pltpu.VMEM((n, rows, WIDE), f32)] + [pltpu.VMEM((n, rows, HALF), f32)] * 2

    return pl.pallas_call(
        mix_kernel,
        out_shape=jax.ShapeDtypeStruct((own, cols * seqs), bf),
        in_specs=[pl.BlockSpec(memory_space=pl.ANY)] * len(operands),
        out_specs=pl.BlockSpec(memory_space=pltpu.VMEM),
        scratch_shapes=[pltpu.VMEM(a.shape, a.dtype) for a in operands[1:11]]
        + [pltpu.SMEM(a.shape, a.dtype) for a in operands[11:]]
        + [
            pltpu.VMEM((CHIPS, 2, SEQS, OWN, depth), bf),
            pltpu.VMEM((total, HALF), jnp.int32),
            pltpu.VMEM((16 + total, WIDE), f32),
            pltpu.VMEM((total, WIDE), f32),
            pltpu.VMEM((16 + SPAN, WIDE), f32),
            pltpu.VMEM((SEQS, 16, WIDE), f32),
            pltpu.VMEM((GROUPS, 32, SPAN), bf),
            pltpu.VMEM((SEQS, GROUPS, 32, SPAN), bf),
            pltpu.VMEM((2, SEQS, OWN, WIDE), f32),
            pltpu.VMEM((16, total), bf),
            pltpu.VMEM((3, 16, total), bf),
            pltpu.VMEM((16, total), f32),
            pltpu.VMEM((SEQS, 2 * SEQS, SPAN // 2, WIDE), bf),
            pltpu.VMEM((SPAN // 2, SEQS * WIDE), bf),
            pltpu.VMEM((2 * SEQS, 2, CHIPS, OWN // 2, cols), bf),
            pltpu.VMEM((2 * SEQS, CHIPS, OWN // 2, cols), bf),
            pltpu.VMEM((2 * SEQS, CHIPS, OWN // 2, cols), bf),
            pltpu.VMEM((2 * SEQS, CHIPS - 1, OWN // 2, cols), bf),
            pltpu.VMEM((2 * SEQS, OWN // 2, cols), bf),
            pltpu.VMEM((SEQS, 2, OWN // 2, cols), bf),
        ]
        + sums(8, SPAN)
        + sums(4, 2 * OWN)
        + sums(1, 16)
        + [
            dma((15,)), dma((3,)), dma((3,)), dma((4, 4)), dma((4, 4)), dma((4, 4)), dma((4, 4)), dma((4, 4)),
            dma((8, 4)), dma((8, 4)), dma((4, 4)), dma((4, 4)),
            dma((1, 4)), dma((1, 4)), dma((3,)), dma((3,)), dma((7,)), dma((7,)), dma((3,)), dma((3,)),
            dma((8, 3)), dma((8, 3)), dma((8,)), dma((8,)), dma((8, 3)), dma((8, 3)), dma((8,)), dma((4, 2)),
        ],
        compiler_params=pltpu.CompilerParams(
            collective_id=2, has_side_effects=True, vmem_limit_bytes=56 * 2**20
        ),
    )(*operands)


def shards(
    tokens,
    w_gate,
    w_xin,
    w_bc,
    w_dt,
    conv_x,
    conv_x_bias,
    conv_bc,
    conv_bc_bias,
    dt_bias,
    decay_rate,
    d_skip,
    norm_gain,
    w_out,
    lengths,
):
    operands = (
        tokens, w_gate, w_xin, w_bc, w_dt.T, conv_x, conv_x_bias[None, :], conv_bc, conv_bc_bias[None, :],
        norm_gain[None, :], w_out, dt_bias, decay_rate, d_skip, lengths,
    )
    return mix(operands, tokens.shape[0], lax.axis_size("seq"))


def solution(mesh):
    seqs, tens = mesh.shape["seq"], mesh.shape["tensor"]
    narrow = seqs == SEQS and tens == GROUPS == 2 * CHIPS
    body = shards if narrow else shards_wide
    in_specs = (
        P(("seq", "tensor"), None),
        P("seq", "tensor"),
        P("seq", "tensor"),
        P("seq", "tensor"),
        P("seq", "tensor"),
        P(None, "tensor"),
        P("tensor"),
        P(None, "tensor"),
        P("tensor"),
        P("tensor"),
        P("tensor"),
        P("tensor"),
        P("tensor"),
        P("tensor", "seq"),
        P(),
    )
    out_specs = P(("seq", "tensor"), None)
    return jax.shard_map(body, mesh=mesh, in_specs=in_specs, out_specs=out_specs, check_vma=False)
```

```python
import jax
import jax.numpy as jnp
import numpy as np
from jax import lax
from jax.experimental import pallas as pl
from jax.experimental.pallas import tpu as pltpu
from jax.sharding import PartitionSpec as P

HDIM = 64
GROUPS = 8
STATE = 128
CONV = 4
STRETCH = 256
INNER = 8192


HIGH = lax.Precision.HIGHEST


def from_behind(x, axis, by):
    count = lax.axis_size(axis)
    pairs = [(i, i + by) for i in range(count) if 0 <= i + by < count]
    return lax.ppermute(x, axis, pairs)


def carried_in(x, axis, combine, identity):
    count, here = (lax.axis_size(axis), lax.axis_index(axis))
    everything = jax.tree.map(
        lambda part, kind: lax.all_gather(part.astype(kind), axis), x, (jnp.bfloat16, jnp.bfloat16)
    )
    start = jax.tree.map(
        lambda part, zero: jnp.broadcast_to(jnp.asarray(zero, part.dtype), part.shape), x, identity
    )

    def hop(k, before):
        reached = k < here
        new = combine(
            before, jax.tree.map(lambda part, own: part[k].astype(own.dtype), everything, x)
        )
        return jax.tree.map(lambda a, b: jnp.where(reached, a, b), new, before)

    return lax.fori_loop(0, count, hop, start)


def doc_ids(lengths, positions):
    starts = jnp.cumsum(lengths) - lengths
    counted = jnp.sum((starts[None, :] <= positions[:, None]).astype(jnp.int32), axis=1)
    return counted - 1


def causal_conv(values, edge, weights, bias, docs, edge_docs):
    count = values.shape[0]
    extended = jnp.concatenate([edge, values], axis=0).astype(jnp.float32)
    all_docs = jnp.concatenate([edge_docs, docs])
    summed = jnp.zeros(values.shape, jnp.float32) + bias[None, :]
    for offset in range(weights.shape[0]):
        same = (all_docs[offset : offset + count] == docs).astype(jnp.float32)
        summed = (
            summed + weights[offset][None, :] * extended[offset : offset + count] * same[:, None]
        )
    return lax.optimization_barrier(jax.nn.silu(summed).astype(jnp.bfloat16))


def ssd_blocks(xvals, dtv, rate, bmat, cmat, docs, prev_doc, head_group, block):
    count, heads, hdim = xvals.shape
    nstate = bmat.shape[2]
    blocks = count // block
    logs = -dtv * rate[None, :]

    def split(array):
        return array.reshape((blocks, block) + array.shape[1:])

    lower = jnp.tril(jnp.ones((block, block), bool))

    def step(carry, pieces):
        state, last_doc = carry
        xblk, dblk, lblk, bblk, cblk, docblk = pieces
        cum = jnp.cumsum(lblk, axis=0)
        same = (docblk[:, None] == docblk[None, :]) & lower
        diff = cum.T[:, :, None] - cum.T[:, None, :]
        decay = jnp.exp(jnp.where(same[None], diff, -jnp.inf))
        scores = jnp.einsum("ign,jgn->gij", cblk, bblk, precision=HIGH)
        mixing = scores[head_group] * decay * dblk.T[:, None, :]
        inner = jnp.einsum("hij,jhp->ihp", mixing, xblk, precision=HIGH)
        open_in = (docblk == last_doc).astype(jnp.float32)
        carry_in = jnp.exp(cum) * open_in[:, None]
        chead = cblk[:, head_group, :]
        outer = jnp.einsum("ihn,hpn->ihp", chead, state, precision=HIGH) * carry_in[:, :, None]
        end_doc = docblk[-1]
        tail = (
            jnp.exp(cum[-1][None, :] - cum)
            * (docblk == end_doc).astype(jnp.float32)[:, None]
            * dblk
        )
        bhead = bblk[:, head_group, :]
        fresh = jnp.einsum("jh,jhp,jhn->hpn", tail, xblk, bhead, precision=HIGH)
        state = carry_in[-1][:, None, None] * state + fresh
        return ((state, end_doc), inner + outer)

    init = (jnp.zeros((heads, hdim, nstate), jnp.float32), prev_doc)
    (state, end_doc), outs = lax.scan(
        step, init, (split(xvals), split(dtv), split(logs), split(bmat), split(cmat), split(docs))
    )
    return (outs.reshape(count, heads, hdim), state)


def shards_wide(
    tokens,
    w_gate,
    w_xin,
    w_bc,
    w_dt,
    conv_x,
    conv_x_bias,
    conv_bc,
    conv_bc_bias,
    dt_bias,
    decay_rate,
    d_skip,
    norm_gain,
    w_out,
    lengths,
):
    tensor_count = lax.axis_size("tensor")
    seq_index = lax.axis_index("seq")
    tensor_index = lax.axis_index("tensor")
    span_rows = lax.all_gather(tokens, "tensor", axis=0, tiled=True)
    span_len = span_rows.shape[0]
    pieces = (
        lax.all_gather(w_gate, "seq", axis=0, tiled=True),
        lax.all_gather(w_xin, "seq", axis=0, tiled=True),
        lax.all_gather(w_bc, "seq", axis=0, tiled=True),
        lax.all_gather(w_dt, "seq", axis=0, tiled=True),
    )
    gate_acc, xin_acc, bc_acc, dt_acc = tuple(
        (
            jnp.dot(span_rows, weight_piece, preferred_element_type=jnp.float32)
            for weight_piece in pieces
        )
    )
    gate = gate_acc.astype(jnp.bfloat16)
    xin = xin_acc.astype(jnp.bfloat16)
    bcin = bc_acc.astype(jnp.bfloat16)
    dtin = dt_acc.astype(jnp.bfloat16)
    gate, xin, bcin, dtin = lax.optimization_barrier((gate, xin, bcin, dtin))
    positions = seq_index * span_len + jnp.arange(span_len, dtype=jnp.int32)
    docs = doc_ids(lengths, positions)
    edge_docs = doc_ids(lengths, seq_index * span_len + jnp.arange(-(CONV - 1), 0, dtype=jnp.int32))
    prev_span_doc = doc_ids(lengths, positions[:1] - 1)[0]
    edge_x, edge_bc = from_behind(
        (xin[span_len - (CONV - 1) :], bcin[span_len - (CONV - 1) :]), "seq", 1
    )
    x_conv = causal_conv(xin, edge_x, conv_x, conv_x_bias, docs, edge_docs)
    bc_conv = causal_conv(bcin, edge_bc, conv_bc, conv_bc_bias, docs, edge_docs)
    group_span = tensor_count // GROUPS
    my_group = tensor_index // group_span
    every_group = lax.all_gather(bc_conv, "tensor", axis=1, tiled=True)
    arranged = every_group.reshape(span_len, 2 * STATE, GROUPS)
    group_cols = lax.dynamic_slice_in_dim(arranged, my_group, 1, 2).reshape(span_len, 2 * STATE)
    head_dev = w_dt.shape[1]
    head_group = np.zeros(head_dev, dtype=np.int32)
    both = group_cols.astype(jnp.float32)
    bmat = both[:, None, :STATE]
    cmat = both[:, None, STATE:]
    xvals = x_conv.astype(jnp.float32).reshape(span_len, head_dev, HDIM)
    dtv = jax.nn.softplus(dtin.astype(jnp.float32) + dt_bias[None, :])
    block = min(STRETCH, span_len)
    y_local, end_state = ssd_blocks(
        xvals, dtv, decay_rate, bmat, cmat, docs, prev_span_doc, head_group, block
    )
    cum_span = jnp.cumsum(-dtv * decay_rate[None, :], axis=0)
    open_span = (docs == prev_span_doc).astype(jnp.float32)
    span_decay = jnp.exp(cum_span[-1]) * open_span[-1]

    def combine(earlier, later):
        return (earlier[0] * later[0], later[0][:, None, None] * earlier[1] + later[1])

    entering = carried_in(
        (span_decay, end_state),
        "seq",
        combine,
        (jnp.ones_like(span_decay), jnp.zeros_like(end_state)),
    )[1]
    carried = jnp.exp(cum_span) * open_span[:, None]
    y_enter = (
        jnp.einsum("ihn,hpn->ihp", cmat[:, head_group, :], entering, precision=HIGH)
        * carried[:, :, None]
    )
    yvals = (y_local + y_enter + d_skip[None, :, None] * xvals).reshape(span_len, head_dev * HDIM)
    gated = yvals * jax.nn.silu(gate.astype(jnp.float32))
    local_sq = jnp.sum(gated * gated, axis=1)
    group_mark = (jnp.arange(GROUPS) == my_group).astype(jnp.float32)
    every_sum = lax.psum(local_sq[:, None] * group_mark[None, :], "tensor")
    group_mean = jnp.sum(every_sum * group_mark[None, :], axis=1) / (INNER // GROUPS)
    normed = (gated * lax.rsqrt(group_mean + 1e-05)[:, None] * norm_gain[None, :]).astype(
        jnp.bfloat16
    )
    w_full = lax.all_gather(w_out, "seq", axis=1, tiled=True)
    return lax.psum_scatter(
        jnp.dot(normed, w_full, preferred_element_type=jnp.float32).astype(jnp.bfloat16),
        "tensor",
        scatter_dimension=0,
        tiled=True,
    )


def enter(peers):
    barrier = pltpu.get_barrier_semaphore()
    for peer in peers:
        pl.semaphore_signal(barrier, inc=1, device_id=peer, device_id_type=pl.DeviceIdType.MESH)
    pl.semaphore_wait(barrier, len(peers))


def remote(src, dst, send, recv, peer):
    return pltpu.make_async_remote_copy(
        src_ref=src,
        dst_ref=dst,
        send_sem=send,
        recv_sem=recv,
        device_id=peer,
        device_id_type=pl.DeviceIdType.MESH,
    )


SEQS, CHIPS, OWN, SPAN, WIDE, HALF = 4, 4, 32, 256, 256, 128
LOG2E = 1.4426950408889634


def silu(v):
    return v / (1.0 + jnp.exp(-v))


class Sums:
    def __init__(self, bufs, sems, s, z, c):
        self.sa, self.sb, self.ra, self.rb, self.qa, self.qb, self.pa, self.pb, self.k0, self.k1, self.k2 = bufs
        self.sems = sems
        self.x, self.y = (s ^ 1, 2 * z + c), (s ^ 2, 2 * z + c)

    def copies(self, u):
        send, recv = self.sems
        return (
            remote(self.sa.at[u], self.ra.at[u], send.at[u, 0], recv.at[u, 0], self.x),
            remote(self.sb.at[u], self.rb.at[u], send.at[u, 1], recv.at[u, 1], self.y),
            remote(self.qa.at[u], self.pa.at[u], send.at[u, 2], recv.at[u, 2], self.y),
            remote(self.qb.at[u], self.pb.at[u], send.at[u, 3], recv.at[u, 3], self.x),
        )

    def emit(self, u, get):
        first, second, _, _ = self.copies(u)
        far = get(3)
        self.sa[u, 1] = far[:, :HALF].astype(jnp.bfloat16)
        self.sb[u, 1] = far[:, HALF:].astype(jnp.bfloat16)
        near = get(1)
        self.sa[u, 0] = near[:, :HALF].astype(jnp.bfloat16)
        first.start()
        self.k1[u] = near[:, HALF:]
        near = get(2)
        self.sb[u, 0] = near[:, HALF:].astype(jnp.bfloat16)
        second.start()
        self.k2[u] = near[:, :HALF]
        self.k0[u] = get(0)

    def relay(self, u):
        first, second, third, fourth = self.copies(u)
        first.wait_recv()
        self.qa[u] = (self.k2[u] + self.ra[u, 1].astype(jnp.float32)).astype(jnp.bfloat16)
        third.start()
        second.wait_recv()
        self.qb[u] = (self.k1[u] + self.rb[u, 1].astype(jnp.float32)).astype(jnp.bfloat16)
        fourth.start()

    def final(self, u):
        _, _, third, fourth = self.copies(u)
        third.wait_recv()
        fourth.wait_recv()
        own = self.k0[u]
        left = own[:, :HALF] + self.ra[u, 0].astype(jnp.float32) + self.pa[u].astype(jnp.float32)
        right = own[:, HALF:] + self.rb[u, 0].astype(jnp.float32) + self.pb[u].astype(jnp.float32)
        return jnp.concatenate([left, right], axis=1).astype(jnp.bfloat16)

    def drain(self, u):
        for copy in self.copies(u):
            copy.wait_send()


def mix_kernel(
    tok_hbm, wg_hbm, wx_hbm, wb_hbm, wdt_hbm, cx_hbm, cxb_hbm, cb_hbm, cbb_hbm, gain_hbm, wo_hbm,
    bias_hbm, rate_hbm, skip_hbm, len_hbm, out_ref,
    wg, wx, wb, wdt, cx, cxb, cb, cbb, gain, wo, bias_s, rate_s, skip_s, len_s,
    tok, rel, xs, xc, gs, bs, halo, bct, bca, bcp, dtp, dts, dtg, dtv,
    held, normed, part, sib, pair, got, done, res,
    *rest,
):
    big, rest = rest[:11], rest[11:]
    few, rest = rest[:11], rest[11:]
    rim, rest = rest[:11], rest[11:]
    three, rest = rest[:11], rest[11:]
    (
        w_sem, t_send, t_recv, zu_send, zd_send, z_recv, f_send, f_recv,
        g_send, g_recv, v_send, v_recv, b_send, b_recv, h_send, h_recv, d_send, d_recv,
        e_send, e_recv, a_send, a_recv,
        y_send, y_recv, p_send, p_recv, r_send, r_recv, o_send, o_recv,
    ) = rest
    s, t = lax.axis_index("seq"), lax.axis_index("tensor")
    tens = 2 * CHIPS
    z, c = t // 2, t % 2
    sibling = (s, 2 * z + 1 - c)
    depth = wx.shape[0]
    own_cols = pl.ds(pl.multiple_of(s * depth, depth), depth)
    loads = [
        pltpu.make_async_copy(src, dst, w_sem.at[i])
        for i, (src, dst) in enumerate((
            (len_hbm, len_s), (tok_hbm.at[:, own_cols], tok.at[z, c, s]), (wb_hbm, wb), (wx_hbm, wx),
            (wdt_hbm, wdt), (wg_hbm, wg), (cb_hbm, cb), (cbb_hbm, cbb), (cx_hbm, cx), (cxb_hbm, cxb),
            (bias_hbm, bias_s), (rate_hbm, rate_s), (skip_hbm, skip_s), (gain_hbm, gain), (wo_hbm, wo),
        ))
    ]
    for load in loads:
        load.start()
    along = [(s ^ r, t) for r in range(1, SEQS)]
    across = [(s, lax.rem(t + d, tens)) for d in range(1, tens)]
    enter(along + across)

    spread = [
        remote(
            tok_hbm.at[:, pl.ds(pl.multiple_of(peer[0] * depth, depth), depth)],
            tok.at[z, c, s], t_send.at[i], t_recv.at[i], peer,
        )
        for i, peer in enumerate(along)
    ]
    for copy in spread:
        copy.start()
    loads[0].wait()

    total = SEQS * SPAN
    pos = lax.broadcasted_iota(jnp.int32, (total, HALF), 0)
    begin, start = jnp.zeros((total, HALF), jnp.int32), jnp.int32(0)
    for r in range(len_s.shape[0]):
        begin = jnp.where(pos >= start, start, begin)
        start = start + len_s[r]
    rel[...] = pos - begin

    first = z - 1 + 2 * ((3 - z) // 3)
    last = 3 * (1 - z // 2)
    order = [z, first, 6 - z - first - last, last]

    inner_chip = (z > 0) & (z < CHIPS - 1)

    def hops(zb, r):
        part = tok.at[zb, c, s ^ r]
        up = remote(part, part, zu_send.at[zb, r], z_recv.at[zb, r], (s, 2 * lax.rem(z + 1, CHIPS) + c))
        down = remote(
            part, part, zd_send.at[zb, r], z_recv.at[zb, r], (s, 2 * lax.rem(z + CHIPS - 1, CHIPS) + c)
        )
        over = remote(part, part, f_send.at[zb, r], f_recv.at[zb, r], sibling)
        return up, down, over, (z < CHIPS - 1) & (zb <= z), (z > 0) & (zb >= z)

    def arrive(i, pieces=range(1, SEQS)):
        for r in pieces:
            up, down, over, goes_up, goes_down = hops(order[i], r)
            if i:
                up.wait_recv()
            elif r:
                spread[r - 1].wait_recv()
            else:
                loads[1].wait()
            pl.when(goes_up)(up.start)
            pl.when(goes_down)(down.start)
            over.start()

    def arrive_if(which, i, pieces=range(SEQS)):
        if i < CHIPS:
            pl.when(which)(lambda: arrive(i, pieces))

    sums = Sums(big, (g_send, g_recv), s, z, c)
    sumg = Sums(three, (v_send, v_recv), s, z, c)
    sumb = Sums(few, (b_send, b_recv), s, z, c)
    sumh = Sums(rim, (h_send, h_recv), s, z, c)

    def product(rows, w):
        def get(r):
            cols = pl.ds(pl.multiple_of((s ^ r) * WIDE, WIDE), WIDE)
            return jnp.dot(rows, w[:, cols], preferred_element_type=jnp.float32)

        return get

    arrive(0, [0])
    arrive(1, [0])
    arrive_if(inner_chip, 2, [0])
    arrive(0)
    for i in range(CHIPS):
        if i:
            if i == 1:
                arrive(i)
            else:
                arrive_if(~inner_chip, i)
            arrive_if(inner_chip, i + 1, range(1 if i == 1 else 0, SEQS))
        for r in range(SEQS):
            hops(order[i], r)[2].wait_recv()
        rows = tok[order[i]].reshape(SPAN, depth)
        if i == 0:
            loads[2].wait()
        bcp[...] = jnp.dot(rows, wb[...], preferred_element_type=jnp.float32).reshape(2, SEQS, OWN, WIDE)
        sumb.emit(i, lambda r: bcp[:, s ^ r].reshape(2 * OWN, WIDE))

        @pl.when(order[i] == CHIPS - 1)
        def _():
            halo[...] = bcp[1, :, OWN - 16 :, :]

        if i == CHIPS - 1:
            sumh.emit(0, lambda r: halo[lax.rem((s ^ r) + SEQS - 1, SEQS)])
        if i == 0:
            loads[3].wait()
        sums.emit(i, product(rows, wx))
        if i == 0:
            loads[5].wait()
            sums.emit(CHIPS, product(rows, wg))
        if i:
            sumb.relay(i - 1)
            sums.relay(i - 1)
    sumb.relay(CHIPS - 1)
    sumh.relay(0)

    def span_rows(q):
        return tok[:, :, q].reshape(SPAN, depth)

    sums.relay(CHIPS)
    def other_rows(q):
        rows = [tok[zb, :, q].reshape(2 * OWN, depth) for zb in order[1:]]
        return jnp.concatenate(rows, axis=0)

    sumg.emit(0, product(other_rows(0), wg))
    bs[:16, :] = sumh.final(0).astype(jnp.float32)
    for i in range(CHIPS):
        bs[pl.ds(pl.multiple_of(16 + order[i] * 2 * OWN, 16), 2 * OWN), :] = sumb.final(i).astype(jnp.float32)

    for load in loads[4:5] + loads[6:]:
        load.wait()
    away = rel[pl.ds(pl.multiple_of(s * SPAN, SPAN), SPAN), :1]

    def conv(src, begin, w, bias, away):
        out = w[CONV - 1 :, :] * src[begin : begin + SPAN, :] + bias
        for back in range(1, CONV):
            tap = w[CONV - 1 - back : CONV - back, :] * src[begin - back : begin - back + SPAN, :]
            out = out + jnp.where(away >= back, tap, 0.0)
        return silu(out).astype(jnp.bfloat16)

    bcc = conv(bs, 16, cb[...], cbb[...], away)
    to = lax.broadcasted_iota(jnp.int32, (WIDE, WIDE), 0)
    frm = lax.broadcasted_iota(jnp.int32, (WIDE, WIDE), 1)
    pick = (frm == (to % 32) * GROUPS + to // 32).astype(jnp.float32).astype(jnp.bfloat16)
    bct[...] = (
        lax.dot_general(pick, bcc, (((1,), (1,)), ((), ())), preferred_element_type=jnp.float32)
        .astype(jnp.bfloat16)
        .reshape(GROUPS, 32, SPAN)
    )
    swaps = [
        remote(bct.at[peer[1]], bca.at[s, t], e_send.at[i], e_recv.at[i], peer)
        for i, peer in enumerate(across)
    ]
    for copy in swaps:
        copy.start()
    bca[s, t] = bct[t]
    sums.relay(CHIPS - 1)
    heads = 4
    for q in range(SEQS):
        some = lax.dot_general(
            wdt[...], span_rows(q), (((1,), (1,)), ((), ())), preferred_element_type=jnp.float32
        )
        for d in range(SEQS):
            dtp[d, heads * q : heads * (q + 1), :] = some[heads * d : heads * (d + 1), :]
    dts[...] = dtp[...].astype(jnp.bfloat16)
    steps = [
        remote(dts.at[peer[0]], dtg.at[i], d_send.at[i], d_recv.at[i], peer) for i, peer in enumerate(along)
    ]
    for copy in steps:
        copy.start()
    sumg.emit(1, product(other_rows(1), wg))
    for copy in swaps:
        copy.wait_recv()
    groups = [
        remote(bca.at[s], bca.at[s], a_send.at[i], a_recv.at[i], peer)
        for i, peer in enumerate(along)
    ]
    for copy in groups:
        copy.start()
    sumg.relay(0)
    for i in range(CHIPS):
        full = sums.final(i).astype(jnp.float32).reshape(2, SEQS, OWN, WIDE)
        for half in range(2):
            for q in range(SEQS):
                at = 16 + q * SPAN + half * OWN + order[i] * 2 * OWN
                xs[pl.ds(pl.multiple_of(at, 16), OWN), :] = full[half, q]
    sumg.emit(2, product(other_rows(2), wg))
    full = sums.final(CHIPS).astype(jnp.float32).reshape(2, SEQS, OWN, WIDE)
    for half in range(2):
        for q in range(SEQS):
            gs[q, pl.ds(pl.multiple_of(z * 2 * OWN + half * OWN, 16), OWN), :] = full[half, q]
    xs[:16, :] = jnp.zeros((16, WIDE), jnp.float32)
    mine = pl.ds(pl.multiple_of(s * WIDE, WIDE), WIDE)
    for q in range(SEQS):
        xc[q * SPAN : (q + 1) * SPAN, :] = conv(
            xs, 16 + q * SPAN, cx[:, mine], cxb[:, mine], rel[q * SPAN : (q + 1) * SPAN, :1]
        ).astype(jnp.float32)
    sumg.relay(1)
    sumg.emit(3, product(other_rows(3), wg))
    for copy in steps:
        copy.wait_recv()
    small = dts[s].astype(jnp.float32)
    for i in range(SEQS - 1):
        small = small + dtg[i].astype(jnp.float32)
    line = to[: heads * SEQS, :] % heads
    bias, rate = jnp.zeros(line.shape, jnp.float32), jnp.zeros(line.shape, jnp.float32)
    for h in range(heads):
        bias = jnp.where(line == h, bias_s[heads * s + h], bias)
        rate = jnp.where(line == h, -LOG2E * rate_s[heads * s + h], rate)
    small = small.astype(jnp.bfloat16).astype(jnp.float32) + bias
    small = jnp.maximum(small, 0.0) + jnp.log1p(jnp.exp(-jnp.abs(small)))
    for q in range(SEQS):
        dtv[q, :heads, :] = small[heads * q : heads * (q + 1), :]
        dtv[q, heads:, :] = (small * rate)[heads * q : heads * (q + 1), :]

    dif = to - frm
    upto = (dif <= 0).astype(jnp.float32)
    lane = frm // HDIM
    skip = jnp.zeros((1, WIDE), jnp.float32)
    for h in range(heads):
        skip = jnp.where(lane[:1] == h, skip_s[heads * s + h], skip)
    for copy in groups:
        copy.wait_recv()

    cols_out = wo.shape[1]
    few_rows = OWN // 2
    gathers = [
        [
            remote(held.at[s, k], held.at[s, k], y_send.at[k, i], y_recv.at[k, i], peer)
            for i, peer in enumerate(along)
        ]
        for k in range(2 * SEQS)
    ]
    pairs = [
        remote(part.at[k, 1 - c], sib.at[k], p_send.at[k], p_recv.at[k], sibling)
        for k in range(2 * SEQS)
    ]

    def reduces(k):
        peers = [lax.rem(z + d, CHIPS) for d in range(1, CHIPS)]
        return [
            remote(pair.at[k, to], got.at[k, i], r_send.at[k, i], r_recv.at[k, i], (s, 2 * to + c))
            for i, to in enumerate(peers)
        ]

    def deliver(k, frm):
        return remote(done.at[k], res.at[frm, k % 2], o_send.at[k], o_recv.at[frm, k % 2], (k // 2, t))

    def project(k):
        for copy in gathers[k]:
            copy.wait_recv()
        squares = jnp.zeros((SPAN // 2, HALF), jnp.float32)
        for n in range(2 * SEQS):
            piece = held[n // 2, k, n % 2].astype(jnp.float32)
            squares = squares + piece * piece
        scale = lax.rsqrt(jnp.sum(squares, axis=1, keepdims=True) / (SEQS * WIDE) + 1e-05)
        for n in range(2 * SEQS):
            wide = slice(n * HALF, (n + 1) * HALF)
            piece = held[n // 2, k, n % 2].astype(jnp.float32)
            normed[:, wide] = (piece * scale * gain[:, wide]).astype(jnp.bfloat16)
        for n in range(cols_out // WIDE):
            wide = slice(n * WIDE, (n + 1) * WIDE)
            acc = jnp.dot(normed[...], wo[:, wide], preferred_element_type=jnp.float32)
            acc = acc.reshape(CHIPS, 2, few_rows, WIDE).astype(jnp.bfloat16)
            for half in range(2):
                part[k, half, :, :, wide] = acc[:, half]
        pairs[k].start()

    def combine(k):
        pairs[k].wait_recv()
        pair[k] = (part[k, c].astype(jnp.float32) + sib[k].astype(jnp.float32)).astype(jnp.bfloat16)
        for copy in reduces(k):
            copy.start()

    def collect(k):
        for copy in reduces(k):
            copy.wait_recv()
        total = pair[k, z].astype(jnp.float32)
        for i in range(CHIPS - 1):
            total = total + got[k, i].astype(jnp.float32)
        done[k] = total.astype(jnp.bfloat16)
        pl.when(s != k // 2)(deliver(k, s).start)

        @pl.when(s == k // 2)
        def _():
            res[k // 2, k % 2] = done[k]

    def advance(k):
        project(k)
        if k > 0:
            combine(k - 1)
        if k > 1:
            collect(k - 2)

    state = jnp.zeros((STATE, WIDE), jnp.float32)
    local = to[:, :1]
    for q in range(SEQS):
        here = slice(q * SPAN, (q + 1) * SPAN)
        away = rel[here, :1]
        bt = bca[q, :4].reshape(STATE, SPAN)
        cn = bca[q, 4:].reshape(STATE, SPAN).astype(jnp.float32).T.astype(jnp.bfloat16)
        scores = jnp.dot(cn, bt, preferred_element_type=jnp.float32)
        scores = jnp.where((dif >= 0) & (dif <= away), scores, 0.0)
        both = dtv[q]
        cum = jnp.dot(both, upto, precision=HIGH, preferred_element_type=jnp.float32)
        both = jnp.where(to[:8, :] < heads, both, cum)
        cols = jnp.concatenate([both, jnp.zeros((HALF - 8, SPAN), jnp.float32)], axis=0).T

        def expand(first):
            out = jnp.broadcast_to(cols[:, first : first + 1], (SPAN, WIDE))
            for h in range(1, heads):
                out = jnp.where(lane == h, cols[:, first + h : first + h + 1], out)
            return out

        dte, cume = expand(0), expand(heads)
        xv = xc[here, :]
        xdt = xv * dte
        inner = jnp.zeros((SPAN, WIDE), jnp.float32)
        for h in range(heads):
            gap = cols[:, heads + h : heads + h + 1] - both[heads + h : heads + h + 1, :]
            mixing = (jnp.exp2(jnp.minimum(gap, 0.0)) * scores).astype(jnp.bfloat16)
            inner = inner + jnp.dot(
                mixing, jnp.where(lane == h, xdt, 0.0).astype(jnp.bfloat16),
                preferred_element_type=jnp.float32,
            )
        carry = jnp.where(away > local, jnp.exp2(cume), 0.0)
        ends = cume[SPAN - 1 :, :]
        tail = jnp.where(local >= SPAN - 1 - away[SPAN - 1 :, :], jnp.exp2(ends - cume), 0.0)
        fresh = jnp.dot(bt, (tail * xdt).astype(jnp.bfloat16), preferred_element_type=jnp.float32)
        outer = jnp.dot(cn, state.astype(jnp.bfloat16), preferred_element_type=jnp.float32)
        state = carry[SPAN - 1 :, :] * state + fresh
        y = inner + outer * carry + skip * xv
        if q == 0:
            sumg.relay(2)
        if q == 1:
            sumg.relay(3)
        some = sumg.final(q).astype(jnp.float32)
        for i in range(1, CHIPS):
            to_rows = pl.ds(pl.multiple_of(order[i] * 2 * OWN, 16), 2 * OWN)
            gs[q, to_rows, :] = some[(i - 1) * 2 * OWN : i * 2 * OWN]
        gate = gs[q]
        gated = (y * silu(gate)).reshape(2 * CHIPS, 2, few_rows, WIDE)
        for half in range(2):
            k = 2 * q + half
            some = gated[:, half].reshape(SPAN // 2, WIDE).astype(jnp.bfloat16)
            held[s, k, 0], held[s, k, 1] = some[:, :HALF], some[:, HALF:]
            for copy in gathers[k]:
                copy.start()
        for k in range(2 * q - 4, 2 * q - 2):
            if k >= 0:
                advance(k)
    last_k = 2 * SEQS - 1
    for k in range(last_k - 3, last_k + 1):
        advance(k)
    combine(last_k)
    collect(last_k - 1)
    collect(last_k)
    for q in range(SEQS):
        for half in range(2):
            pl.when(s != q)(deliver(half, q).wait_recv)
            out_ref[half * few_rows : (half + 1) * few_rows, q * cols_out : (q + 1) * cols_out] = res[q, half]

    for zb in range(CHIPS):
        for r in range(SEQS):
            up, down, over, goes_up, goes_down = hops(zb, r)
            pl.when(goes_up)(up.wait_send)
            pl.when(goes_down)(down.wait_send)
            over.wait_send()
    for copy in spread + steps + swaps + groups:
        copy.wait_send()
    for k in range(2 * SEQS):
        for copy in gathers[k] + [pairs[k]] + reduces(k):
            copy.wait_send()
        pl.when(s != k // 2)(deliver(k, s).wait_send)
    for u in range(5):
        sums.drain(u)
    for u in range(4):
        sumg.drain(u)
    for u in range(4):
        sumb.drain(u)
    sumh.drain(0)


def mix(operands, own, seqs):
    tokens, w_gate, w_xin, w_bc, w_dt, conv_x, conv_xb, conv_b, conv_bb, gain, w_out = operands[:11]
    depth = w_xin.shape[0]
    total = SEQS * SPAN
    cols = w_out.shape[1]
    dma = pltpu.SemaphoreType.DMA
    bf, f32 = jnp.bfloat16, jnp.float32

    def sums(n, rows):
        pair = pltpu.VMEM((n, 2, rows, HALF), bf)
        one = pltpu.VMEM((n, rows, HALF), bf)
        return [pair] * 4 + [one] * 4 + [pltpu.VMEM((n, rows, WIDE), f32)] + [pltpu.VMEM((n, rows, HALF), f32)] * 2

    return pl.pallas_call(
        mix_kernel,
        out_shape=jax.ShapeDtypeStruct((own, cols * seqs), bf),
        in_specs=[pl.BlockSpec(memory_space=pl.ANY)] * len(operands),
        out_specs=pl.BlockSpec(memory_space=pltpu.VMEM),
        scratch_shapes=[pltpu.VMEM(a.shape, a.dtype) for a in operands[1:11]]
        + [pltpu.SMEM(a.shape, a.dtype) for a in operands[11:]]
        + [
            pltpu.VMEM((CHIPS, 2, SEQS, OWN, depth), bf),
            pltpu.VMEM((total, HALF), jnp.int32),
            pltpu.VMEM((16 + total, WIDE), f32),
            pltpu.VMEM((total, WIDE), f32),
            pltpu.VMEM((SEQS, SPAN, WIDE), f32),
            pltpu.VMEM((16 + SPAN, WIDE), f32),
            pltpu.VMEM((SEQS, 16, WIDE), f32),
            pltpu.VMEM((GROUPS, 32, SPAN), bf),
            pltpu.VMEM((SEQS, GROUPS, 32, SPAN), bf),
            pltpu.VMEM((2, SEQS, OWN, WIDE), f32),
            pltpu.VMEM((SEQS, 16, SPAN), f32),
            pltpu.VMEM((SEQS, 16, SPAN), bf),
            pltpu.VMEM((3, 16, SPAN), bf),
            pltpu.VMEM((SEQS, 8, SPAN), f32),
            pltpu.VMEM((SEQS, 2 * SEQS, 2, SPAN // 2, HALF), bf),
            pltpu.VMEM((SPAN // 2, SEQS * WIDE), bf),
            pltpu.VMEM((2 * SEQS, 2, CHIPS, OWN // 2, cols), bf),
            pltpu.VMEM((2 * SEQS, CHIPS, OWN // 2, cols), bf),
            pltpu.VMEM((2 * SEQS, CHIPS, OWN // 2, cols), bf),
            pltpu.VMEM((2 * SEQS, CHIPS - 1, OWN // 2, cols), bf),
            pltpu.VMEM((2 * SEQS, OWN // 2, cols), bf),
            pltpu.VMEM((SEQS, 2, OWN // 2, cols), bf),
        ]
        + sums(CHIPS + 1, SPAN)
        + sums(CHIPS, 2 * OWN)
        + sums(1, 16)
        + sums(SEQS, SPAN - 2 * OWN)
        + [
            dma((15,)), dma((3,)), dma((3,)), dma((4, 4)), dma((4, 4)), dma((4, 4)), dma((4, 4)), dma((4, 4)),
            dma((5, 4)), dma((5, 4)), dma((4, 4)), dma((4, 4)), dma((4, 4)), dma((4, 4)),
            dma((1, 4)), dma((1, 4)), dma((3,)), dma((3,)), dma((7,)), dma((7,)), dma((3,)), dma((3,)),
            dma((8, 3)), dma((8, 3)), dma((8,)), dma((8,)), dma((8, 3)), dma((8, 3)), dma((8,)), dma((4, 2)),
        ],
        compiler_params=pltpu.CompilerParams(
            collective_id=2, has_side_effects=True, vmem_limit_bytes=56 * 2**20
        ),
    )(*operands)


def shards(
    tokens,
    w_gate,
    w_xin,
    w_bc,
    w_dt,
    conv_x,
    conv_x_bias,
    conv_bc,
    conv_bc_bias,
    dt_bias,
    decay_rate,
    d_skip,
    norm_gain,
    w_out,
    lengths,
):
    operands = (
        tokens, w_gate, w_xin, w_bc, w_dt.T, conv_x, conv_x_bias[None, :], conv_bc, conv_bc_bias[None, :],
        norm_gain[None, :], w_out, dt_bias, decay_rate, d_skip, lengths,
    )
    return mix(operands, tokens.shape[0], lax.axis_size("seq"))


def solution(mesh):
    seqs, tens = mesh.shape["seq"], mesh.shape["tensor"]
    narrow = seqs == SEQS and tens == GROUPS == 2 * CHIPS
    body = shards if narrow else shards_wide
    in_specs = (
        P(("seq", "tensor"), None),
        P("seq", "tensor"),
        P("seq", "tensor"),
        P("seq", "tensor"),
        P("seq", "tensor"),
        P(None, "tensor"),
        P("tensor"),
        P(None, "tensor"),
        P("tensor"),
        P("tensor"),
        P("tensor"),
        P("tensor"),
        P("tensor"),
        P("tensor", "seq"),
        P(),
    )
    out_specs = P(("seq", "tensor"), None)
    return jax.shard_map(body, mesh=mesh, in_specs=in_specs, out_specs=out_specs, check_vma=False)
```

```python
import jax
import jax.numpy as jnp
import numpy as np
from jax import lax
from jax.experimental import pallas as pl
from jax.experimental.pallas import tpu as pltpu
from jax.sharding import PartitionSpec as P

HDIM = 64
GROUPS = 8
STATE = 128
CONV = 4
STRETCH = 256
INNER = 8192


HIGH = lax.Precision.HIGHEST


def from_behind(x, axis, by):
    count = lax.axis_size(axis)
    pairs = [(i, i + by) for i in range(count) if 0 <= i + by < count]
    return lax.ppermute(x, axis, pairs)


def carried_in(x, axis, combine, identity):
    count, here = (lax.axis_size(axis), lax.axis_index(axis))
    everything = jax.tree.map(
        lambda part, kind: lax.all_gather(part.astype(kind), axis), x, (jnp.bfloat16, jnp.bfloat16)
    )
    start = jax.tree.map(
        lambda part, zero: jnp.broadcast_to(jnp.asarray(zero, part.dtype), part.shape), x, identity
    )

    def hop(k, before):
        reached = k < here
        new = combine(
            before, jax.tree.map(lambda part, own: part[k].astype(own.dtype), everything, x)
        )
        return jax.tree.map(lambda a, b: jnp.where(reached, a, b), new, before)

    return lax.fori_loop(0, count, hop, start)


def doc_ids(lengths, positions):
    starts = jnp.cumsum(lengths) - lengths
    counted = jnp.sum((starts[None, :] <= positions[:, None]).astype(jnp.int32), axis=1)
    return counted - 1


def causal_conv(values, edge, weights, bias, docs, edge_docs):
    count = values.shape[0]
    extended = jnp.concatenate([edge, values], axis=0).astype(jnp.float32)
    all_docs = jnp.concatenate([edge_docs, docs])
    summed = jnp.zeros(values.shape, jnp.float32) + bias[None, :]
    for offset in range(weights.shape[0]):
        same = (all_docs[offset : offset + count] == docs).astype(jnp.float32)
        summed = (
            summed + weights[offset][None, :] * extended[offset : offset + count] * same[:, None]
        )
    return lax.optimization_barrier(jax.nn.silu(summed).astype(jnp.bfloat16))


def ssd_blocks(xvals, dtv, rate, bmat, cmat, docs, prev_doc, head_group, block):
    count, heads, hdim = xvals.shape
    nstate = bmat.shape[2]
    blocks = count // block
    logs = -dtv * rate[None, :]

    def split(array):
        return array.reshape((blocks, block) + array.shape[1:])

    lower = jnp.tril(jnp.ones((block, block), bool))

    def step(carry, pieces):
        state, last_doc = carry
        xblk, dblk, lblk, bblk, cblk, docblk = pieces
        cum = jnp.cumsum(lblk, axis=0)
        same = (docblk[:, None] == docblk[None, :]) & lower
        diff = cum.T[:, :, None] - cum.T[:, None, :]
        decay = jnp.exp(jnp.where(same[None], diff, -jnp.inf))
        scores = jnp.einsum("ign,jgn->gij", cblk, bblk, precision=HIGH)
        mixing = scores[head_group] * decay * dblk.T[:, None, :]
        inner = jnp.einsum("hij,jhp->ihp", mixing, xblk, precision=HIGH)
        open_in = (docblk == last_doc).astype(jnp.float32)
        carry_in = jnp.exp(cum) * open_in[:, None]
        chead = cblk[:, head_group, :]
        outer = jnp.einsum("ihn,hpn->ihp", chead, state, precision=HIGH) * carry_in[:, :, None]
        end_doc = docblk[-1]
        tail = (
            jnp.exp(cum[-1][None, :] - cum)
            * (docblk == end_doc).astype(jnp.float32)[:, None]
            * dblk
        )
        bhead = bblk[:, head_group, :]
        fresh = jnp.einsum("jh,jhp,jhn->hpn", tail, xblk, bhead, precision=HIGH)
        state = carry_in[-1][:, None, None] * state + fresh
        return ((state, end_doc), inner + outer)

    init = (jnp.zeros((heads, hdim, nstate), jnp.float32), prev_doc)
    (state, end_doc), outs = lax.scan(
        step, init, (split(xvals), split(dtv), split(logs), split(bmat), split(cmat), split(docs))
    )
    return (outs.reshape(count, heads, hdim), state)


def shards_wide(
    tokens,
    w_gate,
    w_xin,
    w_bc,
    w_dt,
    conv_x,
    conv_x_bias,
    conv_bc,
    conv_bc_bias,
    dt_bias,
    decay_rate,
    d_skip,
    norm_gain,
    w_out,
    lengths,
):
    tensor_count = lax.axis_size("tensor")
    seq_index = lax.axis_index("seq")
    tensor_index = lax.axis_index("tensor")
    span_rows = lax.all_gather(tokens, "tensor", axis=0, tiled=True)
    span_len = span_rows.shape[0]
    pieces = (
        lax.all_gather(w_gate, "seq", axis=0, tiled=True),
        lax.all_gather(w_xin, "seq", axis=0, tiled=True),
        lax.all_gather(w_bc, "seq", axis=0, tiled=True),
        lax.all_gather(w_dt, "seq", axis=0, tiled=True),
    )
    gate_acc, xin_acc, bc_acc, dt_acc = tuple(
        (
            jnp.dot(span_rows, weight_piece, preferred_element_type=jnp.float32)
            for weight_piece in pieces
        )
    )
    gate = gate_acc.astype(jnp.bfloat16)
    xin = xin_acc.astype(jnp.bfloat16)
    bcin = bc_acc.astype(jnp.bfloat16)
    dtin = dt_acc.astype(jnp.bfloat16)
    gate, xin, bcin, dtin = lax.optimization_barrier((gate, xin, bcin, dtin))
    positions = seq_index * span_len + jnp.arange(span_len, dtype=jnp.int32)
    docs = doc_ids(lengths, positions)
    edge_docs = doc_ids(lengths, seq_index * span_len + jnp.arange(-(CONV - 1), 0, dtype=jnp.int32))
    prev_span_doc = doc_ids(lengths, positions[:1] - 1)[0]
    edge_x, edge_bc = from_behind(
        (xin[span_len - (CONV - 1) :], bcin[span_len - (CONV - 1) :]), "seq", 1
    )
    x_conv = causal_conv(xin, edge_x, conv_x, conv_x_bias, docs, edge_docs)
    bc_conv = causal_conv(bcin, edge_bc, conv_bc, conv_bc_bias, docs, edge_docs)
    group_span = tensor_count // GROUPS
    my_group = tensor_index // group_span
    every_group = lax.all_gather(bc_conv, "tensor", axis=1, tiled=True)
    arranged = every_group.reshape(span_len, 2 * STATE, GROUPS)
    group_cols = lax.dynamic_slice_in_dim(arranged, my_group, 1, 2).reshape(span_len, 2 * STATE)
    head_dev = w_dt.shape[1]
    head_group = np.zeros(head_dev, dtype=np.int32)
    both = group_cols.astype(jnp.float32)
    bmat = both[:, None, :STATE]
    cmat = both[:, None, STATE:]
    xvals = x_conv.astype(jnp.float32).reshape(span_len, head_dev, HDIM)
    dtv = jax.nn.softplus(dtin.astype(jnp.float32) + dt_bias[None, :])
    block = min(STRETCH, span_len)
    y_local, end_state = ssd_blocks(
        xvals, dtv, decay_rate, bmat, cmat, docs, prev_span_doc, head_group, block
    )
    cum_span = jnp.cumsum(-dtv * decay_rate[None, :], axis=0)
    open_span = (docs == prev_span_doc).astype(jnp.float32)
    span_decay = jnp.exp(cum_span[-1]) * open_span[-1]

    def combine(earlier, later):
        return (earlier[0] * later[0], later[0][:, None, None] * earlier[1] + later[1])

    entering = carried_in(
        (span_decay, end_state),
        "seq",
        combine,
        (jnp.ones_like(span_decay), jnp.zeros_like(end_state)),
    )[1]
    carried = jnp.exp(cum_span) * open_span[:, None]
    y_enter = (
        jnp.einsum("ihn,hpn->ihp", cmat[:, head_group, :], entering, precision=HIGH)
        * carried[:, :, None]
    )
    yvals = (y_local + y_enter + d_skip[None, :, None] * xvals).reshape(span_len, head_dev * HDIM)
    gated = yvals * jax.nn.silu(gate.astype(jnp.float32))
    local_sq = jnp.sum(gated * gated, axis=1)
    group_mark = (jnp.arange(GROUPS) == my_group).astype(jnp.float32)
    every_sum = lax.psum(local_sq[:, None] * group_mark[None, :], "tensor")
    group_mean = jnp.sum(every_sum * group_mark[None, :], axis=1) / (INNER // GROUPS)
    normed = (gated * lax.rsqrt(group_mean + 1e-05)[:, None] * norm_gain[None, :]).astype(
        jnp.bfloat16
    )
    w_full = lax.all_gather(w_out, "seq", axis=1, tiled=True)
    return lax.psum_scatter(
        jnp.dot(normed, w_full, preferred_element_type=jnp.float32).astype(jnp.bfloat16),
        "tensor",
        scatter_dimension=0,
        tiled=True,
    )


def enter(peers):
    barrier = pltpu.get_barrier_semaphore()
    for peer in peers:
        pl.semaphore_signal(barrier, inc=1, device_id=peer, device_id_type=pl.DeviceIdType.MESH)
    pl.semaphore_wait(barrier, len(peers))


def remote(src, dst, send, recv, peer):
    return pltpu.make_async_remote_copy(
        src_ref=src,
        dst_ref=dst,
        send_sem=send,
        recv_sem=recv,
        device_id=peer,
        device_id_type=pl.DeviceIdType.MESH,
    )


SEQS, CHIPS, OWN, SPAN, WIDE, HALF = 4, 4, 32, 256, 256, 128
LOG2E = 1.4426950408889634


def silu(v):
    return v / (1.0 + jnp.exp(-v))


class Sums:
    def __init__(self, bufs, sems, s, z, c):
        self.sa, self.sb, self.ra, self.rb, self.qa, self.qb, self.pa, self.pb, self.k0, self.k1, self.k2 = bufs
        self.sems = sems
        self.x, self.y = (s ^ 1, 2 * z + c), (s ^ 2, 2 * z + c)

    def copies(self, u):
        send, recv = self.sems
        return (
            remote(self.sa.at[u], self.ra.at[u], send.at[u, 0], recv.at[u, 0], self.x),
            remote(self.sb.at[u], self.rb.at[u], send.at[u, 1], recv.at[u, 1], self.y),
            remote(self.qa.at[u], self.pa.at[u], send.at[u, 2], recv.at[u, 2], self.y),
            remote(self.qb.at[u], self.pb.at[u], send.at[u, 3], recv.at[u, 3], self.x),
        )

    def emit(self, u, get):
        first, second, _, _ = self.copies(u)
        far = get(3)
        self.sa[u, 1] = far[:, :HALF].astype(jnp.bfloat16)
        self.sb[u, 1] = far[:, HALF:].astype(jnp.bfloat16)
        near = get(1)
        self.sa[u, 0] = near[:, :HALF].astype(jnp.bfloat16)
        first.start()
        self.k1[u] = near[:, HALF:]
        near = get(2)
        self.sb[u, 0] = near[:, HALF:].astype(jnp.bfloat16)
        second.start()
        self.k2[u] = near[:, :HALF]
        self.k0[u] = get(0)

    def relay(self, u):
        first, second, third, fourth = self.copies(u)
        first.wait_recv()
        self.qa[u] = (self.k2[u] + self.ra[u, 1].astype(jnp.float32)).astype(jnp.bfloat16)
        third.start()
        second.wait_recv()
        self.qb[u] = (self.k1[u] + self.rb[u, 1].astype(jnp.float32)).astype(jnp.bfloat16)
        fourth.start()

    def final(self, u):
        _, _, third, fourth = self.copies(u)
        third.wait_recv()
        fourth.wait_recv()
        own = self.k0[u]
        left = own[:, :HALF] + self.ra[u, 0].astype(jnp.float32) + self.pa[u].astype(jnp.float32)
        right = own[:, HALF:] + self.rb[u, 0].astype(jnp.float32) + self.pb[u].astype(jnp.float32)
        return jnp.concatenate([left, right], axis=1).astype(jnp.bfloat16)

    def drain(self, u):
        for copy in self.copies(u):
            copy.wait_send()


def mix_kernel(
    tok_hbm, wg_hbm, wx_hbm, wb_hbm, wdt_hbm, cx_hbm, cxb_hbm, cb_hbm, cbb_hbm, gain_hbm, wo_hbm,
    bias_hbm, rate_hbm, skip_hbm, len_hbm, out_ref,
    wg, wx, wb, wdt, cx, cxb, cb, cbb, gain, wo, bias_s, rate_s, skip_s, len_s,
    tok, rel, xs, xc, gs, bs, halo, bct, bca, bcp, dtp, dts, dtg, dtv,
    held, normed, part, sib, pair, got, done,
    *rest,
):
    big, rest = rest[:11], rest[11:]
    few, rest = rest[:11], rest[11:]
    rim, rest = rest[:11], rest[11:]
    three, rest = rest[:11], rest[11:]
    (
        w_sem, t_send, t_recv, zu_send, zd_send, z_recv, f_send, f_recv,
        g_send, g_recv, v_send, v_recv, b_send, b_recv, h_send, h_recv, d_send, d_recv,
        e_send, e_recv, a_send, a_recv,
        y_send, y_recv, p_send, p_recv, r_send, r_recv, o_send, o_recv,
    ) = rest
    s, t = lax.axis_index("seq"), lax.axis_index("tensor")
    tens = 2 * CHIPS
    z, c = t // 2, t % 2
    sibling = (s, 2 * z + 1 - c)
    depth = wx.shape[0]
    own_cols = pl.ds(pl.multiple_of(s * depth, depth), depth)
    loads = [
        pltpu.make_async_copy(src, dst, w_sem.at[i])
        for i, (src, dst) in enumerate((
            (len_hbm, len_s), (tok_hbm.at[:, own_cols], tok.at[z, c, s]), (wb_hbm, wb), (wx_hbm, wx),
            (wdt_hbm, wdt), (wg_hbm, wg), (cb_hbm, cb), (cbb_hbm, cbb), (cx_hbm, cx), (cxb_hbm, cxb),
            (bias_hbm, bias_s), (rate_hbm, rate_s), (skip_hbm, skip_s), (gain_hbm, gain), (wo_hbm, wo),
        ))
    ]
    for load in loads:
        load.start()
    along = [(s ^ r, t) for r in range(1, SEQS)]
    across = [(s, lax.rem(t + d, tens)) for d in range(1, tens)]
    enter(along + across)

    spread = [
        remote(
            tok_hbm.at[:, pl.ds(pl.multiple_of(peer[0] * depth, depth), depth)],
            tok.at[z, c, s], t_send.at[i], t_recv.at[i], peer,
        )
        for i, peer in enumerate(along)
    ]
    for copy in spread:
        copy.start()
    loads[0].wait()

    total = SEQS * SPAN
    pos = lax.broadcasted_iota(jnp.int32, (total, HALF), 0)
    begin, start = jnp.zeros((total, HALF), jnp.int32), jnp.int32(0)
    for r in range(len_s.shape[0]):
        begin = jnp.where(pos >= start, start, begin)
        start = start + len_s[r]
    rel[...] = pos - begin

    first = z - 1 + 2 * ((3 - z) // 3)
    last = 3 * (1 - z // 2)
    order = [z, first, 6 - z - first - last, last]

    inner_chip = (z > 0) & (z < CHIPS - 1)

    def hops(zb, r):
        part = tok.at[zb, c, s ^ r]
        up = remote(part, part, zu_send.at[zb, r], z_recv.at[zb, r], (s, 2 * lax.rem(z + 1, CHIPS) + c))
        down = remote(
            part, part, zd_send.at[zb, r], z_recv.at[zb, r], (s, 2 * lax.rem(z + CHIPS - 1, CHIPS) + c)
        )
        over = remote(part, part, f_send.at[zb, r], f_recv.at[zb, r], sibling)
        return up, down, over, (z < CHIPS - 1) & (zb <= z), (z > 0) & (zb >= z)

    def arrive(i, pieces=range(1, SEQS)):
        for r in pieces:
            up, down, over, goes_up, goes_down = hops(order[i], r)
            if i:
                up.wait_recv()
            elif r:
                spread[r - 1].wait_recv()
            else:
                loads[1].wait()
            pl.when(goes_up)(up.start)
            pl.when(goes_down)(down.start)
            over.start()

    def arrive_if(which, i, pieces=range(SEQS)):
        if i < CHIPS:
            pl.when(which)(lambda: arrive(i, pieces))

    sums = Sums(big, (g_send, g_recv), s, z, c)
    sumg = Sums(three, (v_send, v_recv), s, z, c)
    sumb = Sums(few, (b_send, b_recv), s, z, c)
    sumh = Sums(rim, (h_send, h_recv), s, z, c)

    def product(rows, w):
        def get(r):
            cols = pl.ds(pl.multiple_of((s ^ r) * WIDE, WIDE), WIDE)
            return jnp.dot(rows, w[:, cols], preferred_element_type=jnp.float32)

        return get

    arrive(0, [0])
    arrive(1, [0])
    arrive_if(inner_chip, 2, [0])
    arrive(0)
    for i in range(CHIPS):
        if i:
            if i == 1:
                arrive(i)
            else:
                arrive_if(~inner_chip, i)
            arrive_if(inner_chip, i + 1, range(1 if i == 1 else 0, SEQS))
        for r in range(SEQS):
            hops(order[i], r)[2].wait_recv()
        rows = tok[order[i]].reshape(SPAN, depth)
        if i == 0:
            loads[2].wait()
        bcp[...] = jnp.dot(rows, wb[...], preferred_element_type=jnp.float32).reshape(2, SEQS, OWN, WIDE)
        sumb.emit(i, lambda r: bcp[:, s ^ r].reshape(2 * OWN, WIDE))

        @pl.when(order[i] == CHIPS - 1)
        def _():
            halo[...] = bcp[1, :, OWN - 16 :, :]

        if i == CHIPS - 1:
            sumh.emit(0, lambda r: halo[lax.rem((s ^ r) + SEQS - 1, SEQS)])
        if i == 0:
            loads[3].wait()
        sums.emit(i, product(rows, wx))
        if i == 0:
            loads[5].wait()
            sums.emit(CHIPS, product(rows, wg))
        if i:
            sumb.relay(i - 1)
            sums.relay(i - 1)
    sumb.relay(CHIPS - 1)
    sumh.relay(0)

    def span_rows(q):
        return tok[:, :, q].reshape(SPAN, depth)

    sums.relay(CHIPS)
    def other_rows(q):
        rows = [tok[zb, :, q].reshape(2 * OWN, depth) for zb in order[1:]]
        return jnp.concatenate(rows, axis=0)

    sumg.emit(0, product(other_rows(0), wg))
    bs[:16, :] = sumh.final(0).astype(jnp.float32)
    for i in range(CHIPS):
        bs[pl.ds(pl.multiple_of(16 + order[i] * 2 * OWN, 16), 2 * OWN), :] = sumb.final(i).astype(jnp.float32)

    for load in loads[4:5] + loads[6:]:
        load.wait()
    away = rel[pl.ds(pl.multiple_of(s * SPAN, SPAN), SPAN), :1]

    def conv(src, begin, w, bias, away):
        out = w[CONV - 1 :, :] * src[begin : begin + SPAN, :] + bias
        for back in range(1, CONV):
            tap = w[CONV - 1 - back : CONV - back, :] * src[begin - back : begin - back + SPAN, :]
            out = out + jnp.where(away >= back, tap, 0.0)
        return silu(out).astype(jnp.bfloat16)

    bcc = conv(bs, 16, cb[...], cbb[...], away)
    to = lax.broadcasted_iota(jnp.int32, (WIDE, WIDE), 0)
    frm = lax.broadcasted_iota(jnp.int32, (WIDE, WIDE), 1)
    pick = (frm == (to % 32) * GROUPS + to // 32).astype(jnp.float32).astype(jnp.bfloat16)
    bct[...] = (
        lax.dot_general(pick, bcc, (((1,), (1,)), ((), ())), preferred_element_type=jnp.float32)
        .astype(jnp.bfloat16)
        .reshape(GROUPS, 32, SPAN)
    )
    swaps = [
        remote(bct.at[peer[1]], bca.at[s, t], e_send.at[i], e_recv.at[i], peer)
        for i, peer in enumerate(across)
    ]
    for copy in swaps:
        copy.start()
    bca[s, t] = bct[t]
    sums.relay(CHIPS - 1)
    heads = 4
    for q in range(SEQS):
        some = lax.dot_general(
            wdt[...], span_rows(q), (((1,), (1,)), ((), ())), preferred_element_type=jnp.float32
        )
        for d in range(SEQS):
            dtp[d, heads * q : heads * (q + 1), :] = some[heads * d : heads * (d + 1), :]
    dts[...] = dtp[...].astype(jnp.bfloat16)
    steps = [
        remote(dts.at[peer[0]], dtg.at[i], d_send.at[i], d_recv.at[i], peer) for i, peer in enumerate(along)
    ]
    for copy in steps:
        copy.start()
    sumg.emit(1, product(other_rows(1), wg))
    for copy in swaps:
        copy.wait_recv()
    groups = [
        remote(bca.at[s], bca.at[s], a_send.at[i], a_recv.at[i], peer)
        for i, peer in enumerate(along)
    ]
    for copy in groups:
        copy.start()
    sumg.relay(0)
    for i in range(CHIPS):
        full = sums.final(i).astype(jnp.float32).reshape(2, SEQS, OWN, WIDE)
        for half in range(2):
            for q in range(SEQS):
                at = 16 + q * SPAN + half * OWN + order[i] * 2 * OWN
                xs[pl.ds(pl.multiple_of(at, 16), OWN), :] = full[half, q]
    sumg.emit(2, product(other_rows(2), wg))
    full = sums.final(CHIPS).astype(jnp.float32).reshape(2, SEQS, OWN, WIDE)
    for half in range(2):
        for q in range(SEQS):
            gs[q, pl.ds(pl.multiple_of(z * 2 * OWN + half * OWN, 16), OWN), :] = full[half, q]
    xs[:16, :] = jnp.zeros((16, WIDE), jnp.float32)
    mine = pl.ds(pl.multiple_of(s * WIDE, WIDE), WIDE)
    for q in range(SEQS):
        xc[q * SPAN : (q + 1) * SPAN, :] = conv(
            xs, 16 + q * SPAN, cx[:, mine], cxb[:, mine], rel[q * SPAN : (q + 1) * SPAN, :1]
        ).astype(jnp.float32)
    sumg.relay(1)
    sumg.emit(3, product(other_rows(3), wg))
    for copy in steps:
        copy.wait_recv()
    small = dts[s].astype(jnp.float32)
    for i in range(SEQS - 1):
        small = small + dtg[i].astype(jnp.float32)
    line = to[: heads * SEQS, :] % heads
    bias, rate = jnp.zeros(line.shape, jnp.float32), jnp.zeros(line.shape, jnp.float32)
    for h in range(heads):
        bias = jnp.where(line == h, bias_s[heads * s + h], bias)
        rate = jnp.where(line == h, -LOG2E * rate_s[heads * s + h], rate)
    small = small.astype(jnp.bfloat16).astype(jnp.float32) + bias
    small = jnp.maximum(small, 0.0) + jnp.log1p(jnp.exp(-jnp.abs(small)))
    for q in range(SEQS):
        dtv[q, :heads, :] = small[heads * q : heads * (q + 1), :]
        dtv[q, heads:, :] = (small * rate)[heads * q : heads * (q + 1), :]

    dif = to - frm
    upto = (dif <= 0).astype(jnp.float32)
    lane = frm // HDIM
    skip = jnp.zeros((1, WIDE), jnp.float32)
    for h in range(heads):
        skip = jnp.where(lane[:1] == h, skip_s[heads * s + h], skip)

    cols_out = wo.shape[1]
    few_rows = OWN // 2
    gathers = [
        [
            remote(held.at[s, k], held.at[s, k], y_send.at[k, i], y_recv.at[k, i], peer)
            for i, peer in enumerate(along)
        ]
        for k in range(2 * SEQS)
    ]
    pairs = [
        remote(part.at[k, 1 - c], sib.at[k], p_send.at[k], p_recv.at[k], sibling)
        for k in range(2 * SEQS)
    ]

    def reduces(k):
        peers = [lax.rem(z + d, CHIPS) for d in range(1, CHIPS)]
        return [
            remote(pair.at[k, to], got.at[k, i], r_send.at[k, i], r_recv.at[k, i], (s, 2 * to + c))
            for i, to in enumerate(peers)
        ]

    def place(frm, half):
        cols = pl.ds(pl.multiple_of(frm * cols_out, cols_out), cols_out)
        return out_ref.at[half * few_rows : (half + 1) * few_rows, cols]

    def deliver(k, frm):
        return remote(done.at[k], place(frm, k % 2), o_send.at[k], o_recv.at[frm, k % 2], (k // 2, t))

    def keep(k):
        return pltpu.make_async_copy(done.at[k], place(s, k % 2), o_send.at[k])

    def project(k):
        for copy in gathers[k]:
            copy.wait_recv()
        squares = jnp.zeros((SPAN // 2, HALF), jnp.float32)
        for n in range(2 * SEQS):
            piece = held[n // 2, k, n % 2].astype(jnp.float32)
            squares = squares + piece * piece
        scale = lax.rsqrt(jnp.sum(squares, axis=1, keepdims=True) / (SEQS * WIDE) + 1e-05)
        for n in range(2 * SEQS):
            wide = slice(n * HALF, (n + 1) * HALF)
            piece = held[n // 2, k, n % 2].astype(jnp.float32)
            normed[:, wide] = (piece * scale * gain[:, wide]).astype(jnp.bfloat16)
        for n in range(cols_out // WIDE):
            wide = slice(n * WIDE, (n + 1) * WIDE)
            acc = jnp.dot(normed[...], wo[:, wide], preferred_element_type=jnp.float32)
            acc = acc.reshape(CHIPS, 2, few_rows, WIDE).astype(jnp.bfloat16)
            for half in range(2):
                part[k, half, :, :, wide] = acc[:, half]
        pairs[k].start()

    def combine(k):
        pairs[k].wait_recv()
        pair[k] = (part[k, c].astype(jnp.float32) + sib[k].astype(jnp.float32)).astype(jnp.bfloat16)
        for copy in reduces(k):
            copy.start()

    def collect(k):
        for copy in reduces(k):
            copy.wait_recv()
        total = pair[k, z].astype(jnp.float32)
        for i in range(CHIPS - 1):
            total = total + got[k, i].astype(jnp.float32)
        done[k] = total.astype(jnp.bfloat16)
        pl.when(s != k // 2)(deliver(k, s).start)
        pl.when(s == k // 2)(keep(k).start)

    def advance(k):
        project(k)
        combine(k)
        if k > 1:
            collect(k - 2)

    state = jnp.zeros((STATE, WIDE), jnp.float32)
    local = to[:, :1]
    for q in range(SEQS):
        here = slice(q * SPAN, (q + 1) * SPAN)
        away = rel[here, :1]
        for i, copy in enumerate(groups):
            pl.when((s ^ (i + 1)) == q)(copy.wait_recv)
        bt = bca[q, :4].reshape(STATE, SPAN)
        cn = bca[q, 4:].reshape(STATE, SPAN).astype(jnp.float32).T.astype(jnp.bfloat16)
        scores = jnp.dot(cn, bt, preferred_element_type=jnp.float32)
        scores = jnp.where((dif >= 0) & (dif <= away), scores, 0.0)
        both = dtv[q]
        cum = jnp.dot(both, upto, precision=HIGH, preferred_element_type=jnp.float32)
        both = jnp.where(to[:8, :] < heads, both, cum)
        cols = jnp.concatenate([both, jnp.zeros((HALF - 8, SPAN), jnp.float32)], axis=0).T

        def expand(first):
            out = jnp.broadcast_to(cols[:, first : first + 1], (SPAN, WIDE))
            for h in range(1, heads):
                out = jnp.where(lane == h, cols[:, first + h : first + h + 1], out)
            return out

        dte, cume = expand(0), expand(heads)
        xv = xc[here, :]
        xdt = xv * dte
        inner = jnp.zeros((SPAN, WIDE), jnp.float32)
        for h in range(heads):
            gap = cols[:, heads + h : heads + h + 1] - both[heads + h : heads + h + 1, :]
            mixing = (jnp.exp2(jnp.minimum(gap, 0.0)) * scores).astype(jnp.bfloat16)
            inner = inner + jnp.dot(
                mixing, jnp.where(lane == h, xdt, 0.0).astype(jnp.bfloat16),
                preferred_element_type=jnp.float32,
            )
        carry = jnp.where(away > local, jnp.exp2(cume), 0.0)
        ends = cume[SPAN - 1 :, :]
        tail = jnp.where(local >= SPAN - 1 - away[SPAN - 1 :, :], jnp.exp2(ends - cume), 0.0)
        fresh = jnp.dot(bt, (tail * xdt).astype(jnp.bfloat16), preferred_element_type=jnp.float32)
        outer = jnp.dot(cn, state.astype(jnp.bfloat16), preferred_element_type=jnp.float32)
        state = carry[SPAN - 1 :, :] * state + fresh
        y = inner + outer * carry + skip * xv
        if q == 0:
            sumg.relay(2)
        if q == 1:
            sumg.relay(3)
        some = sumg.final(q).astype(jnp.float32)
        for i in range(1, CHIPS):
            to_rows = pl.ds(pl.multiple_of(order[i] * 2 * OWN, 16), 2 * OWN)
            gs[q, to_rows, :] = some[(i - 1) * 2 * OWN : i * 2 * OWN]
        gate = gs[q]
        gated = (y * silu(gate)).reshape(2 * CHIPS, 2, few_rows, WIDE)
        for half in range(2):
            k = 2 * q + half
            some = gated[:, half].reshape(SPAN // 2, WIDE).astype(jnp.bfloat16)
            held[s, k, 0], held[s, k, 1] = some[:, :HALF], some[:, HALF:]
            for copy in gathers[k]:
                copy.start()
        for k in range(2 * q - 4, 2 * q - 2):
            if k >= 0:
                advance(k)
    last_k = 2 * SEQS - 1
    for k in range(last_k - 3, last_k + 1):
        advance(k)
    collect(last_k - 1)
    collect(last_k)
    for q in range(SEQS):
        for half in range(2):
            pl.when(s != q)(deliver(half, q).wait_recv)

    for zb in range(CHIPS):
        for r in range(SEQS):
            up, down, over, goes_up, goes_down = hops(zb, r)
            pl.when(goes_up)(up.wait_send)
            pl.when(goes_down)(down.wait_send)
            over.wait_send()
    for copy in spread + steps + swaps + groups:
        copy.wait_send()
    for k in range(2 * SEQS):
        for copy in gathers[k] + [pairs[k]] + reduces(k):
            copy.wait_send()
        pl.when(s != k // 2)(deliver(k, s).wait_send)
        pl.when(s == k // 2)(keep(k).wait)
    for u in range(5):
        sums.drain(u)
    for u in range(4):
        sumg.drain(u)
    for u in range(4):
        sumb.drain(u)
    sumh.drain(0)


def mix(operands, own, seqs):
    tokens, w_gate, w_xin, w_bc, w_dt, conv_x, conv_xb, conv_b, conv_bb, gain, w_out = operands[:11]
    depth = w_xin.shape[0]
    total = SEQS * SPAN
    cols = w_out.shape[1]
    dma = pltpu.SemaphoreType.DMA
    bf, f32 = jnp.bfloat16, jnp.float32

    def sums(n, rows):
        pair = pltpu.VMEM((n, 2, rows, HALF), bf)
        one = pltpu.VMEM((n, rows, HALF), bf)
        return [pair] * 4 + [one] * 4 + [pltpu.VMEM((n, rows, WIDE), f32)] + [pltpu.VMEM((n, rows, HALF), f32)] * 2

    return pl.pallas_call(
        mix_kernel,
        out_shape=jax.ShapeDtypeStruct((own, cols * seqs), bf),
        in_specs=[pl.BlockSpec(memory_space=pl.ANY)] * len(operands),
        out_specs=pl.BlockSpec(memory_space=pl.ANY),
        scratch_shapes=[pltpu.VMEM(a.shape, a.dtype) for a in operands[1:11]]
        + [pltpu.SMEM(a.shape, a.dtype) for a in operands[11:]]
        + [
            pltpu.VMEM((CHIPS, 2, SEQS, OWN, depth), bf),
            pltpu.VMEM((total, HALF), jnp.int32),
            pltpu.VMEM((16 + total, WIDE), f32),
            pltpu.VMEM((total, WIDE), f32),
            pltpu.VMEM((SEQS, SPAN, WIDE), f32),
            pltpu.VMEM((16 + SPAN, WIDE), f32),
            pltpu.VMEM((SEQS, 16, WIDE), f32),
            pltpu.VMEM((GROUPS, 32, SPAN), bf),
            pltpu.VMEM((SEQS, GROUPS, 32, SPAN), bf),
            pltpu.VMEM((2, SEQS, OWN, WIDE), f32),
            pltpu.VMEM((SEQS, 16, SPAN), f32),
            pltpu.VMEM((SEQS, 16, SPAN), bf),
            pltpu.VMEM((3, 16, SPAN), bf),
            pltpu.VMEM((SEQS, 8, SPAN), f32),
            pltpu.VMEM((SEQS, 2 * SEQS, 2, SPAN // 2, HALF), bf),
            pltpu.VMEM((SPAN // 2, SEQS * WIDE), bf),
            pltpu.VMEM((2 * SEQS, 2, CHIPS, OWN // 2, cols), bf),
            pltpu.VMEM((2 * SEQS, CHIPS, OWN // 2, cols), bf),
            pltpu.VMEM((2 * SEQS, CHIPS, OWN // 2, cols), bf),
            pltpu.VMEM((2 * SEQS, CHIPS - 1, OWN // 2, cols), bf),
            pltpu.VMEM((2 * SEQS, OWN // 2, cols), bf),
        ]
        + sums(CHIPS + 1, SPAN)
        + sums(CHIPS, 2 * OWN)
        + sums(1, 16)
        + sums(SEQS, SPAN - 2 * OWN)
        + [
            dma((15,)), dma((3,)), dma((3,)), dma((4, 4)), dma((4, 4)), dma((4, 4)), dma((4, 4)), dma((4, 4)),
            dma((5, 4)), dma((5, 4)), dma((4, 4)), dma((4, 4)), dma((4, 4)), dma((4, 4)),
            dma((1, 4)), dma((1, 4)), dma((3,)), dma((3,)), dma((7,)), dma((7,)), dma((3,)), dma((3,)),
            dma((8, 3)), dma((8, 3)), dma((8,)), dma((8,)), dma((8, 3)), dma((8, 3)), dma((8,)), dma((4, 2)),
        ],
        compiler_params=pltpu.CompilerParams(
            collective_id=2, has_side_effects=True, vmem_limit_bytes=56 * 2**20
        ),
    )(*operands)


def shards(
    tokens,
    w_gate,
    w_xin,
    w_bc,
    w_dt,
    conv_x,
    conv_x_bias,
    conv_bc,
    conv_bc_bias,
    dt_bias,
    decay_rate,
    d_skip,
    norm_gain,
    w_out,
    lengths,
):
    operands = (
        tokens, w_gate, w_xin, w_bc, w_dt.T, conv_x, conv_x_bias[None, :], conv_bc, conv_bc_bias[None, :],
        norm_gain[None, :], w_out, dt_bias, decay_rate, d_skip, lengths,
    )
    return mix(operands, tokens.shape[0], lax.axis_size("seq"))


def solution(mesh):
    seqs, tens = mesh.shape["seq"], mesh.shape["tensor"]
    narrow = seqs == SEQS and tens == GROUPS == 2 * CHIPS
    body = shards if narrow else shards_wide
    in_specs = (
        P(("seq", "tensor"), None),
        P("seq", "tensor"),
        P("seq", "tensor"),
        P("seq", "tensor"),
        P("seq", "tensor"),
        P(None, "tensor"),
        P("tensor"),
        P(None, "tensor"),
        P("tensor"),
        P("tensor"),
        P("tensor"),
        P("tensor"),
        P("tensor"),
        P("tensor", "seq"),
        P(),
    )
    out_specs = P(("seq", "tensor"), None)
    return jax.shard_map(body, mesh=mesh, in_specs=in_specs, out_specs=out_specs, check_vma=False)
```

```python
import jax
import jax.numpy as jnp
import numpy as np
from jax import lax
from jax.experimental import pallas as pl
from jax.experimental.pallas import tpu as pltpu
from jax.sharding import PartitionSpec as P

HDIM = 64
GROUPS = 8
STATE = 128
CONV = 4
STRETCH = 256
INNER = 8192


HIGH = lax.Precision.HIGHEST


def from_behind(x, axis, by):
    count = lax.axis_size(axis)
    pairs = [(i, i + by) for i in range(count) if 0 <= i + by < count]
    return lax.ppermute(x, axis, pairs)


def carried_in(x, axis, combine, identity):
    count, here = (lax.axis_size(axis), lax.axis_index(axis))
    everything = jax.tree.map(
        lambda part, kind: lax.all_gather(part.astype(kind), axis), x, (jnp.bfloat16, jnp.bfloat16)
    )
    start = jax.tree.map(
        lambda part, zero: jnp.broadcast_to(jnp.asarray(zero, part.dtype), part.shape), x, identity
    )

    def hop(k, before):
        reached = k < here
        new = combine(
            before, jax.tree.map(lambda part, own: part[k].astype(own.dtype), everything, x)
        )
        return jax.tree.map(lambda a, b: jnp.where(reached, a, b), new, before)

    return lax.fori_loop(0, count, hop, start)


def doc_ids(lengths, positions):
    starts = jnp.cumsum(lengths) - lengths
    counted = jnp.sum((starts[None, :] <= positions[:, None]).astype(jnp.int32), axis=1)
    return counted - 1


def causal_conv(values, edge, weights, bias, docs, edge_docs):
    count = values.shape[0]
    extended = jnp.concatenate([edge, values], axis=0).astype(jnp.float32)
    all_docs = jnp.concatenate([edge_docs, docs])
    summed = jnp.zeros(values.shape, jnp.float32) + bias[None, :]
    for offset in range(weights.shape[0]):
        same = (all_docs[offset : offset + count] == docs).astype(jnp.float32)
        summed = (
            summed + weights[offset][None, :] * extended[offset : offset + count] * same[:, None]
        )
    return lax.optimization_barrier(jax.nn.silu(summed).astype(jnp.bfloat16))


def ssd_blocks(xvals, dtv, rate, bmat, cmat, docs, prev_doc, head_group, block):
    count, heads, hdim = xvals.shape
    nstate = bmat.shape[2]
    blocks = count // block
    logs = -dtv * rate[None, :]

    def split(array):
        return array.reshape((blocks, block) + array.shape[1:])

    lower = jnp.tril(jnp.ones((block, block), bool))

    def step(carry, pieces):
        state, last_doc = carry
        xblk, dblk, lblk, bblk, cblk, docblk = pieces
        cum = jnp.cumsum(lblk, axis=0)
        same = (docblk[:, None] == docblk[None, :]) & lower
        diff = cum.T[:, :, None] - cum.T[:, None, :]
        decay = jnp.exp(jnp.where(same[None], diff, -jnp.inf))
        scores = jnp.einsum("ign,jgn->gij", cblk, bblk, precision=HIGH)
        mixing = scores[head_group] * decay * dblk.T[:, None, :]
        inner = jnp.einsum("hij,jhp->ihp", mixing, xblk, precision=HIGH)
        open_in = (docblk == last_doc).astype(jnp.float32)
        carry_in = jnp.exp(cum) * open_in[:, None]
        chead = cblk[:, head_group, :]
        outer = jnp.einsum("ihn,hpn->ihp", chead, state, precision=HIGH) * carry_in[:, :, None]
        end_doc = docblk[-1]
        tail = (
            jnp.exp(cum[-1][None, :] - cum)
            * (docblk == end_doc).astype(jnp.float32)[:, None]
            * dblk
        )
        bhead = bblk[:, head_group, :]
        fresh = jnp.einsum("jh,jhp,jhn->hpn", tail, xblk, bhead, precision=HIGH)
        state = carry_in[-1][:, None, None] * state + fresh
        return ((state, end_doc), inner + outer)

    init = (jnp.zeros((heads, hdim, nstate), jnp.float32), prev_doc)
    (state, end_doc), outs = lax.scan(
        step, init, (split(xvals), split(dtv), split(logs), split(bmat), split(cmat), split(docs))
    )
    return (outs.reshape(count, heads, hdim), state)


def shards_wide(
    tokens,
    w_gate,
    w_xin,
    w_bc,
    w_dt,
    conv_x,
    conv_x_bias,
    conv_bc,
    conv_bc_bias,
    dt_bias,
    decay_rate,
    d_skip,
    norm_gain,
    w_out,
    lengths,
):
    tensor_count = lax.axis_size("tensor")
    seq_index = lax.axis_index("seq")
    tensor_index = lax.axis_index("tensor")
    span_rows = lax.all_gather(tokens, "tensor", axis=0, tiled=True)
    span_len = span_rows.shape[0]
    pieces = (
        lax.all_gather(w_gate, "seq", axis=0, tiled=True),
        lax.all_gather(w_xin, "seq", axis=0, tiled=True),
        lax.all_gather(w_bc, "seq", axis=0, tiled=True),
        lax.all_gather(w_dt, "seq", axis=0, tiled=True),
    )
    gate_acc, xin_acc, bc_acc, dt_acc = tuple(
        (
            jnp.dot(span_rows, weight_piece, preferred_element_type=jnp.float32)
            for weight_piece in pieces
        )
    )
    gate = gate_acc.astype(jnp.bfloat16)
    xin = xin_acc.astype(jnp.bfloat16)
    bcin = bc_acc.astype(jnp.bfloat16)
    dtin = dt_acc.astype(jnp.bfloat16)
    gate, xin, bcin, dtin = lax.optimization_barrier((gate, xin, bcin, dtin))
    positions = seq_index * span_len + jnp.arange(span_len, dtype=jnp.int32)
    docs = doc_ids(lengths, positions)
    edge_docs = doc_ids(lengths, seq_index * span_len + jnp.arange(-(CONV - 1), 0, dtype=jnp.int32))
    prev_span_doc = doc_ids(lengths, positions[:1] - 1)[0]
    edge_x, edge_bc = from_behind(
        (xin[span_len - (CONV - 1) :], bcin[span_len - (CONV - 1) :]), "seq", 1
    )
    x_conv = causal_conv(xin, edge_x, conv_x, conv_x_bias, docs, edge_docs)
    bc_conv = causal_conv(bcin, edge_bc, conv_bc, conv_bc_bias, docs, edge_docs)
    group_span = tensor_count // GROUPS
    my_group = tensor_index // group_span
    every_group = lax.all_gather(bc_conv, "tensor", axis=1, tiled=True)
    arranged = every_group.reshape(span_len, 2 * STATE, GROUPS)
    group_cols = lax.dynamic_slice_in_dim(arranged, my_group, 1, 2).reshape(span_len, 2 * STATE)
    head_dev = w_dt.shape[1]
    head_group = np.zeros(head_dev, dtype=np.int32)
    both = group_cols.astype(jnp.float32)
    bmat = both[:, None, :STATE]
    cmat = both[:, None, STATE:]
    xvals = x_conv.astype(jnp.float32).reshape(span_len, head_dev, HDIM)
    dtv = jax.nn.softplus(dtin.astype(jnp.float32) + dt_bias[None, :])
    block = min(STRETCH, span_len)
    y_local, end_state = ssd_blocks(
        xvals, dtv, decay_rate, bmat, cmat, docs, prev_span_doc, head_group, block
    )
    cum_span = jnp.cumsum(-dtv * decay_rate[None, :], axis=0)
    open_span = (docs == prev_span_doc).astype(jnp.float32)
    span_decay = jnp.exp(cum_span[-1]) * open_span[-1]

    def combine(earlier, later):
        return (earlier[0] * later[0], later[0][:, None, None] * earlier[1] + later[1])

    entering = carried_in(
        (span_decay, end_state),
        "seq",
        combine,
        (jnp.ones_like(span_decay), jnp.zeros_like(end_state)),
    )[1]
    carried = jnp.exp(cum_span) * open_span[:, None]
    y_enter = (
        jnp.einsum("ihn,hpn->ihp", cmat[:, head_group, :], entering, precision=HIGH)
        * carried[:, :, None]
    )
    yvals = (y_local + y_enter + d_skip[None, :, None] * xvals).reshape(span_len, head_dev * HDIM)
    gated = yvals * jax.nn.silu(gate.astype(jnp.float32))
    local_sq = jnp.sum(gated * gated, axis=1)
    group_mark = (jnp.arange(GROUPS) == my_group).astype(jnp.float32)
    every_sum = lax.psum(local_sq[:, None] * group_mark[None, :], "tensor")
    group_mean = jnp.sum(every_sum * group_mark[None, :], axis=1) / (INNER // GROUPS)
    normed = (gated * lax.rsqrt(group_mean + 1e-05)[:, None] * norm_gain[None, :]).astype(
        jnp.bfloat16
    )
    w_full = lax.all_gather(w_out, "seq", axis=1, tiled=True)
    return lax.psum_scatter(
        jnp.dot(normed, w_full, preferred_element_type=jnp.float32).astype(jnp.bfloat16),
        "tensor",
        scatter_dimension=0,
        tiled=True,
    )


def enter(peers):
    barrier = pltpu.get_barrier_semaphore()
    for peer in peers:
        pl.semaphore_signal(barrier, inc=1, device_id=peer, device_id_type=pl.DeviceIdType.MESH)
    pl.semaphore_wait(barrier, len(peers))


def remote(src, dst, send, recv, peer):
    return pltpu.make_async_remote_copy(
        src_ref=src,
        dst_ref=dst,
        send_sem=send,
        recv_sem=recv,
        device_id=peer,
        device_id_type=pl.DeviceIdType.MESH,
    )


SEQS, CHIPS, OWN, SPAN, WIDE, HALF = 4, 4, 32, 256, 256, 128
LOG2E = 1.4426950408889634


def silu(v):
    return v / (1.0 + jnp.exp(-v))


class Sums:
    def __init__(self, bufs, sems, s, z, c):
        self.sa, self.sb, self.ra, self.rb, self.qa, self.qb, self.pa, self.pb, self.k0, self.k1, self.k2 = bufs
        self.sems = sems
        self.x, self.y = (s ^ 1, 2 * z + c), (s ^ 2, 2 * z + c)

    def copies(self, u):
        send, recv = self.sems
        return (
            remote(self.sa.at[u], self.ra.at[u], send.at[u, 0], recv.at[u, 0], self.x),
            remote(self.sb.at[u], self.rb.at[u], send.at[u, 1], recv.at[u, 1], self.y),
            remote(self.qa.at[u], self.pa.at[u], send.at[u, 2], recv.at[u, 2], self.y),
            remote(self.qb.at[u], self.pb.at[u], send.at[u, 3], recv.at[u, 3], self.x),
        )

    def emit(self, u, get):
        first, second, _, _ = self.copies(u)
        far = get(3)
        self.sa[u, 1] = far[:, :HALF].astype(jnp.bfloat16)
        self.sb[u, 1] = far[:, HALF:].astype(jnp.bfloat16)
        near = get(1)
        self.sa[u, 0] = near[:, :HALF].astype(jnp.bfloat16)
        first.start()
        self.k1[u] = near[:, HALF:]
        near = get(2)
        self.sb[u, 0] = near[:, HALF:].astype(jnp.bfloat16)
        second.start()
        self.k2[u] = near[:, :HALF]
        self.k0[u] = get(0)

    def relay(self, u):
        first, second, third, fourth = self.copies(u)
        first.wait_recv()
        self.qa[u] = (self.k2[u] + self.ra[u, 1].astype(jnp.float32)).astype(jnp.bfloat16)
        third.start()
        second.wait_recv()
        self.qb[u] = (self.k1[u] + self.rb[u, 1].astype(jnp.float32)).astype(jnp.bfloat16)
        fourth.start()

    def final(self, u):
        _, _, third, fourth = self.copies(u)
        third.wait_recv()
        fourth.wait_recv()
        own = self.k0[u]
        left = own[:, :HALF] + self.ra[u, 0].astype(jnp.float32) + self.pa[u].astype(jnp.float32)
        right = own[:, HALF:] + self.rb[u, 0].astype(jnp.float32) + self.pb[u].astype(jnp.float32)
        return jnp.concatenate([left, right], axis=1).astype(jnp.bfloat16)

    def drain(self, u):
        for copy in self.copies(u):
            copy.wait_send()


def mix_kernel(
    tok_hbm, wg_hbm, wx_hbm, wb_hbm, wdt_hbm, cx_hbm, cxb_hbm, cb_hbm, cbb_hbm, gain_hbm, wo_hbm,
    bias_hbm, rate_hbm, skip_hbm, len_hbm, out_ref,
    wg, wx, wb, wdt, cx, cxb, cb, cbb, gain, wo, bias_s, rate_s, skip_s, len_s,
    tok, rel, xs, xc, gs, bs, halo, bct, bca, bcp, dtp, dts, dtg, dtv,
    held, normed, part, sib, pair, got, done,
    *rest,
):
    big, rest = rest[:11], rest[11:]
    few, rest = rest[:11], rest[11:]
    rim, rest = rest[:11], rest[11:]
    three, rest = rest[:11], rest[11:]
    (
        w_sem, t_send, t_recv, zu_send, zd_send, z_recv, f_send, f_recv,
        g_send, g_recv, v_send, v_recv, b_send, b_recv, h_send, h_recv, d_send, d_recv,
        e_send, e_recv, a_send, a_recv,
        y_send, y_recv, p_send, p_recv, r_send, r_recv, o_send, o_recv,
    ) = rest
    s, t = lax.axis_index("seq"), lax.axis_index("tensor")
    tens = 2 * CHIPS
    z, c = t // 2, t % 2
    sibling = (s, 2 * z + 1 - c)
    depth = wx.shape[0]
    own_cols = pl.ds(pl.multiple_of(s * depth, depth), depth)
    loads = [
        pltpu.make_async_copy(src, dst, w_sem.at[i])
        for i, (src, dst) in enumerate((
            (len_hbm, len_s), (tok_hbm.at[:, own_cols], tok.at[z, c, s]), (wb_hbm, wb), (wx_hbm, wx),
            (wdt_hbm, wdt), (wg_hbm, wg), (cb_hbm, cb), (cbb_hbm, cbb), (cx_hbm, cx), (cxb_hbm, cxb),
            (bias_hbm, bias_s), (rate_hbm, rate_s), (skip_hbm, skip_s), (gain_hbm, gain), (wo_hbm, wo),
        ))
    ]
    for load in loads:
        load.start()
    along = [(s ^ r, t) for r in range(1, SEQS)]
    across = [(s, lax.rem(t + d, tens)) for d in range(1, tens)]
    enter(along + across)

    spread = [
        remote(
            tok_hbm.at[:, pl.ds(pl.multiple_of(peer[0] * depth, depth), depth)],
            tok.at[z, c, s], t_send.at[i], t_recv.at[i], peer,
        )
        for i, peer in enumerate(along)
    ]
    for copy in spread[::-1]:
        copy.start()
    loads[0].wait()

    total = SEQS * SPAN
    pos = lax.broadcasted_iota(jnp.int32, (total, HALF), 0)
    begin, start = jnp.zeros((total, HALF), jnp.int32), jnp.int32(0)
    for r in range(len_s.shape[0]):
        begin = jnp.where(pos >= start, start, begin)
        start = start + len_s[r]
    rel[...] = pos - begin

    first = z - 1 + 2 * ((3 - z) // 3)
    last = 3 * (1 - z // 2)
    order = [z, first, 6 - z - first - last, last]

    inner_chip = (z > 0) & (z < CHIPS - 1)

    def hops(zb, r):
        part = tok.at[zb, c, s ^ r]
        up = remote(part, part, zu_send.at[zb, r], z_recv.at[zb, r], (s, 2 * lax.rem(z + 1, CHIPS) + c))
        down = remote(
            part, part, zd_send.at[zb, r], z_recv.at[zb, r], (s, 2 * lax.rem(z + CHIPS - 1, CHIPS) + c)
        )
        over = remote(part, part, f_send.at[zb, r], f_recv.at[zb, r], sibling)
        return up, down, over, (z < CHIPS - 1) & (zb <= z), (z > 0) & (zb >= z)

    def arrive(i, pieces=range(1, SEQS)):
        for r in pieces:
            up, down, over, goes_up, goes_down = hops(order[i], r)
            if i:
                up.wait_recv()
            elif r:
                spread[r - 1].wait_recv()
            else:
                loads[1].wait()
            pl.when(goes_up)(up.start)
            pl.when(goes_down)(down.start)
            over.start()

    def arrive_if(which, i, pieces=range(SEQS)):
        if i < CHIPS:
            pl.when(which)(lambda: arrive(i, pieces))

    sums = Sums(big, (g_send, g_recv), s, z, c)
    sumg = Sums(three, (v_send, v_recv), s, z, c)
    sumb = Sums(few, (b_send, b_recv), s, z, c)
    sumh = Sums(rim, (h_send, h_recv), s, z, c)

    def product(rows, w):
        def get(r):
            cols = pl.ds(pl.multiple_of((s ^ r) * WIDE, WIDE), WIDE)
            return jnp.dot(rows, w[:, cols], preferred_element_type=jnp.float32)

        return get

    arrive(0, [0])
    arrive(1, [0])
    arrive_if(inner_chip, 2, [0])
    arrive(0)
    for i in range(CHIPS):
        if i:
            if i == 1:
                arrive(i)
            else:
                arrive_if(~inner_chip, i)
            arrive_if(inner_chip, i + 1, range(1 if i == 1 else 0, SEQS))
        for r in range(SEQS):
            hops(order[i], r)[2].wait_recv()
        rows = tok[order[i]].reshape(SPAN, depth)
        if i == 0:
            loads[2].wait()
        bcp[...] = jnp.dot(rows, wb[...], preferred_element_type=jnp.float32).reshape(2, SEQS, OWN, WIDE)
        sumb.emit(i, lambda r: bcp[:, s ^ r].reshape(2 * OWN, WIDE))

        @pl.when(order[i] == CHIPS - 1)
        def _():
            halo[...] = bcp[1, :, OWN - 16 :, :]

        if i == CHIPS - 1:
            sumh.emit(0, lambda r: halo[lax.rem((s ^ r) + SEQS - 1, SEQS)])
        if i == 0:
            loads[3].wait()
        sums.emit(i, product(rows, wx))
        if i == 0:
            loads[5].wait()
            sums.emit(CHIPS, product(rows, wg))
        if i:
            sumb.relay(i - 1)
            sums.relay(i - 1)
    sumb.relay(CHIPS - 1)
    sumh.relay(0)

    def span_rows(q):
        return tok[:, :, q].reshape(SPAN, depth)

    sums.relay(CHIPS)
    def other_rows(q):
        rows = [tok[zb, :, q].reshape(2 * OWN, depth) for zb in order[1:]]
        return jnp.concatenate(rows, axis=0)

    sumg.emit(0, product(other_rows(0), wg))
    bs[:16, :] = sumh.final(0).astype(jnp.float32)
    for i in range(CHIPS):
        bs[pl.ds(pl.multiple_of(16 + order[i] * 2 * OWN, 16), 2 * OWN), :] = sumb.final(i).astype(jnp.float32)

    for load in loads[4:5] + loads[6:]:
        load.wait()
    away = rel[pl.ds(pl.multiple_of(s * SPAN, SPAN), SPAN), :1]

    def conv(src, begin, w, bias, away):
        out = w[CONV - 1 :, :] * src[begin : begin + SPAN, :] + bias
        for back in range(1, CONV):
            tap = w[CONV - 1 - back : CONV - back, :] * src[begin - back : begin - back + SPAN, :]
            out = out + jnp.where(away >= back, tap, 0.0)
        return silu(out).astype(jnp.bfloat16)

    bcc = conv(bs, 16, cb[...], cbb[...], away)
    to = lax.broadcasted_iota(jnp.int32, (WIDE, WIDE), 0)
    frm = lax.broadcasted_iota(jnp.int32, (WIDE, WIDE), 1)
    pick = (frm == (to % 32) * GROUPS + to // 32).astype(jnp.float32).astype(jnp.bfloat16)
    bct[...] = (
        lax.dot_general(pick, bcc, (((1,), (1,)), ((), ())), preferred_element_type=jnp.float32)
        .astype(jnp.bfloat16)
        .reshape(GROUPS, 32, SPAN)
    )
    swaps = [
        remote(bct.at[peer[1]], bca.at[s, t], e_send.at[i], e_recv.at[i], peer)
        for i, peer in enumerate(across)
    ]
    for copy in swaps:
        copy.start()
    bca[s, t] = bct[t]
    sums.relay(CHIPS - 1)
    heads = 4
    for q in range(SEQS):
        some = lax.dot_general(
            wdt[...], span_rows(q), (((1,), (1,)), ((), ())), preferred_element_type=jnp.float32
        )
        for d in range(SEQS):
            dtp[d, heads * q : heads * (q + 1), :] = some[heads * d : heads * (d + 1), :]
    dts[...] = dtp[...].astype(jnp.bfloat16)
    steps = [
        remote(dts.at[peer[0]], dtg.at[i], d_send.at[i], d_recv.at[i], peer) for i, peer in enumerate(along)
    ]
    for copy in steps:
        copy.start()
    sumg.emit(1, product(other_rows(1), wg))
    for copy in swaps:
        copy.wait_recv()
    groups = [
        remote(bca.at[s], bca.at[s], a_send.at[i], a_recv.at[i], peer)
        for i, peer in enumerate(along)
    ]
    for copy in groups:
        copy.start()
    sumg.relay(0)
    for i in range(CHIPS):
        full = sums.final(i).astype(jnp.float32).reshape(2, SEQS, OWN, WIDE)
        for half in range(2):
            for q in range(SEQS):
                at = 16 + q * SPAN + half * OWN + order[i] * 2 * OWN
                xs[pl.ds(pl.multiple_of(at, 16), OWN), :] = full[half, q]
    sumg.emit(2, product(other_rows(2), wg))
    full = sums.final(CHIPS).astype(jnp.float32).reshape(2, SEQS, OWN, WIDE)
    for half in range(2):
        for q in range(SEQS):
            gs[q, pl.ds(pl.multiple_of(z * 2 * OWN + half * OWN, 16), OWN), :] = full[half, q]
    xs[:16, :] = jnp.zeros((16, WIDE), jnp.float32)
    mine = pl.ds(pl.multiple_of(s * WIDE, WIDE), WIDE)
    for q in range(SEQS):
        xc[q * SPAN : (q + 1) * SPAN, :] = conv(
            xs, 16 + q * SPAN, cx[:, mine], cxb[:, mine], rel[q * SPAN : (q + 1) * SPAN, :1]
        ).astype(jnp.float32)
    sumg.relay(1)
    sumg.emit(3, product(other_rows(3), wg))
    for copy in steps:
        copy.wait_recv()
    small = dts[s].astype(jnp.float32)
    for i in range(SEQS - 1):
        small = small + dtg[i].astype(jnp.float32)
    line = to[: heads * SEQS, :] % heads
    bias, rate = jnp.zeros(line.shape, jnp.float32), jnp.zeros(line.shape, jnp.float32)
    for h in range(heads):
        bias = jnp.where(line == h, bias_s[heads * s + h], bias)
        rate = jnp.where(line == h, -LOG2E * rate_s[heads * s + h], rate)
    small = small.astype(jnp.bfloat16).astype(jnp.float32) + bias
    small = jnp.maximum(small, 0.0) + jnp.log1p(jnp.exp(-jnp.abs(small)))
    for q in range(SEQS):
        dtv[q, :heads, :] = small[heads * q : heads * (q + 1), :]
        dtv[q, heads:, :] = (small * rate)[heads * q : heads * (q + 1), :]

    dif = to - frm
    upto = (dif <= 0).astype(jnp.float32)
    lane = frm // HDIM
    skip = jnp.zeros((1, WIDE), jnp.float32)
    for h in range(heads):
        skip = jnp.where(lane[:1] == h, skip_s[heads * s + h], skip)

    cols_out = wo.shape[1]
    few_rows = OWN // 2
    gathers = [
        [
            remote(held.at[s, k], held.at[s, k], y_send.at[k, i], y_recv.at[k, i], peer)
            for i, peer in enumerate(along)
        ]
        for k in range(2 * SEQS)
    ]
    pairs = [
        remote(part.at[k, 1 - c], sib.at[k], p_send.at[k], p_recv.at[k], sibling)
        for k in range(2 * SEQS)
    ]

    def reduces(k):
        peers = [lax.rem(z + d, CHIPS) for d in range(1, CHIPS)]
        return [
            remote(pair.at[k, to], got.at[k, i], r_send.at[k, i], r_recv.at[k, i], (s, 2 * to + c))
            for i, to in enumerate(peers)
        ]

    def place(frm, half):
        cols = pl.ds(pl.multiple_of(frm * cols_out, cols_out), cols_out)
        return out_ref.at[half * few_rows : (half + 1) * few_rows, cols]

    def deliver(k, frm):
        return remote(done.at[k], place(frm, k % 2), o_send.at[k], o_recv.at[frm, k % 2], (k // 2, t))

    def keep(k):
        return pltpu.make_async_copy(done.at[k], place(s, k % 2), o_send.at[k])

    def project(k):
        for copy in gathers[k]:
            copy.wait_recv()
        squares = jnp.zeros((SPAN // 2, HALF), jnp.float32)
        for n in range(2 * SEQS):
            piece = held[n // 2, k, n % 2].astype(jnp.float32)
            squares = squares + piece * piece
        scale = lax.rsqrt(jnp.sum(squares, axis=1, keepdims=True) / (SEQS * WIDE) + 1e-05)
        for n in range(2 * SEQS):
            wide = slice(n * HALF, (n + 1) * HALF)
            piece = held[n // 2, k, n % 2].astype(jnp.float32)
            normed[:, wide] = (piece * scale * gain[:, wide]).astype(jnp.bfloat16)
        for n in range(cols_out // WIDE):
            wide = slice(n * WIDE, (n + 1) * WIDE)
            acc = jnp.dot(normed[...], wo[:, wide], preferred_element_type=jnp.float32)
            acc = acc.reshape(CHIPS, 2, few_rows, WIDE).astype(jnp.bfloat16)
            for half in range(2):
                part[k, half, :, :, wide] = acc[:, half]
        pairs[k].start()

    def combine(k):
        pairs[k].wait_recv()
        pair[k] = (part[k, c].astype(jnp.float32) + sib[k].astype(jnp.float32)).astype(jnp.bfloat16)
        for copy in reduces(k):
            copy.start()

    def collect(k):
        for copy in reduces(k):
            copy.wait_recv()
        total = pair[k, z].astype(jnp.float32)
        for i in range(CHIPS - 1):
            total = total + got[k, i].astype(jnp.float32)
        done[k] = total.astype(jnp.bfloat16)
        pl.when(s != k // 2)(deliver(k, s).start)
        pl.when(s == k // 2)(keep(k).start)

    def settle(first, end):
        for k in range(first, end):
            for copy in gathers[k] + [pairs[k]] + reduces(k):
                copy.wait_send()
            pl.when(s != k // 2)(deliver(k, s).wait_send)
            pl.when(s == k // 2)(keep(k).wait)

    def advance(k):
        project(k)
        combine(k)
        if k > 1:
            collect(k - 2)

    state = jnp.zeros((STATE, WIDE), jnp.float32)
    local = to[:, :1]
    for q in range(SEQS):
        here = slice(q * SPAN, (q + 1) * SPAN)
        away = rel[here, :1]
        for i, copy in enumerate(groups):
            pl.when((s ^ (i + 1)) == q)(copy.wait_recv)
        bt = bca[q, :4].reshape(STATE, SPAN)
        cn = bca[q, 4:].reshape(STATE, SPAN).astype(jnp.float32).T.astype(jnp.bfloat16)
        scores = jnp.dot(cn, bt, preferred_element_type=jnp.float32)
        scores = jnp.where((dif >= 0) & (dif <= away), scores, 0.0)
        both = dtv[q]
        cum = jnp.dot(both, upto, precision=HIGH, preferred_element_type=jnp.float32)
        both = jnp.where(to[:8, :] < heads, both, cum)
        cols = jnp.concatenate([both, jnp.zeros((HALF - 8, SPAN), jnp.float32)], axis=0).T

        def expand(first):
            out = jnp.broadcast_to(cols[:, first : first + 1], (SPAN, WIDE))
            for h in range(1, heads):
                out = jnp.where(lane == h, cols[:, first + h : first + h + 1], out)
            return out

        dte, cume = expand(0), expand(heads)
        xv = xc[here, :]
        xdt = xv * dte
        inner = jnp.zeros((SPAN, WIDE), jnp.float32)
        for h in range(heads):
            gap = cols[:, heads + h : heads + h + 1] - both[heads + h : heads + h + 1, :]
            mixing = (jnp.exp2(jnp.minimum(gap, 0.0)) * scores).astype(jnp.bfloat16)
            inner = inner + jnp.dot(
                mixing, jnp.where(lane == h, xdt, 0.0).astype(jnp.bfloat16),
                preferred_element_type=jnp.float32,
            )
        carry = jnp.where(away > local, jnp.exp2(cume), 0.0)
        ends = cume[SPAN - 1 :, :]
        tail = jnp.where(local >= SPAN - 1 - away[SPAN - 1 :, :], jnp.exp2(ends - cume), 0.0)
        fresh = jnp.dot(bt, (tail * xdt).astype(jnp.bfloat16), preferred_element_type=jnp.float32)
        outer = jnp.dot(cn, state.astype(jnp.bfloat16), preferred_element_type=jnp.float32)
        state = carry[SPAN - 1 :, :] * state + fresh
        y = inner + outer * carry + skip * xv
        if q == 0:
            sumg.relay(2)
        some = sumg.final(q).astype(jnp.float32)
        for i in range(1, CHIPS):
            to_rows = pl.ds(pl.multiple_of(order[i] * 2 * OWN, 16), 2 * OWN)
            gs[q, to_rows, :] = some[(i - 1) * 2 * OWN : i * 2 * OWN]
        gate = gs[q]
        gated = (y * silu(gate)).reshape(2 * CHIPS, 2, few_rows, WIDE)
        for half in range(2):
            k = 2 * q + half
            some = gated[:, half].reshape(SPAN // 2, WIDE).astype(jnp.bfloat16)
            held[s, k, 0], held[s, k, 1] = some[:, :HALF], some[:, HALF:]
            for copy in gathers[k]:
                copy.start()
        if q == 0:
            sumg.relay(3)
        for k in range(2 * q - 4, 2 * q - 2):
            if k >= 0:
                advance(k)
    last_k = 2 * SEQS - 1
    for zb in range(CHIPS):
        for r in range(SEQS):
            up, down, over, goes_up, goes_down = hops(zb, r)
            pl.when(goes_up)(up.wait_send)
            pl.when(goes_down)(down.wait_send)
            over.wait_send()
    for copy in spread + steps + swaps + groups:
        copy.wait_send()
    for u in range(5):
        sums.drain(u)
    for u in range(4):
        sumg.drain(u)
    for u in range(4):
        sumb.drain(u)
    sumh.drain(0)
    for k in range(last_k - 3, last_k + 1):
        advance(k)
    settle(0, last_k - 2)
    collect(last_k - 1)
    collect(last_k)
    for q in range(SEQS):
        for half in range(2):
            pl.when(s != q)(deliver(half, q).wait_recv)

    settle(last_k - 2, last_k + 1)


def mix(operands, own, seqs):
    tokens, w_gate, w_xin, w_bc, w_dt, conv_x, conv_xb, conv_b, conv_bb, gain, w_out = operands[:11]
    depth = w_xin.shape[0]
    total = SEQS * SPAN
    cols = w_out.shape[1]
    dma = pltpu.SemaphoreType.DMA
    bf, f32 = jnp.bfloat16, jnp.float32

    def sums(n, rows):
        pair = pltpu.VMEM((n, 2, rows, HALF), bf)
        one = pltpu.VMEM((n, rows, HALF), bf)
        return [pair] * 4 + [one] * 4 + [pltpu.VMEM((n, rows, WIDE), f32)] + [pltpu.VMEM((n, rows, HALF), f32)] * 2

    return pl.pallas_call(
        mix_kernel,
        out_shape=jax.ShapeDtypeStruct((own, cols * seqs), bf),
        in_specs=[pl.BlockSpec(memory_space=pl.ANY)] * len(operands),
        out_specs=pl.BlockSpec(memory_space=pl.ANY),
        scratch_shapes=[pltpu.VMEM(a.shape, a.dtype) for a in operands[1:11]]
        + [pltpu.SMEM(a.shape, a.dtype) for a in operands[11:]]
        + [
            pltpu.VMEM((CHIPS, 2, SEQS, OWN, depth), bf),
            pltpu.VMEM((total, HALF), jnp.int32),
            pltpu.VMEM((16 + total, WIDE), f32),
            pltpu.VMEM((total, WIDE), f32),
            pltpu.VMEM((SEQS, SPAN, WIDE), f32),
            pltpu.VMEM((16 + SPAN, WIDE), f32),
            pltpu.VMEM((SEQS, 16, WIDE), f32),
            pltpu.VMEM((GROUPS, 32, SPAN), bf),
            pltpu.VMEM((SEQS, GROUPS, 32, SPAN), bf),
            pltpu.VMEM((2, SEQS, OWN, WIDE), f32),
            pltpu.VMEM((SEQS, 16, SPAN), f32),
            pltpu.VMEM((SEQS, 16, SPAN), bf),
            pltpu.VMEM((3, 16, SPAN), bf),
            pltpu.VMEM((SEQS, 8, SPAN), f32),
            pltpu.VMEM((SEQS, 2 * SEQS, 2, SPAN // 2, HALF), bf),
            pltpu.VMEM((SPAN // 2, SEQS * WIDE), bf),
            pltpu.VMEM((2 * SEQS, 2, CHIPS, OWN // 2, cols), bf),
            pltpu.VMEM((2 * SEQS, CHIPS, OWN // 2, cols), bf),
            pltpu.VMEM((2 * SEQS, CHIPS, OWN // 2, cols), bf),
            pltpu.VMEM((2 * SEQS, CHIPS - 1, OWN // 2, cols), bf),
            pltpu.VMEM((2 * SEQS, OWN // 2, cols), bf),
        ]
        + sums(CHIPS + 1, SPAN)
        + sums(CHIPS, 2 * OWN)
        + sums(1, 16)
        + sums(SEQS, SPAN - 2 * OWN)
        + [
            dma((15,)), dma((3,)), dma((3,)), dma((4, 4)), dma((4, 4)), dma((4, 4)), dma((4, 4)), dma((4, 4)),
            dma((5, 4)), dma((5, 4)), dma((4, 4)), dma((4, 4)), dma((4, 4)), dma((4, 4)),
            dma((1, 4)), dma((1, 4)), dma((3,)), dma((3,)), dma((7,)), dma((7,)), dma((3,)), dma((3,)),
            dma((8, 3)), dma((8, 3)), dma((8,)), dma((8,)), dma((8, 3)), dma((8, 3)), dma((8,)), dma((4, 2)),
        ],
        compiler_params=pltpu.CompilerParams(
            collective_id=2, has_side_effects=True, vmem_limit_bytes=56 * 2**20
        ),
    )(*operands)


def shards(
    tokens,
    w_gate,
    w_xin,
    w_bc,
    w_dt,
    conv_x,
    conv_x_bias,
    conv_bc,
    conv_bc_bias,
    dt_bias,
    decay_rate,
    d_skip,
    norm_gain,
    w_out,
    lengths,
):
    operands = (
        tokens, w_gate, w_xin, w_bc, w_dt.T, conv_x, conv_x_bias[None, :], conv_bc, conv_bc_bias[None, :],
        norm_gain[None, :], w_out, dt_bias, decay_rate, d_skip, lengths,
    )
    return mix(operands, tokens.shape[0], lax.axis_size("seq"))


def solution(mesh):
    seqs, tens = mesh.shape["seq"], mesh.shape["tensor"]
    narrow = seqs == SEQS and tens == GROUPS == 2 * CHIPS
    body = shards if narrow else shards_wide
    in_specs = (
        P(("seq", "tensor"), None),
        P("seq", "tensor"),
        P("seq", "tensor"),
        P("seq", "tensor"),
        P("seq", "tensor"),
        P(None, "tensor"),
        P("tensor"),
        P(None, "tensor"),
        P("tensor"),
        P("tensor"),
        P("tensor"),
        P("tensor"),
        P("tensor"),
        P("tensor", "seq"),
        P(),
    )
    out_specs = P(("seq", "tensor"), None)
    return jax.shard_map(body, mesh=mesh, in_specs=in_specs, out_specs=out_specs, check_vma=False)
```

```python
import jax
import jax.numpy as jnp
import numpy as np
from jax import lax
from jax.experimental import pallas as pl
from jax.experimental.pallas import tpu as pltpu
from jax.sharding import PartitionSpec as P

HDIM = 64
GROUPS = 8
STATE = 128
CONV = 4
STRETCH = 256
INNER = 8192


HIGH = lax.Precision.HIGHEST


def from_behind(x, axis, by):
    count = lax.axis_size(axis)
    pairs = [(i, i + by) for i in range(count) if 0 <= i + by < count]
    return lax.ppermute(x, axis, pairs)


def carried_in(x, axis, combine, identity):
    count, here = (lax.axis_size(axis), lax.axis_index(axis))
    everything = jax.tree.map(
        lambda part, kind: lax.all_gather(part.astype(kind), axis), x, (jnp.bfloat16, jnp.bfloat16)
    )
    start = jax.tree.map(
        lambda part, zero: jnp.broadcast_to(jnp.asarray(zero, part.dtype), part.shape), x, identity
    )

    def hop(k, before):
        reached = k < here
        new = combine(
            before, jax.tree.map(lambda part, own: part[k].astype(own.dtype), everything, x)
        )
        return jax.tree.map(lambda a, b: jnp.where(reached, a, b), new, before)

    return lax.fori_loop(0, count, hop, start)


def doc_ids(lengths, positions):
    starts = jnp.cumsum(lengths) - lengths
    counted = jnp.sum((starts[None, :] <= positions[:, None]).astype(jnp.int32), axis=1)
    return counted - 1


def causal_conv(values, edge, weights, bias, docs, edge_docs):
    count = values.shape[0]
    extended = jnp.concatenate([edge, values], axis=0).astype(jnp.float32)
    all_docs = jnp.concatenate([edge_docs, docs])
    summed = jnp.zeros(values.shape, jnp.float32) + bias[None, :]
    for offset in range(weights.shape[0]):
        same = (all_docs[offset : offset + count] == docs).astype(jnp.float32)
        summed = (
            summed + weights[offset][None, :] * extended[offset : offset + count] * same[:, None]
        )
    return lax.optimization_barrier(jax.nn.silu(summed).astype(jnp.bfloat16))


def ssd_blocks(xvals, dtv, rate, bmat, cmat, docs, prev_doc, head_group, block):
    count, heads, hdim = xvals.shape
    nstate = bmat.shape[2]
    blocks = count // block
    logs = -dtv * rate[None, :]

    def split(array):
        return array.reshape((blocks, block) + array.shape[1:])

    lower = jnp.tril(jnp.ones((block, block), bool))

    def step(carry, pieces):
        state, last_doc = carry
        xblk, dblk, lblk, bblk, cblk, docblk = pieces
        cum = jnp.cumsum(lblk, axis=0)
        same = (docblk[:, None] == docblk[None, :]) & lower
        diff = cum.T[:, :, None] - cum.T[:, None, :]
        decay = jnp.exp(jnp.where(same[None], diff, -jnp.inf))
        scores = jnp.einsum("ign,jgn->gij", cblk, bblk, precision=HIGH)
        mixing = scores[head_group] * decay * dblk.T[:, None, :]
        inner = jnp.einsum("hij,jhp->ihp", mixing, xblk, precision=HIGH)
        open_in = (docblk == last_doc).astype(jnp.float32)
        carry_in = jnp.exp(cum) * open_in[:, None]
        chead = cblk[:, head_group, :]
        outer = jnp.einsum("ihn,hpn->ihp", chead, state, precision=HIGH) * carry_in[:, :, None]
        end_doc = docblk[-1]
        tail = (
            jnp.exp(cum[-1][None, :] - cum)
            * (docblk == end_doc).astype(jnp.float32)[:, None]
            * dblk
        )
        bhead = bblk[:, head_group, :]
        fresh = jnp.einsum("jh,jhp,jhn->hpn", tail, xblk, bhead, precision=HIGH)
        state = carry_in[-1][:, None, None] * state + fresh
        return ((state, end_doc), inner + outer)

    init = (jnp.zeros((heads, hdim, nstate), jnp.float32), prev_doc)
    (state, end_doc), outs = lax.scan(
        step, init, (split(xvals), split(dtv), split(logs), split(bmat), split(cmat), split(docs))
    )
    return (outs.reshape(count, heads, hdim), state)


def shards_wide(
    tokens,
    w_gate,
    w_xin,
    w_bc,
    w_dt,
    conv_x,
    conv_x_bias,
    conv_bc,
    conv_bc_bias,
    dt_bias,
    decay_rate,
    d_skip,
    norm_gain,
    w_out,
    lengths,
):
    tensor_count = lax.axis_size("tensor")
    seq_index = lax.axis_index("seq")
    tensor_index = lax.axis_index("tensor")
    span_rows = lax.all_gather(tokens, "tensor", axis=0, tiled=True)
    span_len = span_rows.shape[0]
    pieces = (
        lax.all_gather(w_gate, "seq", axis=0, tiled=True),
        lax.all_gather(w_xin, "seq", axis=0, tiled=True),
        lax.all_gather(w_bc, "seq", axis=0, tiled=True),
        lax.all_gather(w_dt, "seq", axis=0, tiled=True),
    )
    gate_acc, xin_acc, bc_acc, dt_acc = tuple(
        (
            jnp.dot(span_rows, weight_piece, preferred_element_type=jnp.float32)
            for weight_piece in pieces
        )
    )
    gate = gate_acc.astype(jnp.bfloat16)
    xin = xin_acc.astype(jnp.bfloat16)
    bcin = bc_acc.astype(jnp.bfloat16)
    dtin = dt_acc.astype(jnp.bfloat16)
    gate, xin, bcin, dtin = lax.optimization_barrier((gate, xin, bcin, dtin))
    positions = seq_index * span_len + jnp.arange(span_len, dtype=jnp.int32)
    docs = doc_ids(lengths, positions)
    edge_docs = doc_ids(lengths, seq_index * span_len + jnp.arange(-(CONV - 1), 0, dtype=jnp.int32))
    prev_span_doc = doc_ids(lengths, positions[:1] - 1)[0]
    edge_x, edge_bc = from_behind(
        (xin[span_len - (CONV - 1) :], bcin[span_len - (CONV - 1) :]), "seq", 1
    )
    x_conv = causal_conv(xin, edge_x, conv_x, conv_x_bias, docs, edge_docs)
    bc_conv = causal_conv(bcin, edge_bc, conv_bc, conv_bc_bias, docs, edge_docs)
    group_span = tensor_count // GROUPS
    my_group = tensor_index // group_span
    every_group = lax.all_gather(bc_conv, "tensor", axis=1, tiled=True)
    arranged = every_group.reshape(span_len, 2 * STATE, GROUPS)
    group_cols = lax.dynamic_slice_in_dim(arranged, my_group, 1, 2).reshape(span_len, 2 * STATE)
    head_dev = w_dt.shape[1]
    head_group = np.zeros(head_dev, dtype=np.int32)
    both = group_cols.astype(jnp.float32)
    bmat = both[:, None, :STATE]
    cmat = both[:, None, STATE:]
    xvals = x_conv.astype(jnp.float32).reshape(span_len, head_dev, HDIM)
    dtv = jax.nn.softplus(dtin.astype(jnp.float32) + dt_bias[None, :])
    block = min(STRETCH, span_len)
    y_local, end_state = ssd_blocks(
        xvals, dtv, decay_rate, bmat, cmat, docs, prev_span_doc, head_group, block
    )
    cum_span = jnp.cumsum(-dtv * decay_rate[None, :], axis=0)
    open_span = (docs == prev_span_doc).astype(jnp.float32)
    span_decay = jnp.exp(cum_span[-1]) * open_span[-1]

    def combine(earlier, later):
        return (earlier[0] * later[0], later[0][:, None, None] * earlier[1] + later[1])

    entering = carried_in(
        (span_decay, end_state),
        "seq",
        combine,
        (jnp.ones_like(span_decay), jnp.zeros_like(end_state)),
    )[1]
    carried = jnp.exp(cum_span) * open_span[:, None]
    y_enter = (
        jnp.einsum("ihn,hpn->ihp", cmat[:, head_group, :], entering, precision=HIGH)
        * carried[:, :, None]
    )
    yvals = (y_local + y_enter + d_skip[None, :, None] * xvals).reshape(span_len, head_dev * HDIM)
    gated = yvals * jax.nn.silu(gate.astype(jnp.float32))
    local_sq = jnp.sum(gated * gated, axis=1)
    group_mark = (jnp.arange(GROUPS) == my_group).astype(jnp.float32)
    every_sum = lax.psum(local_sq[:, None] * group_mark[None, :], "tensor")
    group_mean = jnp.sum(every_sum * group_mark[None, :], axis=1) / (INNER // GROUPS)
    normed = (gated * lax.rsqrt(group_mean + 1e-05)[:, None] * norm_gain[None, :]).astype(
        jnp.bfloat16
    )
    w_full = lax.all_gather(w_out, "seq", axis=1, tiled=True)
    return lax.psum_scatter(
        jnp.dot(normed, w_full, preferred_element_type=jnp.float32).astype(jnp.bfloat16),
        "tensor",
        scatter_dimension=0,
        tiled=True,
    )


def enter(peers):
    barrier = pltpu.get_barrier_semaphore()
    for peer in peers:
        pl.semaphore_signal(barrier, inc=1, device_id=peer, device_id_type=pl.DeviceIdType.MESH)
    pl.semaphore_wait(barrier, len(peers))


def remote(src, dst, send, recv, peer):
    return pltpu.make_async_remote_copy(
        src_ref=src,
        dst_ref=dst,
        send_sem=send,
        recv_sem=recv,
        device_id=peer,
        device_id_type=pl.DeviceIdType.MESH,
    )


SEQS, CHIPS, OWN, SPAN, WIDE, HALF = 4, 4, 32, 256, 256, 128
LOG2E = 1.4426950408889634


def silu(v):
    return v / (1.0 + jnp.exp(-v))


class Sums:
    def __init__(self, bufs, sems, s, z, c):
        self.sa, self.sb, self.ra, self.rb, self.qa, self.qb, self.pa, self.pb, self.k0, self.k1, self.k2 = bufs
        self.sems = sems
        self.x, self.y = (s ^ 1, 2 * z + c), (s ^ 2, 2 * z + c)

    def copies(self, u):
        send, recv = self.sems
        return (
            remote(self.sa.at[u], self.ra.at[u], send.at[u, 0], recv.at[u, 0], self.x),
            remote(self.sb.at[u], self.rb.at[u], send.at[u, 1], recv.at[u, 1], self.y),
            remote(self.qa.at[u], self.pa.at[u], send.at[u, 2], recv.at[u, 2], self.y),
            remote(self.qb.at[u], self.pb.at[u], send.at[u, 3], recv.at[u, 3], self.x),
        )

    def emit(self, u, get):
        first, second, _, _ = self.copies(u)
        far = get(3)
        self.sa[u, 1] = far[:, :HALF].astype(jnp.bfloat16)
        self.sb[u, 1] = far[:, HALF:].astype(jnp.bfloat16)
        near = get(1)
        self.sa[u, 0] = near[:, :HALF].astype(jnp.bfloat16)
        first.start()
        self.k1[u] = near[:, HALF:]
        near = get(2)
        self.sb[u, 0] = near[:, HALF:].astype(jnp.bfloat16)
        second.start()
        self.k2[u] = near[:, :HALF]
        self.k0[u] = get(0)

    def relay(self, u):
        first, second, third, fourth = self.copies(u)
        first.wait_recv()
        self.qa[u] = (self.k2[u] + self.ra[u, 1].astype(jnp.float32)).astype(jnp.bfloat16)
        third.start()
        second.wait_recv()
        self.qb[u] = (self.k1[u] + self.rb[u, 1].astype(jnp.float32)).astype(jnp.bfloat16)
        fourth.start()

    def final(self, u):
        _, _, third, fourth = self.copies(u)
        third.wait_recv()
        fourth.wait_recv()
        own = self.k0[u]
        left = own[:, :HALF] + self.ra[u, 0].astype(jnp.float32) + self.pa[u].astype(jnp.float32)
        right = own[:, HALF:] + self.rb[u, 0].astype(jnp.float32) + self.pb[u].astype(jnp.float32)
        return jnp.concatenate([left, right], axis=1).astype(jnp.bfloat16)

    def drain(self, u):
        for copy in self.copies(u):
            copy.wait_send()


def mix_kernel(
    tok_hbm, wg_hbm, wx_hbm, wb_hbm, wdt_hbm, cx_hbm, cxb_hbm, cb_hbm, cbb_hbm, gain_hbm, wo_hbm,
    bias_hbm, rate_hbm, skip_hbm, len_hbm, out_ref,
    wg, wx, wb, wdt, cx, cxb, cb, cbb, gain, wo, bias_s, rate_s, skip_s, len_s,
    tok, rel, xs, xc, gs, bs, halo, bct, bca, bcp, dtp, dts, dtg, dtv,
    held, normed, part, sib, pair, got, done,
    *rest,
):
    big, rest = rest[:11], rest[11:]
    few, rest = rest[:11], rest[11:]
    rim, rest = rest[:11], rest[11:]
    three, rest = rest[:11], rest[11:]
    (
        w_sem, t_send, t_recv, zu_send, zd_send, z_recv, f_send, f_recv,
        g_send, g_recv, v_send, v_recv, b_send, b_recv, h_send, h_recv, d_send, d_recv,
        e_send, e_recv, a_send, a_recv,
        y_send, y_recv, p_send, p_recv, r_send, r_recv, o_send, o_recv,
    ) = rest
    s, t = lax.axis_index("seq"), lax.axis_index("tensor")
    tens = 2 * CHIPS
    z, c = t // 2, t % 2
    sibling = (s, 2 * z + 1 - c)
    depth = wx.shape[0]
    own_cols = pl.ds(pl.multiple_of(s * depth, depth), depth)
    loads = [
        pltpu.make_async_copy(src, dst, w_sem.at[i])
        for i, (src, dst) in enumerate((
            (len_hbm, len_s), (tok_hbm.at[:, own_cols], tok.at[z, c, s]), (wb_hbm, wb), (wx_hbm, wx),
            (wdt_hbm, wdt), (wg_hbm, wg), (cb_hbm, cb), (cbb_hbm, cbb), (cx_hbm, cx), (cxb_hbm, cxb),
            (bias_hbm, bias_s), (rate_hbm, rate_s), (skip_hbm, skip_s), (gain_hbm, gain), (wo_hbm, wo),
        ))
    ]
    for load in loads:
        load.start()
    along = [(s ^ r, t) for r in range(1, SEQS)]
    across = [(s, lax.rem(t + d, tens)) for d in range(1, tens)]
    enter(along + across)

    spread = [
        remote(
            tok_hbm.at[:, pl.ds(pl.multiple_of(peer[0] * depth, depth), depth)],
            tok.at[z, c, s], t_send.at[i], t_recv.at[i], peer,
        )
        for i, peer in enumerate(along)
    ]
    for copy in spread[::-1]:
        copy.start()
    loads[0].wait()

    total = SEQS * SPAN
    pos = lax.broadcasted_iota(jnp.int32, (total, HALF), 0)
    begin, start = jnp.zeros((total, HALF), jnp.int32), jnp.int32(0)
    for r in range(len_s.shape[0]):
        begin = jnp.where(pos >= start, start, begin)
        start = start + len_s[r]
    rel[...] = pos - begin

    first = z - 1 + 2 * ((3 - z) // 3)
    last = 3 * (1 - z // 2)
    order = [z, first, 6 - z - first - last, last]

    inner_chip = (z > 0) & (z < CHIPS - 1)

    def hops(zb, r):
        part = tok.at[zb, c, s ^ r]
        up = remote(part, part, zu_send.at[zb, r], z_recv.at[zb, r], (s, 2 * lax.rem(z + 1, CHIPS) + c))
        down = remote(
            part, part, zd_send.at[zb, r], z_recv.at[zb, r], (s, 2 * lax.rem(z + CHIPS - 1, CHIPS) + c)
        )
        over = remote(part, part, f_send.at[zb, r], f_recv.at[zb, r], sibling)
        return up, down, over, (z < CHIPS - 1) & (zb <= z), (z > 0) & (zb >= z)

    def arrive(i, pieces=range(1, SEQS)):
        for r in pieces:
            up, down, over, goes_up, goes_down = hops(order[i], r)
            if i:
                up.wait_recv()
            elif r:
                spread[r - 1].wait_recv()
            else:
                loads[1].wait()
            pl.when(goes_up)(up.start)
            pl.when(goes_down)(down.start)
            over.start()

    def arrive_if(which, i, pieces=range(SEQS)):
        if i < CHIPS:
            pl.when(which)(lambda: arrive(i, pieces))

    sums = Sums(big, (g_send, g_recv), s, z, c)
    sumg = Sums(three, (v_send, v_recv), s, z, c)
    sumb = Sums(few, (b_send, b_recv), s, z, c)
    sumh = Sums(rim, (h_send, h_recv), s, z, c)

    def product(rows, w):
        def get(r):
            cols = pl.ds(pl.multiple_of((s ^ r) * WIDE, WIDE), WIDE)
            return jnp.dot(rows, w[:, cols], preferred_element_type=jnp.float32)

        return get

    arrive(0, [0])
    arrive(1, [0])
    arrive_if(inner_chip, 2, [0])
    arrive(0)
    for i in range(CHIPS):
        if i:
            if i == 1:
                arrive(i)
            else:
                arrive_if(~inner_chip, i)
            arrive_if(inner_chip, i + 1, range(1 if i == 1 else 0, SEQS))
        for r in range(SEQS):
            hops(order[i], r)[2].wait_recv()
        rows = tok[order[i]].reshape(SPAN, depth)
        if i == 0:
            loads[2].wait()
        bcp[...] = jnp.dot(rows, wb[...], preferred_element_type=jnp.float32).reshape(2, SEQS, OWN, WIDE)
        sumb.emit(i, lambda r: bcp[:, s ^ r].reshape(2 * OWN, WIDE))

        @pl.when(order[i] == CHIPS - 1)
        def _():
            halo[...] = bcp[1, :, OWN - 16 :, :]

        if i == CHIPS - 1:
            sumh.emit(0, lambda r: halo[lax.rem((s ^ r) + SEQS - 1, SEQS)])
        if i == 0:
            loads[3].wait()
        sums.emit(i, product(rows, wx))
        if i == 0:
            loads[5].wait()
            sums.emit(CHIPS, product(rows, wg))
        if i:
            sumb.relay(i - 1)
            sums.relay(i - 1)
    sumb.relay(CHIPS - 1)
    sumh.relay(0)

    def span_rows(q):
        return tok[:, :, q].reshape(SPAN, depth)

    sums.relay(CHIPS)
    def other_rows(q):
        rows = [tok[zb, :, q].reshape(2 * OWN, depth) for zb in order[1:]]
        return jnp.concatenate(rows, axis=0)

    sumg.emit(0, product(other_rows(0), wg))
    sumg.emit(1, product(other_rows(1), wg))
    sums.relay(CHIPS - 1)
    bs[:16, :] = sumh.final(0).astype(jnp.float32)
    for i in range(CHIPS):
        bs[pl.ds(pl.multiple_of(16 + order[i] * 2 * OWN, 16), 2 * OWN), :] = sumb.final(i).astype(jnp.float32)

    for load in loads[4:5] + loads[6:]:
        load.wait()
    away = rel[pl.ds(pl.multiple_of(s * SPAN, SPAN), SPAN), :1]

    def conv(src, begin, w, bias, away):
        out = w[CONV - 1 :, :] * src[begin : begin + SPAN, :] + bias
        for back in range(1, CONV):
            tap = w[CONV - 1 - back : CONV - back, :] * src[begin - back : begin - back + SPAN, :]
            out = out + jnp.where(away >= back, tap, 0.0)
        return silu(out).astype(jnp.bfloat16)

    bcc = conv(bs, 16, cb[...], cbb[...], away)
    to = lax.broadcasted_iota(jnp.int32, (WIDE, WIDE), 0)
    frm = lax.broadcasted_iota(jnp.int32, (WIDE, WIDE), 1)
    pick = (frm == (to % 32) * GROUPS + to // 32).astype(jnp.float32).astype(jnp.bfloat16)
    bct[...] = (
        lax.dot_general(pick, bcc, (((1,), (1,)), ((), ())), preferred_element_type=jnp.float32)
        .astype(jnp.bfloat16)
        .reshape(GROUPS, 32, SPAN)
    )
    swaps = [
        remote(bct.at[peer[1]], bca.at[s, t], e_send.at[i], e_recv.at[i], peer)
        for i, peer in enumerate(across)
    ]
    for copy in swaps:
        copy.start()
    bca[s, t] = bct[t]
    heads = 4
    for q in range(SEQS):
        some = lax.dot_general(
            wdt[...], span_rows(q), (((1,), (1,)), ((), ())), preferred_element_type=jnp.float32
        )
        for d in range(SEQS):
            dtp[d, heads * q : heads * (q + 1), :] = some[heads * d : heads * (d + 1), :]
    dts[...] = dtp[...].astype(jnp.bfloat16)
    steps = [
        remote(dts.at[peer[0]], dtg.at[i], d_send.at[i], d_recv.at[i], peer) for i, peer in enumerate(along)
    ]
    for copy in steps:
        copy.start()
    for copy in swaps:
        copy.wait_recv()
    groups = [
        remote(bca.at[s], bca.at[s], a_send.at[i], a_recv.at[i], peer)
        for i, peer in enumerate(along)
    ]
    for copy in groups:
        copy.start()
    sumg.relay(0)
    for i in range(CHIPS):
        full = sums.final(i).astype(jnp.float32).reshape(2, SEQS, OWN, WIDE)
        for half in range(2):
            for q in range(SEQS):
                at = 16 + q * SPAN + half * OWN + order[i] * 2 * OWN
                xs[pl.ds(pl.multiple_of(at, 16), OWN), :] = full[half, q]
    sumg.emit(2, product(other_rows(2), wg))
    full = sums.final(CHIPS).astype(jnp.float32).reshape(2, SEQS, OWN, WIDE)
    for half in range(2):
        for q in range(SEQS):
            gs[q, pl.ds(pl.multiple_of(z * 2 * OWN + half * OWN, 16), OWN), :] = full[half, q]
    xs[:16, :] = jnp.zeros((16, WIDE), jnp.float32)
    mine = pl.ds(pl.multiple_of(s * WIDE, WIDE), WIDE)
    for q in range(SEQS):
        xc[q * SPAN : (q + 1) * SPAN, :] = conv(
            xs, 16 + q * SPAN, cx[:, mine], cxb[:, mine], rel[q * SPAN : (q + 1) * SPAN, :1]
        ).astype(jnp.float32)
    sumg.relay(1)
    sumg.emit(3, product(other_rows(3), wg))
    for copy in steps:
        copy.wait_recv()
    small = dts[s].astype(jnp.float32)
    for i in range(SEQS - 1):
        small = small + dtg[i].astype(jnp.float32)
    line = to[: heads * SEQS, :] % heads
    bias, rate = jnp.zeros(line.shape, jnp.float32), jnp.zeros(line.shape, jnp.float32)
    for h in range(heads):
        bias = jnp.where(line == h, bias_s[heads * s + h], bias)
        rate = jnp.where(line == h, -LOG2E * rate_s[heads * s + h], rate)
    small = small.astype(jnp.bfloat16).astype(jnp.float32) + bias
    small = jnp.maximum(small, 0.0) + jnp.log1p(jnp.exp(-jnp.abs(small)))
    for q in range(SEQS):
        dtv[q, :heads, :] = small[heads * q : heads * (q + 1), :]
        dtv[q, heads:, :] = (small * rate)[heads * q : heads * (q + 1), :]

    dif = to - frm
    upto = (dif <= 0).astype(jnp.float32)
    lane = frm // HDIM
    skip = jnp.zeros((1, WIDE), jnp.float32)
    for h in range(heads):
        skip = jnp.where(lane[:1] == h, skip_s[heads * s + h], skip)

    cols_out = wo.shape[1]
    few_rows = OWN // 2
    gathers = [
        [
            remote(held.at[s, k], held.at[s, k], y_send.at[k, i], y_recv.at[k, i], peer)
            for i, peer in enumerate(along)
        ]
        for k in range(2 * SEQS)
    ]
    pairs = [
        remote(part.at[k, 1 - c], sib.at[k], p_send.at[k], p_recv.at[k], sibling)
        for k in range(2 * SEQS)
    ]

    def reduces(k):
        peers = [lax.rem(z + d, CHIPS) for d in range(1, CHIPS)]
        return [
            remote(pair.at[k, to], got.at[k, i], r_send.at[k, i], r_recv.at[k, i], (s, 2 * to + c))
            for i, to in enumerate(peers)
        ]

    def place(frm, half):
        cols = pl.ds(pl.multiple_of(frm * cols_out, cols_out), cols_out)
        return out_ref.at[half * few_rows : (half + 1) * few_rows, cols]

    def deliver(k, frm):
        return remote(done.at[k], place(frm, k % 2), o_send.at[k], o_recv.at[frm, k % 2], (k // 2, t))

    def keep(k):
        return pltpu.make_async_copy(done.at[k], place(s, k % 2), o_send.at[k])

    def project(k):
        for copy in gathers[k]:
            copy.wait_recv()
        squares = jnp.zeros((SPAN // 2, HALF), jnp.float32)
        for n in range(2 * SEQS):
            piece = held[n // 2, k, n % 2].astype(jnp.float32)
            squares = squares + piece * piece
        scale = lax.rsqrt(jnp.sum(squares, axis=1, keepdims=True) / (SEQS * WIDE) + 1e-05)
        for n in range(2 * SEQS):
            wide = slice(n * HALF, (n + 1) * HALF)
            piece = held[n // 2, k, n % 2].astype(jnp.float32)
            normed[:, wide] = (piece * scale * gain[:, wide]).astype(jnp.bfloat16)
        for n in range(cols_out // WIDE):
            wide = slice(n * WIDE, (n + 1) * WIDE)
            acc = jnp.dot(normed[...], wo[:, wide], preferred_element_type=jnp.float32)
            acc = acc.reshape(CHIPS, 2, few_rows, WIDE).astype(jnp.bfloat16)
            for half in range(2):
                part[k, half, :, :, wide] = acc[:, half]
        pairs[k].start()

    def combine(k):
        pairs[k].wait_recv()
        pair[k] = (part[k, c].astype(jnp.float32) + sib[k].astype(jnp.float32)).astype(jnp.bfloat16)
        for copy in reduces(k):
            copy.start()

    def collect(k):
        for copy in reduces(k):
            copy.wait_recv()
        total = pair[k, z].astype(jnp.float32)
        for i in range(CHIPS - 1):
            total = total + got[k, i].astype(jnp.float32)
        done[k] = total.astype(jnp.bfloat16)
        pl.when(s != k // 2)(deliver(k, s).start)
        pl.when(s == k // 2)(keep(k).start)

    def settle(first, end):
        for k in range(first, end):
            for copy in gathers[k] + [pairs[k]] + reduces(k):
                copy.wait_send()
            pl.when(s != k // 2)(deliver(k, s).wait_send)
            pl.when(s == k // 2)(keep(k).wait)

    def advance(k):
        project(k)
        combine(k)
        if k > 1:
            collect(k - 2)

    state = jnp.zeros((STATE, WIDE), jnp.float32)
    local = to[:, :1]
    for q in range(SEQS):
        here = slice(q * SPAN, (q + 1) * SPAN)
        away = rel[here, :1]
        for i, copy in enumerate(groups):
            pl.when((s ^ (i + 1)) == q)(copy.wait_recv)
        bt = bca[q, :4].reshape(STATE, SPAN)
        cn = bca[q, 4:].reshape(STATE, SPAN).astype(jnp.float32).T.astype(jnp.bfloat16)
        scores = jnp.dot(cn, bt, preferred_element_type=jnp.float32)
        scores = jnp.where((dif >= 0) & (dif <= away), scores, 0.0)
        both = dtv[q]
        cum = jnp.dot(both, upto, precision=HIGH, preferred_element_type=jnp.float32)
        both = jnp.where(to[:8, :] < heads, both, cum)
        cols = jnp.concatenate([both, jnp.zeros((HALF - 8, SPAN), jnp.float32)], axis=0).T

        def expand(first):
            out = jnp.broadcast_to(cols[:, first : first + 1], (SPAN, WIDE))
            for h in range(1, heads):
                out = jnp.where(lane == h, cols[:, first + h : first + h + 1], out)
            return out

        dte, cume = expand(0), expand(heads)
        xv = xc[here, :]
        xdt = xv * dte
        inner = jnp.zeros((SPAN, WIDE), jnp.float32)
        for h in range(heads):
            gap = cols[:, heads + h : heads + h + 1] - both[heads + h : heads + h + 1, :]
            mixing = (jnp.exp2(jnp.minimum(gap, 0.0)) * scores).astype(jnp.bfloat16)
            inner = inner + jnp.dot(
                mixing, jnp.where(lane == h, xdt, 0.0).astype(jnp.bfloat16),
                preferred_element_type=jnp.float32,
            )
        carry = jnp.where(away > local, jnp.exp2(cume), 0.0)
        ends = cume[SPAN - 1 :, :]
        tail = jnp.where(local >= SPAN - 1 - away[SPAN - 1 :, :], jnp.exp2(ends - cume), 0.0)
        fresh = jnp.dot(bt, (tail * xdt).astype(jnp.bfloat16), preferred_element_type=jnp.float32)
        outer = jnp.dot(cn, state.astype(jnp.bfloat16), preferred_element_type=jnp.float32)
        state = carry[SPAN - 1 :, :] * state + fresh
        y = inner + outer * carry + skip * xv
        if q == 0:
            sumg.relay(2)
        some = sumg.final(q).astype(jnp.float32)
        for i in range(1, CHIPS):
            to_rows = pl.ds(pl.multiple_of(order[i] * 2 * OWN, 16), 2 * OWN)
            gs[q, to_rows, :] = some[(i - 1) * 2 * OWN : i * 2 * OWN]
        gate = gs[q]
        gated = (y * silu(gate)).reshape(2 * CHIPS, 2, few_rows, WIDE)
        for half in range(2):
            k = 2 * q + half
            some = gated[:, half].reshape(SPAN // 2, WIDE).astype(jnp.bfloat16)
            held[s, k, 0], held[s, k, 1] = some[:, :HALF], some[:, HALF:]
            for copy in gathers[k]:
                copy.start()
        if q == 0:
            sumg.relay(3)
        for k in range(2 * q - 4, 2 * q - 2):
            if k >= 0:
                advance(k)
    last_k = 2 * SEQS - 1
    for zb in range(CHIPS):
        for r in range(SEQS):
            up, down, over, goes_up, goes_down = hops(zb, r)
            pl.when(goes_up)(up.wait_send)
            pl.when(goes_down)(down.wait_send)
            over.wait_send()
    for copy in spread + steps + swaps + groups:
        copy.wait_send()
    for u in range(5):
        sums.drain(u)
    for u in range(4):
        sumg.drain(u)
    for u in range(4):
        sumb.drain(u)
    sumh.drain(0)
    for k in range(last_k - 3, last_k + 1):
        advance(k)
    settle(0, last_k - 2)
    collect(last_k - 1)
    collect(last_k)
    for q in range(SEQS):
        for half in range(2):
            pl.when(s != q)(deliver(half, q).wait_recv)

    settle(last_k - 2, last_k + 1)


def mix(operands, own, seqs):
    tokens, w_gate, w_xin, w_bc, w_dt, conv_x, conv_xb, conv_b, conv_bb, gain, w_out = operands[:11]
    depth = w_xin.shape[0]
    total = SEQS * SPAN
    cols = w_out.shape[1]
    dma = pltpu.SemaphoreType.DMA
    bf, f32 = jnp.bfloat16, jnp.float32

    def sums(n, rows):
        pair = pltpu.VMEM((n, 2, rows, HALF), bf)
        one = pltpu.VMEM((n, rows, HALF), bf)
        return [pair] * 4 + [one] * 4 + [pltpu.VMEM((n, rows, WIDE), f32)] + [pltpu.VMEM((n, rows, HALF), f32)] * 2

    return pl.pallas_call(
        mix_kernel,
        out_shape=jax.ShapeDtypeStruct((own, cols * seqs), bf),
        in_specs=[pl.BlockSpec(memory_space=pl.ANY)] * len(operands),
        out_specs=pl.BlockSpec(memory_space=pl.ANY),
        scratch_shapes=[pltpu.VMEM(a.shape, a.dtype) for a in operands[1:11]]
        + [pltpu.SMEM(a.shape, a.dtype) for a in operands[11:]]
        + [
            pltpu.VMEM((CHIPS, 2, SEQS, OWN, depth), bf),
            pltpu.VMEM((total, HALF), jnp.int32),
            pltpu.VMEM((16 + total, WIDE), f32),
            pltpu.VMEM((total, WIDE), f32),
            pltpu.VMEM((SEQS, SPAN, WIDE), f32),
            pltpu.VMEM((16 + SPAN, WIDE), f32),
            pltpu.VMEM((SEQS, 16, WIDE), f32),
            pltpu.VMEM((GROUPS, 32, SPAN), bf),
            pltpu.VMEM((SEQS, GROUPS, 32, SPAN), bf),
            pltpu.VMEM((2, SEQS, OWN, WIDE), f32),
            pltpu.VMEM((SEQS, 16, SPAN), f32),
            pltpu.VMEM((SEQS, 16, SPAN), bf),
            pltpu.VMEM((3, 16, SPAN), bf),
            pltpu.VMEM((SEQS, 8, SPAN), f32),
            pltpu.VMEM((SEQS, 2 * SEQS, 2, SPAN // 2, HALF), bf),
            pltpu.VMEM((SPAN // 2, SEQS * WIDE), bf),
            pltpu.VMEM((2 * SEQS, 2, CHIPS, OWN // 2, cols), bf),
            pltpu.VMEM((2 * SEQS, CHIPS, OWN // 2, cols), bf),
            pltpu.VMEM((2 * SEQS, CHIPS, OWN // 2, cols), bf),
            pltpu.VMEM((2 * SEQS, CHIPS - 1, OWN // 2, cols), bf),
            pltpu.VMEM((2 * SEQS, OWN // 2, cols), bf),
        ]
        + sums(CHIPS + 1, SPAN)
        + sums(CHIPS, 2 * OWN)
        + sums(1, 16)
        + sums(SEQS, SPAN - 2 * OWN)
        + [
            dma((15,)), dma((3,)), dma((3,)), dma((4, 4)), dma((4, 4)), dma((4, 4)), dma((4, 4)), dma((4, 4)),
            dma((5, 4)), dma((5, 4)), dma((4, 4)), dma((4, 4)), dma((4, 4)), dma((4, 4)),
            dma((1, 4)), dma((1, 4)), dma((3,)), dma((3,)), dma((7,)), dma((7,)), dma((3,)), dma((3,)),
            dma((8, 3)), dma((8, 3)), dma((8,)), dma((8,)), dma((8, 3)), dma((8, 3)), dma((8,)), dma((4, 2)),
        ],
        compiler_params=pltpu.CompilerParams(
            collective_id=2, has_side_effects=True, vmem_limit_bytes=56 * 2**20
        ),
    )(*operands)


def shards(
    tokens,
    w_gate,
    w_xin,
    w_bc,
    w_dt,
    conv_x,
    conv_x_bias,
    conv_bc,
    conv_bc_bias,
    dt_bias,
    decay_rate,
    d_skip,
    norm_gain,
    w_out,
    lengths,
):
    operands = (
        tokens, w_gate, w_xin, w_bc, w_dt.T, conv_x, conv_x_bias[None, :], conv_bc, conv_bc_bias[None, :],
        norm_gain[None, :], w_out, dt_bias, decay_rate, d_skip, lengths,
    )
    return mix(operands, tokens.shape[0], lax.axis_size("seq"))


def solution(mesh):
    seqs, tens = mesh.shape["seq"], mesh.shape["tensor"]
    narrow = seqs == SEQS and tens == GROUPS == 2 * CHIPS
    body = shards if narrow else shards_wide
    in_specs = (
        P(("seq", "tensor"), None),
        P("seq", "tensor"),
        P("seq", "tensor"),
        P("seq", "tensor"),
        P("seq", "tensor"),
        P(None, "tensor"),
        P("tensor"),
        P(None, "tensor"),
        P("tensor"),
        P("tensor"),
        P("tensor"),
        P("tensor"),
        P("tensor"),
        P("tensor", "seq"),
        P(),
    )
    out_specs = P(("seq", "tensor"), None)
    return jax.shard_map(body, mesh=mesh, in_specs=in_specs, out_specs=out_specs, check_vma=False)
```
